256 devices in a mesh: dp: 16 (over x, y), tensor: 16 (over z, core).
Axes of the slice: x: 4, y: 4, z: 8, core: 2. Of those that a mesh axis runs over, the one named last changes fastest.
Arguments:
- hidden_x: bfloat16 [128, 128, 16384], P('dp', None, 'tensor'), may hold values from -6 to 6
- gate_z: bfloat16 [128, 128, 16384], P('dp', None, 'tensor'), may hold values from -6 to 6
- conv_weight: float32 [4, 16384], P(None, 'tensor'), may hold values from -3 to 3
- conv_bias: float32 [16384], P('tensor'), may hold values from -0.5 to 0.5
- x_weight: bfloat16 [16384, 544], P('tensor'), may hold values from -0.046875 to 0.046875
- dt_weight: bfloat16 [512, 16384], P(None, 'tensor'), may hold values from -0.25 to 0.25
- dt_bias: float32 [16384], P('tensor'), may hold values from -6 to -2
- a_log: float32 [16, 16384], P(None, 'tensor'), may hold values from -2 to 2.7
- skip_gain: float32 [16384], P('tensor'), may hold values from 0.5 to 1.5
- ssm_cache: float32 [512, 16, 16384], P('dp', None, 'tensor'), may hold values from -6 to 6
- conv_cache: float32 [512, 3, 16384], P('dp', None, 'tensor'), may hold values from -6 to 6
- holder_of: int32 [128], replicated, may hold values from 0 to 15, as said below
- slot_of: int32 [128], replicated, may hold values from 0 to 31, as said below
Outputs:
- gated_out: bfloat16 [128, 128, 16384], P('dp', None, 'tensor')
- new_ssm: float32 [512, 16, 16384], P('dp', None, 'tensor')
- new_conv: float32 [512, 3, 16384], P('dp', None, 'tensor')
The draws below stay inside these ranges and needn't reach their ends.
Inputs may be any that keep to these rules, and one draw needn't show every extreme that they name: `holder_of`: requests 8 * g to 8 * g + 7 belong to dp group g. One holder serves at most 2 requests of one group, and in every group some holder serves exactly 2. `slot_of`: requests with the same holder have different slots.
All inputs are finite; a program needn't handle non-finite values.
Results may differ from the reference program's by a relative error of at most 0.0062.
Values may be sent and summed in bfloat16 or wider, within the bound.
No kernel may reach another device: no remote copies, remote signals or barrier semaphores. Data moves between devices by JAX's collectives and lax.ppermute only.
A program may use at most 128 MiB of HBM per device.

```python
import jax
import jax.numpy as jnp
from jax import lax

INNER = 16384
DT_RANK = 512
STATE = 16
CONV = 4
TURN = 128
REQ_DEV = 8
CAP = 2
REQUESTS = 128
SLOTS = 32
N_DP = 16


def routing(key):
    candidates = N_DP * CAP
    noise_draw = jax.random.randint(jax.random.fold_in(key, 101), (N_DP, candidates), 0, 4096)
    hottest = jax.random.randint(jax.random.fold_in(key, 102), (), 0, N_DP)
    partners = jax.random.randint(jax.random.fold_in(key, 105), (N_DP,), 0, N_DP)
    owners = jnp.arange(candidates, dtype=jnp.int32) // CAP
    group_ids = jnp.arange(N_DP, dtype=jnp.int32)
    forced = (group_ids == (hottest + 1) % N_DP) | (group_ids == (hottest + N_DP // 2) % N_DP)
    targets = jnp.where(forced, hottest, partners)
    levels = jnp.where(owners[None, :] == targets[:, None], 2, 0) + jnp.where(owners[None, :] == group_ids[:, None], 1, 0)
    scores = levels * 4194304 + noise_draw * candidates + jnp.arange(candidates, dtype=jnp.int32)[None, :]
    unused, chosen = lax.top_k(scores, REQ_DEV)
    holders = (chosen // CAP).astype(jnp.int32)
    shuffle_scores = jax.random.randint(jax.random.fold_in(key, 103), (N_DP, REQ_DEV), 0, 4096) * REQ_DEV + jnp.arange(REQ_DEV, dtype=jnp.int32)[None, :]
    unused_two, order = lax.top_k(shuffle_scores, REQ_DEV)
    holders = jnp.take_along_axis(holders, order, axis=1)
    earlier = jnp.arange(REQ_DEV)[None, :] < jnp.arange(REQ_DEV)[:, None]
    same_holder = holders[:, :, None] == holders[:, None, :]
    rank_within = jnp.sum((same_holder & earlier[None, :, :]).astype(jnp.int32), axis=2)
    offsets = jax.random.randint(jax.random.fold_in(key, 104), (N_DP,), 0, SLOTS)
    slot_rows = (group_ids[:, None] * CAP + rank_within + offsets[holders]) % SLOTS
    return (holders.reshape(-1).astype(jnp.int32), slot_rows.reshape(-1).astype(jnp.int32))


def draw_holder_of(key, part):
    return routing(key)[0]


def draw_slot_of(key, part):
    return routing(key)[1]


def block_scale(own_key, shape, cuts, low, largest):
    loudness = 1.0
    for position, shards_of in cuts:
        draws = jax.random.uniform(jax.random.fold_in(jax.random.fold_in(own_key, 6), position), (shards_of,), jnp.float32, low / len(cuts), largest / len(cuts))
        loudness = loudness * jnp.repeat(jnp.exp(draws), shape[position] // shards_of).reshape((-1,) + (1,) * (len(shape) - 1 - position))
    return loudness


def scatter_about(rng, shape, width, most, pieces=(), held_as=jnp.bfloat16):
    loudness = block_scale(rng, shape, pieces, -0.22, 0.18) if pieces else 1.0
    values = jax.random.normal(rng, shape, jnp.float32) * width * loudness
    return jnp.minimum(jnp.maximum(values, -most), most).astype(held_as)


def setup_inputs(seed: int = 0) -> dict:
    streams_of = jax.random.split(jax.random.key(seed), 14)
    return {
        "hidden_x": scatter_about(streams_of[0], (REQUESTS, TURN, INNER), 1.0, 6.0, ((0, 16), (2, 16))),
        "gate_z": scatter_about(streams_of[1], (REQUESTS, TURN, INNER), 1.0, 6.0, ((0, 16), (2, 16))),
        "conv_weight": scatter_about(streams_of[2], (CONV, INNER), CONV ** -0.5, 3.0, ((1, 16),), jnp.float32),
        "conv_bias": jnp.clip(jax.random.uniform(streams_of[3], (INNER,), jnp.float32, -0.5, 0.5) * block_scale(streams_of[3], (INNER,), ((0, 16),), -0.4, 0.0), -0.5, 0.5),
        "x_weight": scatter_about(streams_of[4], (INNER, DT_RANK + 2 * STATE), INNER ** -0.5, 0.046875, ((0, 16),)),
        "dt_weight": scatter_about(streams_of[5], (DT_RANK, INNER), DT_RANK ** -0.5, 0.25, ((1, 16),)),
        "dt_bias": jnp.clip(-6.0 + 4.0 * jax.random.uniform(streams_of[6], (INNER,), jnp.float32) ** block_scale(streams_of[6], (INNER,), ((0, 16),), -0.2, 0.2), -6.0, -2.0),
        "a_log": jnp.clip(-2.0 + 4.7 * jax.random.uniform(streams_of[7], (STATE, INNER), jnp.float32) ** block_scale(streams_of[7], (STATE, INNER), ((1, 16),), -0.2, 0.2), -2.0, 2.7),
        "skip_gain": jnp.clip(0.5 + 1.0 * jax.random.uniform(streams_of[8], (INNER,), jnp.float32) ** block_scale(streams_of[8], (INNER,), ((0, 16),), -0.2, 0.2), 0.5, 1.5),
        "ssm_cache": scatter_about(streams_of[9], (SLOTS * N_DP, STATE, INNER), 1.0, 6.0, ((0, 16), (2, 16)), jnp.float32),
        "conv_cache": scatter_about(streams_of[10], (SLOTS * N_DP, CONV - 1, INNER), 1.0, 6.0, ((0, 16), (2, 16)), jnp.float32),
        "holder_of": draw_holder_of(jax.random.fold_in(streams_of[13], 71), 0),
        "slot_of": draw_slot_of(jax.random.fold_in(streams_of[13], 71), 0),
    }


EPSILON = 1e-06
NORM_FLOOR = 0.25

def normalize(projected, rank_width, state_width):
    dt_raw = projected[:, :rank_width]
    inject_raw = projected[:, rank_width:rank_width + state_width]
    readout_raw = projected[:, rank_width + state_width:]
    dt_norm = dt_raw * lax.rsqrt(lax.optimization_barrier(jnp.mean(dt_raw * dt_raw, axis=1, keepdims=True)) + EPSILON)
    inject_norm = inject_raw * lax.rsqrt(jnp.maximum(lax.optimization_barrier(jnp.mean(inject_raw * inject_raw, axis=1, keepdims=True)), NORM_FLOOR))
    readout_norm = readout_raw * lax.rsqrt(jnp.maximum(lax.optimization_barrier(jnp.mean(readout_raw * readout_raw, axis=1, keepdims=True)), NORM_FLOOR))
    joined = jnp.concatenate([inject_norm, readout_norm], axis=1)
    return (dt_norm.astype(jnp.bfloat16), joined.astype(jnp.bfloat16))

def convolve(hidden_rows, conv_start, conv_weight, conv_bias):
    turn_len = hidden_rows.shape[1]
    extended = jnp.concatenate([conv_start, hidden_rows.astype(jnp.float32)], axis=1)
    summed = jnp.zeros(hidden_rows.shape, jnp.float32) + conv_bias[None, None, :]
    for offset in range(conv_weight.shape[0]):
        summed = summed + extended[:, offset:offset + turn_len, :] * conv_weight[offset][None, None, :]
    return jax.nn.silu(summed).astype(jnp.bfloat16)

def advance(carried, decay_rate, dt_now, drive_now, inject_now, readout_now):
    carried = jnp.exp(dt_now[:, None, :] * decay_rate[None, :, :]) * carried + drive_now[:, None, :] * inject_now[:, :, None]
    return (carried, lax.optimization_barrier(jnp.sum(readout_now[:, :, None] * carried, axis=1)))

def reference(hidden_x, gate_z, conv_weight, conv_bias, x_weight, dt_weight, dt_bias, a_log, skip_gain, ssm_cache, conv_cache, holder_of, slot_of):
    where_at = (holder_of * SLOTS + slot_of).astype(jnp.int32)
    state_all = ssm_cache[where_at].reshape(N_DP, REQ_DEV, STATE, INNER)
    conv_all = conv_cache[where_at].reshape(N_DP, REQ_DEV, CONV - 1, INNER)
    grouped_x = hidden_x.reshape(N_DP, REQ_DEV, TURN, INNER)
    grouped_z = gate_z.reshape(N_DP, REQ_DEV, TURN, INNER)
    decay_rate = -jnp.exp(a_log)

    def one_group(inputs):
        group_x, group_z, conv_start, state_start = inputs
        conv_out = convolve(group_x, conv_start, conv_weight, conv_bias)
        flat_rows = conv_out.reshape(-1, INNER)
        projected = jnp.dot(flat_rows, x_weight, preferred_element_type=jnp.float32)
        dt_norm, bc_norm = normalize(projected, DT_RANK, STATE)
        dt_full = jax.nn.softplus(jnp.dot(dt_norm, dt_weight, preferred_element_type=jnp.float32) + dt_bias[None, :])
        dt_full = dt_full.reshape(group_x.shape)
        drive_full = dt_full * conv_out.astype(jnp.float32)
        bc_full = bc_norm.astype(jnp.float32).reshape(group_x.shape[0], group_x.shape[1], 2 * STATE)

        def stepper(carried, slices):
            dt_now, drive_now, inject_now, readout_now = slices
            return advance(carried, decay_rate, dt_now, drive_now, inject_now, readout_now)
        final_state, readout = lax.scan(stepper, state_start, (jnp.swapaxes(dt_full, 0, 1), jnp.swapaxes(drive_full, 0, 1), jnp.swapaxes(bc_full[:, :, :STATE], 0, 1), jnp.swapaxes(bc_full[:, :, STATE:], 0, 1)))
        readout = jnp.swapaxes(readout, 0, 1)
        gated = ((readout + skip_gain[None, None, :] * conv_out.astype(jnp.float32)) * jax.nn.silu(group_z.astype(jnp.float32))).astype(jnp.bfloat16)
        return (gated, final_state)
    gated, final_state = lax.map(one_group, (grouped_x, grouped_z, conv_all, state_all))
    gated_out = gated.reshape(REQUESTS, TURN, INNER)
    new_ssm = ssm_cache.at[where_at].set(final_state.reshape(REQUESTS, STATE, INNER))
    new_conv = conv_cache.at[where_at].set(hidden_x[:, TURN - (CONV - 1):, :].astype(jnp.float32))
    return (gated_out, new_ssm, new_conv)
```

```python
import functools

import jax
import jax.numpy as jnp
from jax import lax
from jax.experimental import pallas as pl
from jax.experimental.pallas import tpu as pltpu
from jax.sharding import Mesh, PartitionSpec as P

EPSILON = 1e-06
NORM_FLOOR = 0.25
LOG2_E = 1.4426950408889634

GROUPS = 16
REQUESTS = 8
CHUNKS = 2
PER = REQUESTS // CHUNKS
TURN = 128
INNER = 1024
RANK = 512
STATE = 16
WIDE = RANK + 2 * STATE
SLOTS = 32
KEPT = 3
DEPTH = 8
CORES = 2
SHARE = PER * TURN // (DEPTH * CORES)
LANES = 128
TILES = INNER // LANES
UNROLL = 4

F32 = jnp.float32
BF16 = jnp.bfloat16
SWAP = [(0, 1), (1, 0)]


def params(mib):
    return pltpu.CompilerParams(vmem_limit_bytes=mib * 2**20)


def cost(us, bytes_accessed):
    return pl.CostEstimate(
        flops=int(us * 1.0e9), bytes_accessed=bytes_accessed, transcendentals=0
    )


def conv_kernel(order_ref, source_ref, hidden, start, weight, bias, x_weight, conv_out, sent, kept, rows):
    step = pl.program_id(0)
    for k in range(KEPT):
        rows[8 - KEPT + k : 9 - KEPT + k, :] = start[0, k : k + 1, :].astype(F32)
    for tile in range(TILES):
        cols = slice(tile * LANES, (tile + 1) * LANES)
        rows[8:, cols] = hidden[0, :, cols].astype(F32)
        total = jnp.zeros((TURN, LANES), F32) + bias[:, cols]
        for tap in range(KEPT + 1):
            first = 8 - KEPT + tap
            total = total + rows[first : first + TURN, cols] * weight[tap : tap + 1, cols]
        conv_out[0, :, cols] = (total / (1.0 + jnp.exp(-total))).astype(BF16)
    part = jnp.dot(conv_out[0], x_weight[...], preferred_element_type=F32)

    @pl.when(step < PER // 2)
    def _():
        sent[0] = part.astype(BF16)

    @pl.when(step >= PER // 2)
    def _():
        kept[0] = part


def convolve(order, source, hidden, arrived, weight, bias, x_weight):
    half = PER // 2
    return pl.pallas_call(
        conv_kernel,
        grid_spec=pltpu.PrefetchScalarGridSpec(
            num_scalar_prefetch=2,
            grid=(PER,),
            in_specs=[
                pl.BlockSpec((1, TURN, INNER), lambda i, o, s: (o[i], 0, 0)),
                pl.BlockSpec((1, 2 * KEPT, INNER), lambda i, o, s: (s[i], 0, 0)),
                pl.BlockSpec((KEPT + 1, INNER), lambda i, o, s: (0, 0)),
                pl.BlockSpec((1, INNER), lambda i, o, s: (0, 0)),
                pl.BlockSpec((INNER, WIDE), lambda i, o, s: (0, 0)),
            ],
            out_specs=[
                pl.BlockSpec((1, TURN, INNER), lambda i, o, s: (i, 0, 0)),
                pl.BlockSpec((1, TURN, WIDE), lambda i, o, s: (jnp.minimum(i, half - 1), 0, 0)),
                pl.BlockSpec((1, TURN, WIDE), lambda i, o, s: (jnp.maximum(i - half, 0), 0, 0)),
            ],
            scratch_shapes=[pltpu.VMEM((8 + TURN, INNER), F32)],
        ),
        out_shape=[
            jax.ShapeDtypeStruct((PER, TURN, INNER), BF16),
            jax.ShapeDtypeStruct((half, TURN, WIDE), BF16),
            jax.ShapeDtypeStruct((half, TURN, WIDE), F32),
        ],
        compiler_params=params(32),
        cost_estimate=cost(5, 4 * 2**20),
        name="convolve",
    )(order, source, hidden, arrived, weight, bias, x_weight)


def norm_kernel(parts, out):
    total = parts[0].astype(F32)
    for k in range(1, DEPTH):
        total = total + parts[k].astype(F32)
    rank = total[:, :RANK]
    inject = total[:, RANK : RANK + STATE]
    readout = total[:, RANK + STATE :]
    rank = rank * lax.rsqrt(jnp.mean(rank * rank, axis=1, keepdims=True) + EPSILON)
    inject = inject * lax.rsqrt(
        jnp.maximum(jnp.mean(inject * inject, axis=1, keepdims=True), NORM_FLOOR)
    )
    readout = readout * lax.rsqrt(
        jnp.maximum(jnp.mean(readout * readout, axis=1, keepdims=True), NORM_FLOOR)
    )
    joined = jnp.concatenate([rank, inject, readout], axis=1).astype(BF16)
    for k in range(DEPTH):
        out[k] = joined


def normalize(parts):
    return pl.pallas_call(
        norm_kernel,
        out_shape=jax.ShapeDtypeStruct((DEPTH, SHARE, WIDE), BF16),
        compiler_params=params(32),
        cost_estimate=cost(1.5, 2**20),
        name="normalize",
    )(parts)


def scan_kernel(
    order_ref,
    source_ref,
    holder_ref,
    own,
    other,
    dt_weight,
    dt_bias,
    a_log,
    skip,
    conv,
    gate,
    start,
    base,
    gated,
    final,
    dts,
    us,
    spread,
    rates,
    states,
):
    mine = pl.program_id(0) < PER // 2
    normed = jnp.where(mine, own[0].astype(F32), other[0].astype(F32))
    columns = normed[:, RANK:].T
    for t in range(TURN):
        spread[t * 2 * STATE : (t + 1) * 2 * STATE, :] = jnp.broadcast_to(
            columns[:, t : t + 1], (2 * STATE, LANES)
        )
    for tile in range(TILES):
        cols = slice(tile * LANES, (tile + 1) * LANES)
        rates[pl.ds(tile, STATE, stride=TILES), :] = -LOG2_E * jnp.exp(a_log[:, cols])
        states[pl.ds(tile, STATE, stride=TILES), :] = start[0, :, cols].astype(F32)
    rank = normed[:, :RANK].astype(BF16)
    pair = 2 * LANES
    for block in range(INNER // pair):
        cols = slice(block * pair, (block + 1) * pair)
        raw = jnp.dot(rank, dt_weight[:, cols], preferred_element_type=F32) + dt_bias[:, cols]
        dt = jnp.maximum(raw, 0.0) + jnp.log1p(jnp.exp(-jnp.abs(raw)))
        for k in range(2):
            tile = 2 * block + k
            dts[pl.ds(tile, TURN, stride=TILES), :] = dt[:, k * LANES : (k + 1) * LANES]
            us[pl.ds(tile, TURN, stride=TILES), :] = conv[
                0, :, tile * LANES : (tile + 1) * LANES
            ].astype(F32)
    decay = [rates[n * TILES : (n + 1) * TILES, :] for n in range(STATE)]

    def steps(i, carried):
        carried = list(carried)
        for k in range(UNROLL):
            t = i * UNROLL + k
            at = pl.multiple_of(t * TILES, TILES)
            row = pl.multiple_of(t * 2 * STATE, 2 * STATE)
            dt = dts[pl.ds(at, TILES), :]
            drive = dt * us[pl.ds(at, TILES), :]
            sums = [None] * 4
            for n in range(STATE):
                carried[n] = (
                    jnp.exp2(dt * decay[n]) * carried[n] + drive * spread[pl.ds(row + n, 1), :]
                )
                term = carried[n] * spread[pl.ds(row + STATE + n, 1), :]
                sums[n % 4] = term if sums[n % 4] is None else sums[n % 4] + term
            dts[pl.ds(at, TILES), :] = (sums[0] + sums[1]) + (sums[2] + sums[3])
        return tuple(carried)

    carried = tuple(states[n * TILES : (n + 1) * TILES, :] for n in range(STATE))
    carried = lax.fori_loop(0, TURN // UNROLL, steps, carried)
    for n in range(STATE):
        states[n * TILES : (n + 1) * TILES, :] = carried[n]
    for tile in range(TILES):
        cols = slice(tile * LANES, (tile + 1) * LANES)
        z = gate[0, :, cols].astype(F32)
        y = dts[pl.ds(tile, TURN, stride=TILES), :] + skip[:, cols] * conv[0, :, cols].astype(F32)
        gated[0, :, cols] = (y * (z / (1.0 + jnp.exp(-z)))).astype(BF16)
        final[0, :, cols] = states[pl.ds(tile, STATE, stride=TILES), :].astype(BF16)


def scan(order, source, holder, own, other, dt_weight, dt_bias, a_log, skip, conv, gate, start, base):
    half = PER // 2
    whole = lambda shape: pl.BlockSpec(shape, lambda i, o, s, h: (0,) * len(shape))
    return pl.pallas_call(
        scan_kernel,
        grid_spec=pltpu.PrefetchScalarGridSpec(
            num_scalar_prefetch=3,
            grid=(PER,),
            in_specs=[
                pl.BlockSpec((1, TURN, WIDE), lambda i, o, s, h: (jnp.minimum(i, half - 1), 0, 0)),
                pl.BlockSpec((1, TURN, WIDE), lambda i, o, s, h: (jnp.maximum(i - half, 0), 0, 0)),
                whole((RANK, INNER)),
                whole((1, INNER)),
                whole((STATE, INNER)),
                whole((1, INNER)),
                pl.BlockSpec((1, TURN, INNER), lambda i, o, s, h: ((i + half) % PER, 0, 0)),
                pl.BlockSpec((1, TURN, INNER), lambda i, o, s, h: (o[i], 0, 0)),
                pl.BlockSpec((1, STATE, INNER), lambda i, o, s, h: (s[i], 0, 0)),
                pl.BlockSpec(memory_space=pl.ANY),
            ],
            out_specs=[
                pl.BlockSpec((1, TURN, INNER), lambda i, o, s, h: (o[i], 0, 0)),
                pl.BlockSpec((1, STATE, INNER), lambda i, o, s, h: (h[i], 0, 0)),
            ],
            scratch_shapes=[
                pltpu.VMEM((TURN * TILES, LANES), F32),
                pltpu.VMEM((TURN * TILES, LANES), F32),
                pltpu.VMEM((TURN * 2 * STATE, LANES), F32),
                pltpu.VMEM((STATE * TILES, LANES), F32),
                pltpu.VMEM((STATE * TILES, LANES), F32),
            ],
        ),
        out_shape=[
            jax.ShapeDtypeStruct((REQUESTS, TURN, INNER), BF16),
            jax.ShapeDtypeStruct((GROUPS, STATE, INNER), BF16),
        ],
        input_output_aliases={12: 0} if base is not None else {},
        compiler_params=params(32),
        cost_estimate=cost(15, 4 * 2**20),
        name="scan",
    )(order, source, holder, own, other, dt_weight, dt_bias, a_log, skip, conv, gate, start,
      base if base is not None else skip)


def place_kernel(state_from, conv_from, ssm, conv, states, inputs, new_ssm, new_conv):
    slot = pl.program_id(0)
    new_ssm[0] = jnp.where(state_from[slot] > 0, states[0].astype(F32), ssm[0])
    last = inputs[0].astype(F32)[KEPT:, :]
    new_conv[0] = jnp.where(conv_from[slot] > 0, last, conv[0])


def place(state_from, conv_from, ssm, conv, states, inputs):
    return pl.pallas_call(
        place_kernel,
        grid_spec=pltpu.PrefetchScalarGridSpec(
            num_scalar_prefetch=2,
            grid=(SLOTS,),
            in_specs=[
                pl.BlockSpec((1, STATE, INNER), lambda i, s, c: (i, 0, 0)),
                pl.BlockSpec((1, KEPT, INNER), lambda i, s, c: (i, 0, 0)),
                pl.BlockSpec((1, STATE, INNER), lambda i, s, c: (jnp.maximum(s[i] - 1, 0), 0, 0)),
                pl.BlockSpec((1, 2 * KEPT, INNER), lambda i, s, c: (jnp.maximum(c[i] - 1, 0), 0, 0)),
            ],
            out_specs=[
                pl.BlockSpec((1, STATE, INNER), lambda i, s, c: (i, 0, 0)),
                pl.BlockSpec((1, KEPT, INNER), lambda i, s, c: (i, 0, 0)),
            ],
        ),
        out_shape=[
            jax.ShapeDtypeStruct((SLOTS, STATE, INNER), F32),
            jax.ShapeDtypeStruct((SLOTS, KEPT, INNER), F32),
        ],
        compiler_params=params(32),
        cost_estimate=cost(8, 6 * 2**20),
        name="place",
    )(state_from, conv_from, ssm, conv, states, inputs)


def store_kernel(slots, states, base, new_ssm, wide, sems):
    def start(g, carry):
        wide[g] = states[g].astype(F32)

        @pl.when(slots[g] < SLOTS)
        def _():
            pltpu.make_async_copy(wide.at[g], new_ssm.at[slots[g]], sems.at[g]).start()

        return carry

    def finish(g, carry):
        @pl.when(slots[g] < SLOTS)
        def _():
            pltpu.make_async_copy(wide.at[g], new_ssm.at[slots[g]], sems.at[g]).wait()

        return carry

    lax.fori_loop(0, GROUPS, start, 0)
    lax.fori_loop(0, GROUPS, finish, 0)


def store(slots, states, base):
    return pl.pallas_call(
        store_kernel,
        grid_spec=pltpu.PrefetchScalarGridSpec(
            num_scalar_prefetch=1,
            grid=(1,),
            in_specs=[
                pl.BlockSpec((GROUPS, STATE, INNER), lambda i, s: (0, 0, 0)),
                pl.BlockSpec(memory_space=pl.ANY),
            ],
            out_specs=pl.BlockSpec(memory_space=pl.ANY),
            scratch_shapes=[
                pltpu.VMEM((GROUPS, STATE, INNER), F32),
                pltpu.SemaphoreType.DMA((GROUPS,)),
            ],
        ),
        out_shape=jax.ShapeDtypeStruct((SLOTS, STATE, INNER), F32),
        input_output_aliases={2: 0},
        compiler_params=params(32),
        cost_estimate=cost(2, 2 * 2**20),
        name="store",
    )(slots, states, base)


def assign(holders):
    index = jnp.arange(REQUESTS)
    earlier = index[None, :] < index[:, None]
    same = holders[:, :, None] == holders[:, None, :]
    twice = jnp.sum(same, axis=2) > 1
    later = jnp.any(same & earlier[None], axis=2)
    first_of_two = twice & ~later
    room = PER - jnp.sum(first_of_two, axis=1, keepdims=True)
    alone_before = jnp.sum(~twice[:, None, :] & earlier[None], axis=2)
    leading = first_of_two | (~twice & (alone_before < room))
    chunk = jnp.where(leading, 0, 1).astype(jnp.int32)
    alike = chunk[:, :, None] == chunk[:, None, :]
    place_in = jnp.sum(alike & earlier[None], axis=2).astype(jnp.int32)
    return chunk, place_in


def exchange(values, axis):
    return lax.all_to_all(values, axis, split_axis=0, concat_axis=0, tiled=True)


def body(
    hidden_x,
    gate_z,
    conv_weight,
    conv_bias,
    x_weight,
    dt_weight,
    dt_bias,
    a_log,
    skip_gain,
    ssm_cache,
    conv_cache,
    holder_of,
    slot_of,
):
    me = lax.axis_index("dp")
    core = lax.axis_index("core")
    holders = holder_of.reshape(GROUPS, REQUESTS)
    places = slot_of.reshape(GROUPS, REQUESTS)
    chunk, place_in = assign(holders)

    chunk_range = jnp.arange(CHUNKS, dtype=jnp.int32)
    served = (holders == me)[:, None, :] & (chunk[:, None, :] == chunk_range[None, :, None])
    occupied = jnp.any(served, axis=2)
    slots = jnp.sum(jnp.where(served, places[:, None, :], 0), axis=2)
    targets = jnp.where(occupied, slots, SLOTS)
    hits = targets[None] == jnp.arange(SLOTS, dtype=jnp.int32)[:, None, None]
    group_range = jnp.arange(GROUPS, dtype=jnp.int32)
    state_from = jnp.sum(jnp.where(hits[:, :, 0], group_range[None] + 1, 0), axis=1)
    numbers = group_range[:, None] * CHUNKS + chunk_range[None, :] + 1
    conv_from = jnp.sum(jnp.where(hits, numbers[None], 0), axis=(1, 2))

    own_holders = holders[me]
    own_number = chunk[me] * PER + place_in[me]
    at = jnp.arange(REQUESTS, dtype=jnp.int32)
    half = PER // 2
    number_of = (at // PER) * PER + ((at % PER) // half + (1 - core)) % 2 * half + at % half
    chosen = own_number[None, :] == number_of[:, None]
    order = jnp.sum(jnp.where(chosen, at[None, :], 0), axis=1)
    holder = jnp.sum(jnp.where(chosen, own_holders[None, :], 0), axis=1)
    source = holder * CHUNKS + at // PER
    sent_to = (own_holders[None, None, :] == group_range[:, None, None]) & (
        chunk[me][None, None, :] == chunk_range[None, :, None]
    )
    picked = jnp.sum(jnp.where(sent_to, at[None, None, :], 0), axis=2)

    first = jnp.concatenate(
        [conv_cache[slots].astype(BF16), hidden_x[:, TURN - KEPT :, :][picked]], axis=2
    )
    first = exchange(first, "dp").reshape(GROUPS * CHUNKS, 2 * KEPT, INNER)
    starts = exchange(ssm_cache[slots].astype(BF16), "dp").reshape(
        GROUPS * CHUNKS, STATE, INNER
    )

    bias = conv_bias.reshape(1, INNER)
    convs, normed = [], []
    for c in range(CHUNKS):
        span = slice(c * PER, (c + 1) * PER)
        conv, sent, kept = convolve(
            order[span], source[span], hidden_x, first, conv_weight, bias, x_weight
        )
        came = lax.ppermute(sent, "core", SWAP)
        parts = (kept + came.astype(F32)).astype(BF16).reshape(DEPTH, SHARE, WIDE)
        own = exchange(normalize(exchange(parts, "z")), "z").reshape(half, TURN, WIDE)
        other = lax.ppermute(own, "core", SWAP)
        convs.append(conv)
        normed.append((own, other))

    gated = None
    returned = []
    for c in range(CHUNKS):
        swap = lambda v: jnp.concatenate([v[c * PER + half : (c + 1) * PER], v[c * PER : c * PER + half]])
        gated, final = scan(
            swap(order),
            swap(source),
            swap(holder),
            normed[c][0],
            normed[c][1],
            dt_weight,
            dt_bias.reshape(1, INNER),
            a_log,
            skip_gain.reshape(1, INNER),
            convs[c],
            gate_z,
            starts,
            gated,
        )
        returned.append(exchange(final, "dp"))
    new_ssm, new_conv = place(state_from, conv_from, ssm_cache, conv_cache, returned[0], first)
    new_ssm = store(targets[:, 1], returned[1], new_ssm)
    return (gated, new_ssm, new_conv)


def solution(mesh):
    fine = Mesh(mesh.devices.reshape(GROUPS, DEPTH, CORES), ("dp", "z", "core"))
    tensor = ("z", "core")
    placed = (
        P("dp", None, tensor),
        P("dp", None, tensor),
        P(None, tensor),
        P(tensor),
        P(tensor, None),
        P(None, tensor),
        P(tensor),
        P(None, tensor),
        P(tensor),
        P("dp", None, tensor),
        P("dp", None, tensor),
        P(),
        P(),
    )
    return jax.shard_map(
        body,
        mesh=fine,
        in_specs=placed,
        out_specs=(P("dp", None, tensor),) * 3,
        check_vma=False,
    )
```

```python
import functools

import jax
import jax.numpy as jnp
from jax import lax
from jax.experimental import pallas as pl
from jax.experimental.pallas import tpu as pltpu
from jax.sharding import Mesh, PartitionSpec as P

EPSILON = 1e-06
NORM_FLOOR = 0.25
LOG2_E = 1.4426950408889634

GROUPS = 16
REQUESTS = 8
CHUNKS = 2
PER = REQUESTS // CHUNKS
TURN = 128
INNER = 1024
RANK = 512
STATE = 16
WIDE = RANK + 2 * STATE
SLOTS = 32
KEPT = 3
DEPTH = 8
CORES = 2
HALF = PER // CORES
SHARE = HALF * TURN // DEPTH
HEAD = 16
FETCHED = CHUNKS * (STATE + KEPT)
RETURNED = STATE + KEPT
LANES = 128
TILES = INNER // LANES
UNROLL = 4

F32 = jnp.float32
BF16 = jnp.bfloat16
SWAP = [(0, 1), (1, 0)]


def params():
    return pltpu.CompilerParams(vmem_limit_bytes=56 * 2**20)


def cost(us, bytes_accessed):
    return pl.CostEstimate(
        flops=int(us * 1.0e9), bytes_accessed=bytes_accessed, transcendentals=0
    )


def rows_to_tiles(tiles, first, rows):
    for tile in range(TILES):
        tiles[pl.ds(first + tile, rows.shape[0], stride=TILES), :] = rows[
            :, tile * LANES : (tile + 1) * LANES
        ]


def pack_kernel(slots, ssm, conv, out, states, tiles, inputs, sems):
    def copy(e):
        return pltpu.make_async_copy(ssm.at[slots[e]], states.at[e], sems.at[e])

    def begin(e, carry):
        copy(e).start()
        return carry

    def finish(e, carry):
        g, c = e // CHUNKS, e % CHUNKS
        for k in range(KEPT):
            row = pl.multiple_of((k * SLOTS + slots[e]) * TILES, TILES)
            out[g, CHUNKS * STATE + c * KEPT + k] = inputs[pl.ds(row, TILES), :].astype(BF16)
        copy(e).wait()
        rows_to_tiles(tiles, 0, states[e])
        for n in range(STATE):
            out[g, c * STATE + n] = tiles[n * TILES : (n + 1) * TILES, :].astype(BF16)
        return carry

    lax.fori_loop(0, GROUPS * CHUNKS, begin, 0)
    for k in range(KEPT):
        rows_to_tiles(inputs, k * SLOTS * TILES, conv[k])
    lax.fori_loop(0, GROUPS * CHUNKS, finish, 0)


def pack(slots, ssm, conv):
    return pl.pallas_call(
        pack_kernel,
        grid_spec=pltpu.PrefetchScalarGridSpec(
            num_scalar_prefetch=1,
            grid=(1,),
            in_specs=[
                pl.BlockSpec(memory_space=pl.ANY),
                pl.BlockSpec((KEPT, SLOTS, INNER), lambda i, s: (0, 0, 0)),
            ],
            out_specs=pl.BlockSpec((GROUPS, FETCHED, TILES, LANES), lambda i, s: (0, 0, 0, 0)),
            scratch_shapes=[
                pltpu.VMEM((GROUPS * CHUNKS, STATE, INNER), F32),
                pltpu.VMEM((STATE * TILES, LANES), F32),
                pltpu.VMEM((KEPT * SLOTS * TILES, LANES), F32),
                pltpu.SemaphoreType.DMA((GROUPS * CHUNKS,)),
            ],
        ),
        out_shape=jax.ShapeDtypeStruct((GROUPS, FETCHED, TILES, LANES), BF16),
        compiler_params=params(),
        cost_estimate=cost(3, 4 * 2**20),
        name="pack",
    )(slots, ssm, conv)


def silu(v):
    return v / (1.0 + jnp.exp(-v))


def conv_kernel(order_ref, hidden, weight, bias, x_weight, conv_out, sent, kept, rows):
    step = pl.program_id(0)
    rows[:8, :] = jnp.zeros((8, INNER), F32)
    for tile in range(TILES):
        cols = slice(tile * LANES, (tile + 1) * LANES)
        rows[8:, cols] = hidden[0, :, cols].astype(F32)
        total = jnp.zeros((TURN, LANES), F32) + bias[:, cols]
        for tap in range(KEPT + 1):
            first = 8 - KEPT + tap
            total = total + rows[first : first + TURN, cols] * weight[tap : tap + 1, cols]
        conv_out[0, :, cols] = silu(total).astype(BF16)
    part = jnp.dot(conv_out[0], x_weight[...], preferred_element_type=F32)
    part = part.reshape(TURN // SHARE, 1, SHARE, WIDE)

    @pl.when(step < PER)
    def _():
        sent[...] = part.astype(BF16)

    @pl.when(step >= PER)
    def _():
        kept[...] = part


def convolve(order, hidden, weight, bias, x_weight):
    spans = TURN // SHARE

    def share(i):
        return (i % HALF, i // HALF, 0, 0)

    return pl.pallas_call(
        conv_kernel,
        grid_spec=pltpu.PrefetchScalarGridSpec(
            num_scalar_prefetch=1,
            grid=(REQUESTS,),
            in_specs=[
                pl.BlockSpec((1, TURN, INNER), lambda i, o: (o[i], 0, 0)),
                pl.BlockSpec((KEPT + 1, INNER), lambda i, o: (0, 0)),
                pl.BlockSpec((1, INNER), lambda i, o: (0, 0)),
                pl.BlockSpec((INNER, WIDE), lambda i, o: (0, 0)),
            ],
            out_specs=[
                pl.BlockSpec((1, TURN, INNER), lambda i, o: (i, 0, 0)),
                pl.BlockSpec((spans, 1, SHARE, WIDE), lambda i, o: share(jnp.minimum(i, PER - 1))),
                pl.BlockSpec((spans, 1, SHARE, WIDE), lambda i, o: share(jnp.maximum(i - PER, 0))),
            ],
            scratch_shapes=[pltpu.VMEM((8 + TURN, INNER), F32)],
        ),
        out_shape=[
            jax.ShapeDtypeStruct((REQUESTS, TURN, INNER), BF16),
            jax.ShapeDtypeStruct((DEPTH, CHUNKS, SHARE, WIDE), BF16),
            jax.ShapeDtypeStruct((DEPTH, CHUNKS, SHARE, WIDE), F32),
        ],
        compiler_params=params(),
        cost_estimate=cost(8, 8 * 2**20),
        name="convolve",
    )(order, hidden, weight, bias, x_weight)


def head_kernel(
    order, holder, hidden, fetched, weight, bias, x_weight, conv_in, sent_in, kept_in,
    conv_out, sent, kept, rows, tiles, head, head_sent, head_kept, sems,
):
    for i in range(REQUESTS):
        c = i % PER // HALF
        for k in range(KEPT):
            tiles[k * TILES : (k + 1) * TILES, :] = fetched[
                holder[i], CHUNKS * STATE + c * KEPT + k
            ].astype(F32)
        for tile in range(TILES):
            rows[8 - KEPT : 8, tile * LANES : (tile + 1) * LANES] = tiles[
                pl.ds(tile, KEPT, stride=TILES), :
            ]
        rows[8:, :] = hidden[order[i]].astype(F32)
        total = jnp.zeros((HEAD, INNER), F32) + bias[...]
        for tap in range(KEPT + 1):
            first = 8 - KEPT + tap
            total = total + rows[first : first + HEAD, :] * weight[tap : tap + 1, :]
        head[i] = silu(total).astype(BF16)
    part = jnp.dot(
        head[...].reshape(REQUESTS * HEAD, INNER), x_weight[...], preferred_element_type=F32
    ).reshape(REQUESTS, HEAD, WIDE)
    head_sent[...] = part[:PER].astype(BF16)
    head_kept[...] = part[PER:]
    copies = []
    for i in range(REQUESTS):
        c, r = i % PER // HALF, i % HALF
        span = r * (TURN // SHARE)
        copies.append((head.at[i], conv_out.at[i, :HEAD]))
        if i < PER:
            copies.append((head_sent.at[i], sent.at[span, c, :HEAD]))
        else:
            copies.append((head_kept.at[i - PER], kept.at[span, c, :HEAD]))
    copies = [
        pltpu.make_async_copy(source, target, sems.at[k])
        for k, (source, target) in enumerate(copies)
    ]
    for one in copies:
        one.start()
    for one in copies:
        one.wait()


def put_heads(order, holder, hidden, fetched, weight, bias, x_weight, conv_out, sent, kept):
    anywhere = pl.BlockSpec(memory_space=pl.ANY)
    return pl.pallas_call(
        head_kernel,
        grid_spec=pltpu.PrefetchScalarGridSpec(
            num_scalar_prefetch=2,
            grid=(1,),
            in_specs=[
                pl.BlockSpec((REQUESTS, HEAD, INNER), lambda i, o, h: (0, 0, 0)),
                pl.BlockSpec((GROUPS, FETCHED, TILES, LANES), lambda i, o, h: (0, 0, 0, 0)),
                pl.BlockSpec((KEPT + 1, INNER), lambda i, o, h: (0, 0)),
                pl.BlockSpec((1, INNER), lambda i, o, h: (0, 0)),
                pl.BlockSpec((INNER, WIDE), lambda i, o, h: (0, 0)),
                anywhere,
                anywhere,
                anywhere,
            ],
            out_specs=[anywhere, anywhere, anywhere],
            scratch_shapes=[
                pltpu.VMEM((8 + HEAD, INNER), F32),
                pltpu.VMEM((KEPT * TILES, LANES), F32),
                pltpu.VMEM((REQUESTS, HEAD, INNER), BF16),
                pltpu.VMEM((PER, HEAD, WIDE), BF16),
                pltpu.VMEM((PER, HEAD, WIDE), F32),
                pltpu.SemaphoreType.DMA((2 * REQUESTS,)),
            ],
        ),
        out_shape=[
            jax.ShapeDtypeStruct(conv_out.shape, conv_out.dtype),
            jax.ShapeDtypeStruct(sent.shape, sent.dtype),
            jax.ShapeDtypeStruct(kept.shape, kept.dtype),
        ],
        input_output_aliases={7: 0, 8: 1, 9: 2},
        compiler_params=params(),
        cost_estimate=cost(3, 4 * 2**20),
        name="put_heads",
    )(order, holder, hidden, fetched, weight, bias, x_weight, conv_out, sent, kept)


def norm_kernel(parts, *outs):
    for c in range(CHUNKS):
        total = parts[0, c].astype(F32)
        for k in range(1, DEPTH):
            total = total + parts[k, c].astype(F32)
        rank = total[:, :RANK]
        inject = total[:, RANK : RANK + STATE]
        readout = total[:, RANK + STATE :]
        rank = rank * lax.rsqrt(jnp.mean(rank * rank, axis=1, keepdims=True) + EPSILON)
        inject = inject * lax.rsqrt(
            jnp.maximum(jnp.mean(inject * inject, axis=1, keepdims=True), NORM_FLOOR)
        )
        readout = readout * lax.rsqrt(
            jnp.maximum(jnp.mean(readout * readout, axis=1, keepdims=True), NORM_FLOOR)
        )
        joined = jnp.concatenate([rank, inject, readout], axis=1).astype(BF16)
        for k in range(DEPTH):
            outs[c][k] = joined


def normalize(parts):
    return pl.pallas_call(
        norm_kernel,
        out_shape=[jax.ShapeDtypeStruct((DEPTH, SHARE, WIDE), BF16)] * CHUNKS,
        compiler_params=params(),
        cost_estimate=cost(1.5, 2**20),
        name="normalize",
    )(parts)


def scan_kernel(
    order_ref, holder_ref, own, other, dt_weight, dt_bias, a_log, skip, conv, gate, start, last,
    base, gated, final, dts, us, spread, rates,
):
    step = pl.program_id(0)

    @pl.when(step == 0)
    def _():
        rows_to_tiles(rates, 0, -LOG2_E * jnp.exp(a_log[...]))

    normed = jnp.where(step < HALF, own[0].astype(F32), other[0].astype(F32))
    columns = normed[:, RANK:].T
    for t in range(TURN):
        spread[t * 2 * STATE : (t + 1) * 2 * STATE, :] = jnp.broadcast_to(
            columns[:, t : t + 1], (2 * STATE, LANES)
        )
    rows_to_tiles(dts, 0, last[0].astype(F32)[HEAD - KEPT :, :])
    for k in range(KEPT):
        final[0, STATE + k] = dts[k * TILES : (k + 1) * TILES, :].astype(BF16)
    rank = normed[:, :RANK].astype(BF16)
    pair = 2 * LANES
    for block in range(INNER // pair):
        cols = slice(block * pair, (block + 1) * pair)
        raw = jnp.dot(rank, dt_weight[:, cols], preferred_element_type=F32) + dt_bias[:, cols]
        dt = jnp.maximum(raw, 0.0) + jnp.log1p(jnp.exp(-jnp.abs(raw)))
        for k in range(2):
            tile = 2 * block + k
            dts[pl.ds(tile, TURN, stride=TILES), :] = dt[:, k * LANES : (k + 1) * LANES]
            us[pl.ds(tile, TURN, stride=TILES), :] = conv[
                0, :, tile * LANES : (tile + 1) * LANES
            ].astype(F32)
    decay = [rates[n * TILES : (n + 1) * TILES, :] for n in range(STATE)]

    def steps(i, carried):
        carried = list(carried)
        for k in range(UNROLL):
            t = i * UNROLL + k
            at = pl.multiple_of(t * TILES, TILES)
            row = pl.multiple_of(t * 2 * STATE, 2 * STATE)
            dt = dts[pl.ds(at, TILES), :]
            drive = dt * us[pl.ds(at, TILES), :]
            sums = [None] * 4
            for n in range(STATE):
                carried[n] = (
                    jnp.exp2(dt * decay[n]) * carried[n] + drive * spread[pl.ds(row + n, 1), :]
                )
                term = carried[n] * spread[pl.ds(row + STATE + n, 1), :]
                sums[n % 4] = term if sums[n % 4] is None else sums[n % 4] + term
            dts[pl.ds(at, TILES), :] = (sums[0] + sums[1]) + (sums[2] + sums[3])
        return tuple(carried)

    carried = tuple(start[0, n].astype(F32) for n in range(STATE))
    carried = lax.fori_loop(0, TURN // UNROLL, steps, carried)
    for n in range(STATE):
        final[0, n] = carried[n].astype(BF16)
    for tile in range(TILES):
        cols = slice(tile * LANES, (tile + 1) * LANES)
        z = gate[0, :, cols].astype(F32)
        y = dts[pl.ds(tile, TURN, stride=TILES), :] + skip[:, cols] * conv[0, :, cols].astype(F32)
        gated[0, :, cols] = (y * silu(z)).astype(BF16)


def scan(c, order, holder, own, other, dt_weight, dt_bias, a_log, skip, conv, gate, fetched, hidden, base):
    whole = lambda shape: pl.BlockSpec(shape, lambda i, o, h: (0,) * len(shape))

    def at(i):
        return jnp.where(i < HALF, PER + c * HALF + i, c * HALF + i - HALF)

    return pl.pallas_call(
        scan_kernel,
        grid_spec=pltpu.PrefetchScalarGridSpec(
            num_scalar_prefetch=2,
            grid=(PER,),
            in_specs=[
                pl.BlockSpec((1, TURN, WIDE), lambda i, o, h: (jnp.minimum(i, HALF - 1), 0, 0)),
                pl.BlockSpec((1, TURN, WIDE), lambda i, o, h: (jnp.maximum(i - HALF, 0), 0, 0)),
                whole((RANK, INNER)),
                whole((1, INNER)),
                whole((STATE, INNER)),
                whole((1, INNER)),
                pl.BlockSpec((1, TURN, INNER), lambda i, o, h: (at(i), 0, 0)),
                pl.BlockSpec((1, TURN, INNER), lambda i, o, h: (o[at(i)], 0, 0)),
                pl.BlockSpec((1, STATE, TILES, LANES), lambda i, o, h: (h[at(i)], c, 0, 0)),
                pl.BlockSpec((1, HEAD, INNER), lambda i, o, h: (o[at(i)], TURN // HEAD - 1, 0)),
                pl.BlockSpec(memory_space=pl.ANY),
            ],
            out_specs=[
                pl.BlockSpec((1, TURN, INNER), lambda i, o, h: (o[at(i)], 0, 0)),
                pl.BlockSpec((1, RETURNED, TILES, LANES), lambda i, o, h: (h[at(i)], 0, 0, 0)),
            ],
            scratch_shapes=[
                pltpu.VMEM((TURN * TILES, LANES), F32),
                pltpu.VMEM((TURN * TILES, LANES), F32),
                pltpu.VMEM((TURN * 2 * STATE, LANES), F32),
                pltpu.VMEM((STATE * TILES, LANES), F32),
            ],
        ),
        out_shape=[
            jax.ShapeDtypeStruct((REQUESTS, TURN, INNER), BF16),
            jax.ShapeDtypeStruct((GROUPS, RETURNED, TILES, LANES), BF16),
        ],
        input_output_aliases={12: 0} if base is not None else {},
        compiler_params=params(),
        cost_estimate=cost(15, 4 * 2**20),
        name="scan",
    )(order, holder, own, other, dt_weight, dt_bias, a_log, skip, conv, gate, fetched, hidden,
      base if base is not None else skip)


def store_kernel(slots, came, ssm_in, conv, new_ssm, new_conv, wide, tiles, inputs, sems):
    for k in range(KEPT):
        rows_to_tiles(inputs, k * SLOTS * TILES, conv[k])

    def copy(g):
        return pltpu.make_async_copy(wide.at[g], new_ssm.at[slots[g]], sems.at[g])

    def begin(g, carry):
        @pl.when(slots[g] < SLOTS)
        def _():
            for n in range(STATE):
                tiles[n * TILES : (n + 1) * TILES, :] = came[g, n].astype(F32)
            for tile in range(TILES):
                wide[g, :, tile * LANES : (tile + 1) * LANES] = tiles[
                    pl.ds(tile, STATE, stride=TILES), :
                ]
            copy(g).start()
            for k in range(KEPT):
                row = pl.multiple_of((k * SLOTS + slots[g]) * TILES, TILES)
                inputs[pl.ds(row, TILES), :] = came[g, STATE + k].astype(F32)

        return carry

    def finish(g, carry):
        @pl.when(slots[g] < SLOTS)
        def _():
            copy(g).wait()

        return carry

    lax.fori_loop(0, GROUPS, begin, 0)
    for k in range(KEPT):
        for tile in range(TILES):
            new_conv[k, :, tile * LANES : (tile + 1) * LANES] = inputs[
                pl.ds(k * SLOTS * TILES + tile, SLOTS, stride=TILES), :
            ]
    lax.fori_loop(0, GROUPS, finish, 0)


def store(slots, came, ssm, conv):
    return pl.pallas_call(
        store_kernel,
        grid_spec=pltpu.PrefetchScalarGridSpec(
            num_scalar_prefetch=1,
            grid=(1,),
            in_specs=[
                pl.BlockSpec((GROUPS, RETURNED, TILES, LANES), lambda i, s: (0, 0, 0, 0)),
                pl.BlockSpec(memory_space=pl.ANY),
                pl.BlockSpec((KEPT, SLOTS, INNER), lambda i, s: (0, 0, 0)),
            ],
            out_specs=[
                pl.BlockSpec(memory_space=pl.ANY),
                pl.BlockSpec((KEPT, SLOTS, INNER), lambda i, s: (0, 0, 0)),
            ],
            scratch_shapes=[
                pltpu.VMEM((GROUPS, STATE, INNER), F32),
                pltpu.VMEM((STATE * TILES, LANES), F32),
                pltpu.VMEM((KEPT * SLOTS * TILES, LANES), F32),
                pltpu.SemaphoreType.DMA((GROUPS,)),
            ],
        ),
        out_shape=[
            jax.ShapeDtypeStruct((SLOTS, STATE, INNER), F32),
            jax.ShapeDtypeStruct((KEPT, SLOTS, INNER), F32),
        ],
        input_output_aliases={2: 0},
        compiler_params=params(),
        cost_estimate=cost(3, 2 * 2**20),
        name="store",
    )(slots, came, ssm, conv)


def exchange(values, axis):
    return lax.all_to_all(values, axis, split_axis=0, concat_axis=0, tiled=True)


def body(
    hidden_x,
    gate_z,
    conv_weight,
    conv_bias,
    x_weight,
    dt_weight,
    dt_bias,
    a_log,
    skip_gain,
    ssm_cache,
    conv_cache,
    holder_of,
    slot_of,
):
    me = lax.axis_index("dp")
    core = lax.axis_index("core")
    holders = holder_of.reshape(GROUPS, REQUESTS)
    places = slot_of.reshape(GROUPS, REQUESTS)

    keys = holders * REQUESTS + jnp.arange(REQUESTS, dtype=jnp.int32)
    rank = jnp.sum((keys[:, None, :] < keys[:, :, None]).astype(jnp.int32), axis=2)
    served = (holders == me)[:, None, :] & (
        rank[:, None, :] % CHUNKS == jnp.arange(CHUNKS, dtype=jnp.int32)[None, :, None]
    )
    slots = jnp.sum(jnp.where(served, places[:, None, :], 0), axis=2)
    targets = jnp.where(jnp.any(served, axis=2), slots, SLOTS)

    at = jnp.arange(REQUESTS, dtype=jnp.int32)
    side = jnp.where(at < PER, 1 - core, core)
    number = (side * HALF + at % HALF) * CHUNKS + at % PER // HALF
    chosen = rank[me][None, :] == number[:, None]
    order = jnp.sum(jnp.where(chosen, at[None, :], 0), axis=1)
    holder = jnp.sum(jnp.where(chosen, holders[me][None, :], 0), axis=1)

    conv_rows = jnp.swapaxes(conv_cache, 0, 1)
    bias = conv_bias.reshape(1, INNER)
    fetched = exchange(pack(slots.reshape(-1), ssm_cache, conv_rows), "dp")
    conv, sent, kept = convolve(order, hidden_x, conv_weight, bias, x_weight)
    conv, sent, kept = put_heads(
        order, holder, hidden_x, fetched, conv_weight, bias, x_weight, conv, sent, kept
    )
    parts = (kept + lax.ppermute(sent, "core", SWAP).astype(F32)).astype(BF16)
    shares = normalize(exchange(parts, "z"))

    own = [exchange(share, "z").reshape(HALF, TURN, WIDE) for share in shares]
    other = [lax.ppermute(half, "core", SWAP) for half in own]
    gated = None
    came = []
    for c in range(CHUNKS):
        gated, final = scan(
            c,
            order,
            holder,
            own[c],
            other[c],
            dt_weight,
            dt_bias.reshape(1, INNER),
            a_log,
            skip_gain.reshape(1, INNER),
            conv,
            gate_z,
            fetched,
            hidden_x,
            gated,
        )
        came.append(exchange(final, "dp"))
    new_ssm, new_conv = ssm_cache, conv_rows
    for c in range(CHUNKS):
        new_ssm, new_conv = store(targets[:, c], came[c], new_ssm, new_conv)
    return (gated, new_ssm, jnp.swapaxes(new_conv, 0, 1))


def solution(mesh):
    fine = Mesh(mesh.devices.reshape(GROUPS, DEPTH, CORES), ("dp", "z", "core"))
    tensor = ("z", "core")
    placed = (
        P("dp", None, tensor),
        P("dp", None, tensor),
        P(None, tensor),
        P(tensor),
        P(tensor, None),
        P(None, tensor),
        P(tensor),
        P(None, tensor),
        P(tensor),
        P("dp", None, tensor),
        P("dp", None, tensor),
        P(),
        P(),
    )
    return jax.shard_map(
        body,
        mesh=fine,
        in_specs=placed,
        out_specs=(P("dp", None, tensor),) * 3,
        check_vma=False,
    )
```

```python
import functools

import jax
import jax.numpy as jnp
from jax import lax
from jax.experimental import pallas as pl
from jax.experimental.pallas import tpu as pltpu
from jax.sharding import Mesh, PartitionSpec as P

EPSILON = 1e-06
NORM_FLOOR = 0.25
LOG2_E = 1.4426950408889634

GROUPS = 16
REQUESTS = 8
CHUNKS = 2
PER = REQUESTS // CHUNKS
TURN = 128
INNER = 1024
RANK = 512
STATE = 16
WIDE = RANK + 2 * STATE
SLOTS = 32
KEPT = 3
DEPTH = 8
CORES = 2
SHARE = PER * TURN // DEPTH
HEAD = 16
FETCHED = CHUNKS * (STATE + KEPT)
RETURNED = STATE + CHUNKS * KEPT
LANES = 128
TILES = INNER // LANES
UNROLL = 4

F32 = jnp.float32
BF16 = jnp.bfloat16
SWAP = [(0, 1), (1, 0)]


def params():
    return pltpu.CompilerParams(vmem_limit_bytes=56 * 2**20)


def cost(us, bytes_accessed):
    return pl.CostEstimate(
        flops=int(us * 1.0e9), bytes_accessed=bytes_accessed, transcendentals=0
    )


def rows_to_tiles(tiles, first, rows):
    for tile in range(TILES):
        tiles[pl.ds(first + tile, rows.shape[0], stride=TILES), :] = rows[
            :, tile * LANES : (tile + 1) * LANES
        ]


def block_of(part, tile):
    return slice(part * 8, (part + 1) * 8), slice(tile * LANES, (tile + 1) * LANES)


def pack_kernel(slots, ssm, conv, out, states, inputs, sems):
    def copy(e):
        return pltpu.make_async_copy(ssm.at[slots[e]], states.at[e], sems.at[e])

    def begin(e, carry):
        copy(e).start()
        return carry

    def finish(e, carry):
        g, c = e // CHUNKS, e % CHUNKS
        for k in range(KEPT):
            row = pl.multiple_of((k * SLOTS + slots[e]) * TILES, TILES)
            out[g, CHUNKS * STATE + c * KEPT + k] = inputs[pl.ds(row, TILES), :].astype(BF16)
        copy(e).wait()
        for part in range(STATE // 8):
            for tile in range(TILES):
                rows, cols = block_of(part, tile)
                out[g, c * STATE + part * TILES + tile] = states[e, rows, cols].astype(BF16)
        return carry

    lax.fori_loop(0, GROUPS * CHUNKS, begin, 0)
    for k in range(KEPT):
        rows_to_tiles(inputs, k * SLOTS * TILES, conv[k])
    lax.fori_loop(0, GROUPS * CHUNKS, finish, 0)


def pack(slots, ssm, conv):
    return pl.pallas_call(
        pack_kernel,
        grid_spec=pltpu.PrefetchScalarGridSpec(
            num_scalar_prefetch=1,
            grid=(1,),
            in_specs=[
                pl.BlockSpec(memory_space=pl.ANY),
                pl.BlockSpec((KEPT, SLOTS, INNER), lambda i, s: (0, 0, 0)),
            ],
            out_specs=pl.BlockSpec((GROUPS, FETCHED, TILES, LANES), lambda i, s: (0, 0, 0, 0)),
            scratch_shapes=[
                pltpu.VMEM((GROUPS * CHUNKS, STATE, INNER), F32),
                pltpu.VMEM((KEPT * SLOTS * TILES, LANES), F32),
                pltpu.SemaphoreType.DMA((GROUPS * CHUNKS,)),
            ],
        ),
        out_shape=jax.ShapeDtypeStruct((GROUPS, FETCHED, TILES, LANES), BF16),
        compiler_params=params(),
        cost_estimate=cost(3, 4 * 2**20),
        name="pack",
    )(slots, ssm, conv)


def silu(v):
    return v / (1.0 + jnp.exp(-v))


def conv_kernel(order_ref, hidden, weight, bias, x_weight, conv_out, sent, kept, rows):
    step = pl.program_id(0)
    rows[:8, :] = jnp.zeros((8, INNER), F32)
    for tile in range(TILES):
        cols = slice(tile * LANES, (tile + 1) * LANES)
        rows[8:, cols] = hidden[0, :, cols].astype(F32)
        total = jnp.zeros((TURN, LANES), F32) + bias[:, cols]
        for tap in range(KEPT + 1):
            first = 8 - KEPT + tap
            total = total + rows[first : first + TURN, cols] * weight[tap : tap + 1, cols]
        conv_out[0, :, cols] = silu(total).astype(BF16)
    part = jnp.dot(conv_out[0], x_weight[...], preferred_element_type=F32)

    @pl.when(step < PER)
    def _():
        sent[0] = part.astype(BF16)

    @pl.when(step >= PER)
    def _():
        kept[0] = part


def convolve(order, hidden, weight, bias, x_weight):
    return pl.pallas_call(
        conv_kernel,
        grid_spec=pltpu.PrefetchScalarGridSpec(
            num_scalar_prefetch=1,
            grid=(REQUESTS,),
            in_specs=[
                pl.BlockSpec((1, TURN, INNER), lambda i, o: (o[i], 0, 0)),
                pl.BlockSpec((KEPT + 1, INNER), lambda i, o: (0, 0)),
                pl.BlockSpec((1, INNER), lambda i, o: (0, 0)),
                pl.BlockSpec((INNER, WIDE), lambda i, o: (0, 0)),
            ],
            out_specs=[
                pl.BlockSpec((1, TURN, INNER), lambda i, o: (i, 0, 0)),
                pl.BlockSpec((1, TURN, WIDE), lambda i, o: (jnp.minimum(i, PER - 1), 0, 0)),
                pl.BlockSpec((1, TURN, WIDE), lambda i, o: (jnp.maximum(i - PER, 0), 0, 0)),
            ],
            scratch_shapes=[pltpu.VMEM((8 + TURN, INNER), F32)],
        ),
        out_shape=[
            jax.ShapeDtypeStruct((REQUESTS, TURN, INNER), BF16),
            jax.ShapeDtypeStruct((PER, TURN, WIDE), BF16),
            jax.ShapeDtypeStruct((PER, TURN, WIDE), F32),
        ],
        compiler_params=params(),
        cost_estimate=cost(8, 8 * 2**20),
        name="convolve",
    )(order, hidden, weight, bias, x_weight)


def head_kernel(
    order, holder, sides, hidden, fetched, weight, bias, x_weight, conv_in, sent_in, kept_in,
    conv_out, sent, kept, starts, rows, tiles, head, head_sent, head_kept, sems, start_sems,
):
    arriving = []
    for i in range(REQUESTS):
        first = CHUNKS * STATE + sides[i // PER] * KEPT
        arriving.append(
            pltpu.make_async_copy(
                fetched.at[holder[i], pl.ds(first, KEPT)], starts.at[i], start_sems.at[i]
            )
        )
        arriving[i].start()
    for i in range(REQUESTS):
        arriving[i].wait()
        for k in range(KEPT):
            tiles[k * TILES : (k + 1) * TILES, :] = starts[i, k].astype(F32)
        for tile in range(TILES):
            rows[8 - KEPT : 8, tile * LANES : (tile + 1) * LANES] = tiles[
                pl.ds(tile, KEPT, stride=TILES), :
            ]
        rows[8:, :] = hidden[order[i]].astype(F32)
        total = jnp.zeros((HEAD, INNER), F32) + bias[...]
        for tap in range(KEPT + 1):
            first = 8 - KEPT + tap
            total = total + rows[first : first + HEAD, :] * weight[tap : tap + 1, :]
        head[i] = silu(total).astype(BF16)
    part = jnp.dot(
        head[...].reshape(REQUESTS * HEAD, INNER), x_weight[...], preferred_element_type=F32
    ).reshape(REQUESTS, HEAD, WIDE)
    head_sent[...] = part[:PER].astype(BF16)
    head_kept[...] = part[PER:]
    copies = []
    for i in range(REQUESTS):
        copies.append((head.at[i], conv_out.at[i, :HEAD]))
        if i < PER:
            copies.append((head_sent.at[i], sent.at[i, :HEAD]))
        else:
            copies.append((head_kept.at[i - PER], kept.at[i - PER, :HEAD]))
    copies = [
        pltpu.make_async_copy(source, target, sems.at[k])
        for k, (source, target) in enumerate(copies)
    ]
    for one in copies:
        one.start()
    for one in copies:
        one.wait()


def put_heads(order, holder, sides, hidden, fetched, weight, bias, x_weight, conv_out, sent, kept):
    anywhere = pl.BlockSpec(memory_space=pl.ANY)
    return pl.pallas_call(
        head_kernel,
        grid_spec=pltpu.PrefetchScalarGridSpec(
            num_scalar_prefetch=3,
            grid=(1,),
            in_specs=[
                pl.BlockSpec((REQUESTS, HEAD, INNER), lambda i, o, h, s: (0, 0, 0)),
                anywhere,
                pl.BlockSpec((KEPT + 1, INNER), lambda i, o, h, s: (0, 0)),
                pl.BlockSpec((1, INNER), lambda i, o, h, s: (0, 0)),
                pl.BlockSpec((INNER, WIDE), lambda i, o, h, s: (0, 0)),
                anywhere,
                anywhere,
                anywhere,
            ],
            out_specs=[anywhere, anywhere, anywhere],
            scratch_shapes=[
                pltpu.VMEM((REQUESTS, KEPT, TILES, LANES), BF16),
                pltpu.VMEM((8 + HEAD, INNER), F32),
                pltpu.VMEM((KEPT * TILES, LANES), F32),
                pltpu.VMEM((REQUESTS, HEAD, INNER), BF16),
                pltpu.VMEM((PER, HEAD, WIDE), BF16),
                pltpu.VMEM((PER, HEAD, WIDE), F32),
                pltpu.SemaphoreType.DMA((2 * REQUESTS,)),
                pltpu.SemaphoreType.DMA((REQUESTS,)),
            ],
        ),
        out_shape=[
            jax.ShapeDtypeStruct(conv_out.shape, conv_out.dtype),
            jax.ShapeDtypeStruct(sent.shape, sent.dtype),
            jax.ShapeDtypeStruct(kept.shape, kept.dtype),
        ],
        input_output_aliases={8: 0, 9: 1, 10: 2},
        compiler_params=params(),
        cost_estimate=cost(3, 4 * 2**20),
        name="put_heads",
    )(order, holder, sides, hidden, fetched, weight, bias, x_weight, conv_out, sent, kept)


def norm_kernel(parts, out):
    total = parts[0].astype(F32)
    for k in range(1, DEPTH):
        total = total + parts[k].astype(F32)
    rank = total[:, :RANK]
    inject = total[:, RANK : RANK + STATE]
    readout = total[:, RANK + STATE :]
    rank = rank * lax.rsqrt(jnp.mean(rank * rank, axis=1, keepdims=True) + EPSILON)
    inject = inject * lax.rsqrt(
        jnp.maximum(jnp.mean(inject * inject, axis=1, keepdims=True), NORM_FLOOR)
    )
    readout = readout * lax.rsqrt(
        jnp.maximum(jnp.mean(readout * readout, axis=1, keepdims=True), NORM_FLOOR)
    )
    joined = jnp.concatenate([rank, inject, readout], axis=1).astype(BF16)
    for k in range(DEPTH):
        out[k] = joined


def normalize(parts):
    return pl.pallas_call(
        norm_kernel,
        out_shape=jax.ShapeDtypeStruct((DEPTH, SHARE, WIDE), BF16),
        compiler_params=params(),
        cost_estimate=cost(1.5, 2**20),
        name="normalize",
    )(parts)


def scan_kernel(
    own, order_ref, holder, sides, normed_ref, dt_weight, dt_bias, a_log, skip, conv, gate, start,
    last, other_last, base, gated, final, dts, us, spread, rates, states,
):
    step = pl.program_id(0)
    to = holder[PER + step] if own else holder[step]

    @pl.when(step == 0)
    def _():
        rows_to_tiles(rates, 0, -LOG2_E * jnp.exp(a_log[...]))

    columns = normed_ref[0, :, RANK:].astype(F32).T
    for t in range(TURN):
        spread[t * 2 * STATE : (t + 1) * 2 * STATE, :] = jnp.broadcast_to(
            columns[:, t : t + 1], (2 * STATE, LANES)
        )
    if own:
        for which, (rows, at) in enumerate(((last, to), (other_last, holder[step]))):
            rows_to_tiles(states, 0, rows[0].astype(F32)[HEAD - KEPT :, :])
            for k in range(KEPT):
                final[at, STATE + which * KEPT + k] = states[
                    k * TILES : (k + 1) * TILES, :
                ].astype(BF16)
    for part in range(STATE // 8):
        for tile in range(TILES):
            states[pl.ds(part * 8 * TILES + tile, 8, stride=TILES), :] = start[
                0, part * TILES + tile
            ].astype(F32)
    rank = normed_ref[0, :, :RANK]
    pair = 2 * LANES
    for block in range(INNER // pair):
        cols = slice(block * pair, (block + 1) * pair)
        raw = jnp.dot(rank, dt_weight[:, cols], preferred_element_type=F32) + dt_bias[:, cols]
        dt = jnp.maximum(raw, 0.0) + jnp.log1p(jnp.exp(-jnp.abs(raw)))
        for k in range(2):
            tile = 2 * block + k
            dts[pl.ds(tile, TURN, stride=TILES), :] = dt[:, k * LANES : (k + 1) * LANES]
            us[pl.ds(tile, TURN, stride=TILES), :] = conv[
                0, :, tile * LANES : (tile + 1) * LANES
            ].astype(F32)
    decay = [rates[n * TILES : (n + 1) * TILES, :] for n in range(STATE)]

    def steps(i, carried):
        carried = list(carried)
        for k in range(UNROLL):
            t = i * UNROLL + k
            at = pl.multiple_of(t * TILES, TILES)
            row = pl.multiple_of(t * 2 * STATE, 2 * STATE)
            dt = dts[pl.ds(at, TILES), :]
            drive = dt * us[pl.ds(at, TILES), :]
            sums = [None] * 4
            for n in range(STATE):
                carried[n] = (
                    jnp.exp2(dt * decay[n]) * carried[n] + drive * spread[pl.ds(row + n, 1), :]
                )
                term = carried[n] * spread[pl.ds(row + STATE + n, 1), :]
                sums[n % 4] = term if sums[n % 4] is None else sums[n % 4] + term
            dts[pl.ds(at, TILES), :] = (sums[0] + sums[1]) + (sums[2] + sums[3])
        return tuple(carried)

    carried = tuple(states[n * TILES : (n + 1) * TILES, :] for n in range(STATE))
    carried = lax.fori_loop(0, TURN // UNROLL, steps, carried)
    for n in range(STATE):
        states[n * TILES : (n + 1) * TILES, :] = carried[n]
    for part in range(STATE // 8):
        for tile in range(TILES):
            final[to, part * TILES + tile] = states[
                pl.ds(part * 8 * TILES + tile, 8, stride=TILES), :
            ].astype(BF16)
    for tile in range(TILES):
        cols = slice(tile * LANES, (tile + 1) * LANES)
        z = gate[0, :, cols].astype(F32)
        y = dts[pl.ds(tile, TURN, stride=TILES), :] + skip[:, cols] * conv[0, :, cols].astype(F32)
        gated[0, :, cols] = (y * silu(z)).astype(BF16)


def scan(order, holder, sides, normed, dt_weight, dt_bias, a_log, skip, conv, gate, fetched, hidden, base):
    own = base is None
    first = PER if own else 0
    blocks = RETURNED if own else STATE
    whole = lambda shape: pl.BlockSpec(shape, lambda i, o, h, s: (0,) * len(shape))
    ends = lambda at: pl.BlockSpec(
        (1, HEAD, INNER), lambda i, o, h, s: (o[at + i], TURN // HEAD - 1, 0)
    )
    return pl.pallas_call(
        functools.partial(scan_kernel, own),
        grid_spec=pltpu.PrefetchScalarGridSpec(
            num_scalar_prefetch=3,
            grid=(PER,),
            in_specs=[
                pl.BlockSpec((1, TURN, WIDE), lambda i, o, h, s: (i, 0, 0)),
                whole((RANK, INNER)),
                whole((1, INNER)),
                whole((STATE, INNER)),
                whole((1, INNER)),
                pl.BlockSpec((1, TURN, INNER), lambda i, o, h, s: (first + i, 0, 0)),
                pl.BlockSpec((1, TURN, INNER), lambda i, o, h, s: (o[first + i], 0, 0)),
                pl.BlockSpec(
                    (1, STATE, TILES, LANES),
                    lambda i, o, h, s: (h[first + i], s[1 if own else 0], 0, 0),
                ),
                ends(PER),
                ends(0),
                pl.BlockSpec(memory_space=pl.ANY),
            ],
            out_specs=[
                pl.BlockSpec((1, TURN, INNER), lambda i, o, h, s: (o[first + i], 0, 0)),
                whole((GROUPS, blocks, TILES, LANES)),
            ],
            scratch_shapes=[
                pltpu.VMEM((TURN * TILES, LANES), F32),
                pltpu.VMEM((TURN * TILES, LANES), F32),
                pltpu.VMEM((TURN * 2 * STATE, LANES), F32),
                pltpu.VMEM((STATE * TILES, LANES), F32),
                pltpu.VMEM((STATE * TILES, LANES), F32),
            ],
        ),
        out_shape=[
            jax.ShapeDtypeStruct((REQUESTS, TURN, INNER), BF16),
            jax.ShapeDtypeStruct((GROUPS, blocks, TILES, LANES), BF16),
        ],
        input_output_aliases={} if own else {13: 0},
        compiler_params=params(),
        cost_estimate=cost(15, 4 * 2**20),
        name="scan",
    )(order, holder, sides, normed, dt_weight, dt_bias, a_log, skip, conv, gate, fetched, hidden,
      hidden, skip if own else base)


def widen(came, wide, g):
    for part in range(STATE // 8):
        for tile in range(TILES):
            rows, cols = block_of(part, tile)
            wide[g, rows, cols] = came[g, part * TILES + tile].astype(F32)


def place_kernel(
    slots, other_slots, taken, came, ssm, conv, new_ssm, new_conv, wide, inputs, sems, base_sems
):
    def base(s):
        return pltpu.make_async_copy(ssm.at[s], new_ssm.at[s], base_sems.at[s])

    def copy(g):
        return pltpu.make_async_copy(wide.at[g], new_ssm.at[slots[g]], sems.at[g])

    def begin_base(s, carry):
        @pl.when(taken[s] == 0)
        def _():
            base(s).start()

        return carry

    def finish_base(s, carry):
        @pl.when(taken[s] == 0)
        def _():
            base(s).wait()

        return carry

    def put(slot, g, first):
        for k in range(KEPT):
            row = pl.multiple_of((k * SLOTS + slot) * TILES, TILES)
            inputs[pl.ds(row, TILES), :] = came[g, first + k].astype(F32)

    def begin(g, carry):
        @pl.when(slots[g] < SLOTS)
        def _():
            widen(came, wide, g)
            copy(g).start()
            put(slots[g], g, STATE)

        @pl.when(other_slots[g] < SLOTS)
        def _():
            put(other_slots[g], g, STATE + KEPT)

        return carry

    def finish(g, carry):
        @pl.when(slots[g] < SLOTS)
        def _():
            copy(g).wait()

        return carry

    lax.fori_loop(0, SLOTS, begin_base, 0)
    for k in range(KEPT):
        rows_to_tiles(inputs, k * SLOTS * TILES, conv[k])
    lax.fori_loop(0, GROUPS, begin, 0)
    for k in range(KEPT):
        for tile in range(TILES):
            new_conv[k, :, tile * LANES : (tile + 1) * LANES] = inputs[
                pl.ds(k * SLOTS * TILES + tile, SLOTS, stride=TILES), :
            ]
    lax.fori_loop(0, GROUPS, finish, 0)
    lax.fori_loop(0, SLOTS, finish_base, 0)


def place(slots, other_slots, taken, came, ssm, conv):
    anywhere = pl.BlockSpec(memory_space=pl.ANY)
    rows = pl.BlockSpec((KEPT, SLOTS, INNER), lambda i, s, o, t: (0, 0, 0))
    return pl.pallas_call(
        place_kernel,
        grid_spec=pltpu.PrefetchScalarGridSpec(
            num_scalar_prefetch=3,
            grid=(1,),
            in_specs=[
                pl.BlockSpec((GROUPS, RETURNED, TILES, LANES), lambda i, s, o, t: (0, 0, 0, 0)),
                anywhere,
                rows,
            ],
            out_specs=[anywhere, rows],
            scratch_shapes=[
                pltpu.VMEM((GROUPS, STATE, INNER), F32),
                pltpu.VMEM((KEPT * SLOTS * TILES, LANES), F32),
                pltpu.SemaphoreType.DMA((GROUPS,)),
                pltpu.SemaphoreType.DMA((SLOTS,)),
            ],
        ),
        out_shape=[
            jax.ShapeDtypeStruct((SLOTS, STATE, INNER), F32),
            jax.ShapeDtypeStruct((KEPT, SLOTS, INNER), F32),
        ],
        compiler_params=params(),
        cost_estimate=cost(4, 6 * 2**20),
        name="place",
    )(slots, other_slots, taken, came, ssm, conv)


def store_kernel(slots, came, ssm_in, new_ssm, wide, sems):
    def copy(g):
        return pltpu.make_async_copy(wide.at[g], new_ssm.at[slots[g]], sems.at[g])

    def begin(g, carry):
        @pl.when(slots[g] < SLOTS)
        def _():
            widen(came, wide, g)
            copy(g).start()

        return carry

    def finish(g, carry):
        @pl.when(slots[g] < SLOTS)
        def _():
            copy(g).wait()

        return carry

    lax.fori_loop(0, GROUPS, begin, 0)
    lax.fori_loop(0, GROUPS, finish, 0)


def store(slots, came, ssm):
    anywhere = pl.BlockSpec(memory_space=pl.ANY)
    return pl.pallas_call(
        store_kernel,
        grid_spec=pltpu.PrefetchScalarGridSpec(
            num_scalar_prefetch=1,
            grid=(1,),
            in_specs=[
                pl.BlockSpec((GROUPS, STATE, TILES, LANES), lambda i, s: (0, 0, 0, 0)),
                anywhere,
            ],
            out_specs=anywhere,
            scratch_shapes=[
                pltpu.VMEM((GROUPS, STATE, INNER), F32),
                pltpu.SemaphoreType.DMA((GROUPS,)),
            ],
        ),
        out_shape=jax.ShapeDtypeStruct((SLOTS, STATE, INNER), F32),
        input_output_aliases={2: 0},
        compiler_params=params(),
        cost_estimate=cost(2, 2 * 2**20),
        name="store",
    )(slots, came, ssm)


def exchange(values, axis):
    return lax.all_to_all(values, axis, split_axis=0, concat_axis=0, tiled=True)


def body(
    hidden_x,
    gate_z,
    conv_weight,
    conv_bias,
    x_weight,
    dt_weight,
    dt_bias,
    a_log,
    skip_gain,
    ssm_cache,
    conv_cache,
    holder_of,
    slot_of,
):
    me = lax.axis_index("dp")
    core = lax.axis_index("core")
    holders = holder_of.reshape(GROUPS, REQUESTS)
    places = slot_of.reshape(GROUPS, REQUESTS)

    keys = holders * REQUESTS + jnp.arange(REQUESTS, dtype=jnp.int32)
    rank = jnp.sum((keys[:, None, :] < keys[:, :, None]).astype(jnp.int32), axis=2)
    served = (holders == me)[:, None, :] & (
        rank[:, None, :] % CHUNKS == jnp.arange(CHUNKS, dtype=jnp.int32)[None, :, None]
    )
    slots = jnp.sum(jnp.where(served, places[:, None, :], 0), axis=2)
    targets = jnp.where(jnp.any(served, axis=2), slots, SLOTS)
    own_slots = jnp.where(core == 0, targets[:, 0], targets[:, 1])
    other_slots = jnp.where(core == 0, targets[:, 1], targets[:, 0])
    taken = jnp.sum(
        (own_slots[None, :] == jnp.arange(SLOTS, dtype=jnp.int32)[:, None]).astype(jnp.int32),
        axis=1,
    )

    at = jnp.arange(REQUESTS, dtype=jnp.int32)
    sides = jnp.stack([1 - core, core]).astype(jnp.int32)
    number = at % PER * CHUNKS + jnp.where(at < PER, 1 - core, core)
    chosen = rank[me][None, :] == number[:, None]
    order = jnp.sum(jnp.where(chosen, at[None, :], 0), axis=1)
    holder = jnp.sum(jnp.where(chosen, holders[me][None, :], 0), axis=1)

    conv_rows = jnp.swapaxes(conv_cache, 0, 1)
    bias = conv_bias.reshape(1, INNER)
    fetched = exchange(pack(slots.reshape(-1), ssm_cache, conv_rows), "dp")
    conv, sent, kept = convolve(order, hidden_x, conv_weight, bias, x_weight)
    conv, sent, kept = put_heads(
        order, holder, sides, hidden_x, fetched, conv_weight, bias, x_weight, conv, sent, kept
    )
    parts = (kept + lax.ppermute(sent, "core", SWAP).astype(F32)).astype(BF16)
    share = normalize(exchange(parts.reshape(DEPTH, SHARE, WIDE), "z"))

    normed = exchange(share, "z").reshape(PER, TURN, WIDE)
    gated, came = None, []
    for values in (normed, lax.ppermute(normed, "core", SWAP)):
        gated, final = scan(
            order,
            holder,
            sides,
            values,
            dt_weight,
            dt_bias.reshape(1, INNER),
            a_log,
            skip_gain.reshape(1, INNER),
            conv,
            gate_z,
            fetched,
            hidden_x,
            gated,
        )
        came.append(exchange(final, "dp"))
    new_ssm, new_conv = place(own_slots, other_slots, taken, came[0], ssm_cache, conv_rows)
    new_ssm = store(other_slots, came[1], new_ssm)
    return (gated, new_ssm, jnp.swapaxes(new_conv, 0, 1))


def solution(mesh):
    fine = Mesh(mesh.devices.reshape(GROUPS, DEPTH, CORES), ("dp", "z", "core"))
    tensor = ("z", "core")
    placed = (
        P("dp", None, tensor),
        P("dp", None, tensor),
        P(None, tensor),
        P(tensor),
        P(tensor, None),
        P(None, tensor),
        P(tensor),
        P(None, tensor),
        P(tensor),
        P("dp", None, tensor),
        P("dp", None, tensor),
        P(),
        P(),
    )
    return jax.shard_map(
        body,
        mesh=fine,
        in_specs=placed,
        out_specs=(P("dp", None, tensor),) * 3,
        check_vma=False,
    )
```

```python
import functools

import jax
import jax.numpy as jnp
from jax import lax
from jax.experimental import pallas as pl
from jax.experimental.pallas import tpu as pltpu
from jax.sharding import Mesh, PartitionSpec as P

EPSILON = 1e-06
NORM_FLOOR = 0.25
LOG2_E = 1.4426950408889634

GROUPS = 16
REQUESTS = 8
CHUNKS = 2
PER = REQUESTS // CHUNKS
TURN = 128
INNER = 1024
RANK = 512
STATE = 16
USED = RANK + 2 * STATE
WIDE = 640
SLOTS = 32
KEPT = 3
DEPTH = 8
CORES = 2
SHARE = PER * TURN // DEPTH
HEAD = 16
EDGE = 4
EDGES = PER * EDGE
FETCHED = CHUNKS * (STATE + KEPT)
RETURNED = STATE + CHUNKS * KEPT
LANES = 128
TILES = INNER // LANES
UNROLL = 16

F32 = jnp.float32
BF16 = jnp.bfloat16
SWAP = [(0, 1), (1, 0)]


def params():
    return pltpu.CompilerParams(vmem_limit_bytes=56 * 2**20)


def cost(us, bytes_accessed):
    return pl.CostEstimate(
        flops=int(us * 1.0e9), bytes_accessed=bytes_accessed, transcendentals=0
    )


def rows_to_tiles(tiles, first, rows):
    for tile in range(TILES):
        tiles[pl.ds(first + tile, rows.shape[0], stride=TILES), :] = rows[
            :, tile * LANES : (tile + 1) * LANES
        ]


def block_of(part, tile):
    return slice(part * 8, (part + 1) * 8), slice(tile * LANES, (tile + 1) * LANES)


def pack_kernel(slots, ssm, conv, out, states, inputs, sems):
    def copy(e):
        return pltpu.make_async_copy(ssm.at[slots[e]], states.at[e], sems.at[e])

    def begin(e, carry):
        copy(e).start()
        return carry

    def finish(e, carry):
        g, c = e // CHUNKS, e % CHUNKS
        for k in range(KEPT):
            row = pl.multiple_of((k * SLOTS + slots[e]) * TILES, TILES)
            out[g, CHUNKS * STATE + c * KEPT + k] = inputs[pl.ds(row, TILES), :].astype(BF16)
        copy(e).wait()
        for part in range(STATE // 8):
            for tile in range(TILES):
                rows, cols = block_of(part, tile)
                out[g, c * STATE + part * TILES + tile] = states[e, rows, cols].astype(BF16)
        return carry

    lax.fori_loop(0, GROUPS * CHUNKS, begin, 0)
    for k in range(KEPT):
        rows_to_tiles(inputs, k * SLOTS * TILES, conv[k])
    lax.fori_loop(0, GROUPS * CHUNKS, finish, 0)


def pack(slots, ssm, conv):
    return pl.pallas_call(
        pack_kernel,
        grid_spec=pltpu.PrefetchScalarGridSpec(
            num_scalar_prefetch=1,
            grid=(1,),
            in_specs=[
                pl.BlockSpec(memory_space=pl.ANY),
                pl.BlockSpec((KEPT, SLOTS, INNER), lambda i, s: (0, 0, 0)),
            ],
            out_specs=pl.BlockSpec((GROUPS, FETCHED, TILES, LANES), lambda i, s: (0, 0, 0, 0)),
            scratch_shapes=[
                pltpu.VMEM((GROUPS * CHUNKS, STATE, INNER), F32),
                pltpu.VMEM((KEPT * SLOTS * TILES, LANES), F32),
                pltpu.SemaphoreType.DMA((GROUPS * CHUNKS,)),
            ],
        ),
        out_shape=jax.ShapeDtypeStruct((GROUPS, FETCHED, TILES, LANES), BF16),
        compiler_params=params(),
        cost_estimate=cost(3, 4 * 2**20),
        name="pack",
    )(slots, ssm, conv)


def silu(v):
    half = 0.5 * v
    return half + half * jnp.tanh(half)


def conv_kernel(order_ref, hidden, weight, bias, x_weight, conv_out, sent, kept, rows):
    step = pl.program_id(0)
    rows[:8, :] = jnp.zeros((8, INNER), F32)
    for tile in range(TILES):
        cols = slice(tile * LANES, (tile + 1) * LANES)
        rows[8:, cols] = hidden[0, :, cols].astype(F32)
        total = jnp.zeros((TURN, LANES), F32) + bias[:, cols]
        for tap in range(KEPT + 1):
            first = 8 - KEPT + tap
            total = total + rows[first : first + TURN, cols] * weight[tap : tap + 1, cols]
        conv_out[0, :, cols] = silu(total).astype(BF16)
    part = jnp.dot(conv_out[0], x_weight[...], preferred_element_type=F32)

    @pl.when(step < PER)
    def _():
        sent[0] = part.astype(BF16)

    @pl.when(step >= PER)
    def _():
        kept[0] = part


def convolve(order, hidden, weight, bias, x_weight):
    return pl.pallas_call(
        conv_kernel,
        grid_spec=pltpu.PrefetchScalarGridSpec(
            num_scalar_prefetch=1,
            grid=(REQUESTS,),
            in_specs=[
                pl.BlockSpec((1, TURN, INNER), lambda i, o: (o[i], 0, 0)),
                pl.BlockSpec((KEPT + 1, INNER), lambda i, o: (0, 0)),
                pl.BlockSpec((1, INNER), lambda i, o: (0, 0)),
                pl.BlockSpec((INNER, WIDE), lambda i, o: (0, 0)),
            ],
            out_specs=[
                pl.BlockSpec((1, TURN, INNER), lambda i, o: (i, 0, 0)),
                pl.BlockSpec((1, TURN, WIDE), lambda i, o: (jnp.minimum(i, PER - 1), 0, 0)),
                pl.BlockSpec((1, TURN, WIDE), lambda i, o: (jnp.maximum(i - PER, 0), 0, 0)),
            ],
            scratch_shapes=[pltpu.VMEM((8 + TURN, INNER), F32)],
        ),
        out_shape=[
            jax.ShapeDtypeStruct((REQUESTS, TURN, INNER), BF16),
            jax.ShapeDtypeStruct((PER, TURN, WIDE), BF16),
            jax.ShapeDtypeStruct((PER, TURN, WIDE), F32),
        ],
        compiler_params=params(),
        cost_estimate=cost(8, 8 * 2**20),
        name="convolve",
    )(order, hidden, weight, bias, x_weight)


def head_kernel(
    order, holder, sides, hidden, fetched, weight, bias, x_weight, conv_in,
    conv_out, sent, kept, starts, rows, tiles, head, sems, start_sems,
):
    arriving = []
    for i in range(REQUESTS):
        first = CHUNKS * STATE + sides[i // PER] * KEPT
        arriving.append(
            pltpu.make_async_copy(
                fetched.at[holder[i], pl.ds(first, KEPT)], starts.at[i], start_sems.at[i]
            )
        )
        arriving[i].start()
    leaving = []
    for i in range(REQUESTS):
        arriving[i].wait()
        for k in range(KEPT):
            tiles[k * TILES : (k + 1) * TILES, :] = starts[i, k].astype(F32)
        for tile in range(TILES):
            rows[8 - KEPT : 8, tile * LANES : (tile + 1) * LANES] = tiles[
                pl.ds(tile, KEPT, stride=TILES), :
            ]
        rows[8:, :] = hidden[order[i]].astype(F32)
        total = jnp.zeros((HEAD, INNER), F32) + bias[...]
        for tap in range(KEPT + 1):
            first = 8 - KEPT + tap
            total = total + rows[first : first + HEAD, :] * weight[tap : tap + 1, :]
        head[i] = silu(total).astype(BF16)
        leaving.append(pltpu.make_async_copy(head.at[i], conv_out.at[i, :HEAD], sems.at[i]))
        leaving[i].start()
    part = jnp.dot(
        head[...].reshape(REQUESTS * HEAD, INNER), x_weight[...], preferred_element_type=F32
    ).reshape(REQUESTS, HEAD, WIDE)[:, :EDGE]
    sent[...] = part[:PER].reshape(EDGES, WIDE).astype(BF16)
    kept[...] = part[PER:].reshape(EDGES, WIDE)
    for one in leaving:
        one.wait()


def put_heads(order, holder, sides, hidden, fetched, weight, bias, x_weight, conv_out):
    anywhere = pl.BlockSpec(memory_space=pl.ANY)
    edges = pl.BlockSpec((EDGES, WIDE), lambda i, o, h, s: (0, 0))
    return pl.pallas_call(
        head_kernel,
        grid_spec=pltpu.PrefetchScalarGridSpec(
            num_scalar_prefetch=3,
            grid=(1,),
            in_specs=[
                pl.BlockSpec((REQUESTS, HEAD, INNER), lambda i, o, h, s: (0, 0, 0)),
                anywhere,
                pl.BlockSpec((KEPT + 1, INNER), lambda i, o, h, s: (0, 0)),
                pl.BlockSpec((1, INNER), lambda i, o, h, s: (0, 0)),
                pl.BlockSpec((INNER, WIDE), lambda i, o, h, s: (0, 0)),
                anywhere,
            ],
            out_specs=[anywhere, edges, edges],
            scratch_shapes=[
                pltpu.VMEM((REQUESTS, KEPT, TILES, LANES), BF16),
                pltpu.VMEM((8 + HEAD, INNER), F32),
                pltpu.VMEM((KEPT * TILES, LANES), F32),
                pltpu.VMEM((REQUESTS, HEAD, INNER), BF16),
                pltpu.SemaphoreType.DMA((REQUESTS,)),
                pltpu.SemaphoreType.DMA((REQUESTS,)),
            ],
        ),
        out_shape=[
            jax.ShapeDtypeStruct(conv_out.shape, conv_out.dtype),
            jax.ShapeDtypeStruct((EDGES, WIDE), BF16),
            jax.ShapeDtypeStruct((EDGES, WIDE), F32),
        ],
        input_output_aliases={8: 0},
        compiler_params=params(),
        cost_estimate=cost(4, 4 * 2**20),
        name="put_heads",
    )(order, holder, sides, hidden, fetched, weight, bias, x_weight, conv_out)


def norm(total):
    rank = total[:, :RANK]
    inject = total[:, RANK : RANK + STATE]
    readout = total[:, RANK + STATE : USED]
    rank = rank * lax.rsqrt(jnp.mean(rank * rank, axis=1, keepdims=True) + EPSILON)
    inject = inject * lax.rsqrt(
        jnp.maximum(jnp.mean(inject * inject, axis=1, keepdims=True), NORM_FLOOR)
    )
    readout = readout * lax.rsqrt(
        jnp.maximum(jnp.mean(readout * readout, axis=1, keepdims=True), NORM_FLOOR)
    )
    rest = jnp.zeros((total.shape[0], WIDE - USED), F32)
    return jnp.concatenate([rank, inject, readout, rest], axis=1)


def norm_kernel(parts, edge, edge_came, out):
    total = parts[0].astype(F32)
    for k in range(1, DEPTH):
        total = total + parts[k].astype(F32)
    joined = norm(total).astype(BF16)
    edges = (edge[...] + edge_came[...].astype(F32)).astype(BF16)
    for k in range(DEPTH):
        out[k, :SHARE] = joined
        out[k, SHARE:] = edges


def normalize(parts, edge, edge_came):
    return pl.pallas_call(
        norm_kernel,
        out_shape=jax.ShapeDtypeStruct((DEPTH, SHARE + EDGES, WIDE), BF16),
        compiler_params=params(),
        cost_estimate=cost(1.5, 2**20),
        name="normalize",
    )(parts, edge, edge_came)


def scan_kernel(
    own, order_ref, holder, sides, shares, edge_parts, dt_weight, dt_bias, a_log, skip, conv, gate, start,
    last, other_last, base, gated, final, dts, us, spread, rates, states, edges,
):
    step = pl.program_id(0)
    to = holder[PER + step] if own else holder[step]

    @pl.when(step == 0)
    def _():
        rows_to_tiles(rates, 0, -LOG2_E * jnp.exp(a_log[...]))
        total = edge_parts[0, SHARE:].astype(F32)
        for k in range(1, DEPTH):
            total = total + edge_parts[k, SHARE:].astype(F32)
        total = norm(total).astype(BF16).astype(F32)
        for k in range(PER):
            edges[k, :EDGE] = total[k * EDGE : (k + 1) * EDGE]

    normed = jnp.concatenate([shares[0, :SHARE], shares[1, :SHARE]], axis=0).astype(F32)
    first = lax.broadcasted_iota(jnp.int32, (8, WIDE), 0) < KEPT
    normed = jnp.concatenate([jnp.where(first, edges[step], normed[:8]), normed[8:]], axis=0)
    columns = normed[:, RANK:].T[: 2 * STATE]
    for t in range(TURN):
        spread[t * 2 * STATE : (t + 1) * 2 * STATE, :] = jnp.broadcast_to(
            columns[:, t : t + 1], (2 * STATE, LANES)
        )
    if own:
        for which, (rows, at) in enumerate(((last, to), (other_last, holder[step]))):
            rows_to_tiles(states, 0, rows[0].astype(F32)[HEAD - KEPT :, :])
            for k in range(KEPT):
                final[at, STATE + which * KEPT + k] = states[
                    k * TILES : (k + 1) * TILES, :
                ].astype(BF16)
    for part in range(STATE // 8):
        for tile in range(TILES):
            states[pl.ds(part * 8 * TILES + tile, 8, stride=TILES), :] = start[
                0, part * TILES + tile
            ].astype(F32)
    rank = normed[:, :RANK].astype(BF16)
    pair = 2 * LANES
    for block in range(INNER // pair):
        cols = slice(block * pair, (block + 1) * pair)
        raw = jnp.dot(rank, dt_weight[:, cols], preferred_element_type=F32) + dt_bias[:, cols]
        dt = jnp.maximum(raw, 0.0) + jnp.log1p(jnp.exp(-jnp.abs(raw)))
        for k in range(2):
            tile = 2 * block + k
            dts[pl.ds(tile, TURN, stride=TILES), :] = dt[:, k * LANES : (k + 1) * LANES]
            us[pl.ds(tile, TURN, stride=TILES), :] = conv[
                0, :, tile * LANES : (tile + 1) * LANES
            ].astype(F32)
    decay = [rates[n * TILES : (n + 1) * TILES, :] for n in range(STATE)]

    def steps(i, carried):
        carried = list(carried)
        for k in range(UNROLL):
            t = i * UNROLL + k
            at = pl.multiple_of(t * TILES, TILES)
            row = pl.multiple_of(t * 2 * STATE, 2 * STATE)
            dt = dts[pl.ds(at, TILES), :]
            drive = dt * us[pl.ds(at, TILES), :]
            sums = [None] * 4
            for n in range(STATE):
                carried[n] = (
                    jnp.exp2(dt * decay[n]) * carried[n] + drive * spread[pl.ds(row + n, 1), :]
                )
                term = carried[n] * spread[pl.ds(row + STATE + n, 1), :]
                sums[n % 4] = term if sums[n % 4] is None else sums[n % 4] + term
            dts[pl.ds(at, TILES), :] = (sums[0] + sums[1]) + (sums[2] + sums[3])
        return tuple(carried)

    carried = tuple(states[n * TILES : (n + 1) * TILES, :] for n in range(STATE))
    carried = lax.fori_loop(0, TURN // UNROLL, steps, carried)
    for n in range(STATE):
        states[n * TILES : (n + 1) * TILES, :] = carried[n]
    for part in range(STATE // 8):
        for tile in range(TILES):
            final[to, part * TILES + tile] = states[
                pl.ds(part * 8 * TILES + tile, 8, stride=TILES), :
            ].astype(BF16)
    for tile in range(TILES):
        cols = slice(tile * LANES, (tile + 1) * LANES)
        z = gate[0, :, cols].astype(F32)
        y = dts[pl.ds(tile, TURN, stride=TILES), :] + skip[:, cols] * conv[0, :, cols].astype(F32)
        gated[0, :, cols] = (y * silu(z)).astype(BF16)


def scan(order, holder, sides, normed, dt_weight, dt_bias, a_log, skip, conv, gate, fetched, hidden, base):
    own = base is None
    first = PER if own else 0
    blocks = RETURNED if own else STATE
    whole = lambda shape: pl.BlockSpec(shape, lambda i, o, h, s: (0,) * len(shape))
    ends = lambda at: pl.BlockSpec(
        (1, HEAD, INNER), lambda i, o, h, s: (o[at + i], TURN // HEAD - 1, 0)
    )
    return pl.pallas_call(
        functools.partial(scan_kernel, own),
        grid_spec=pltpu.PrefetchScalarGridSpec(
            num_scalar_prefetch=3,
            grid=(PER,),
            in_specs=[
                pl.BlockSpec((DEPTH // PER, SHARE + EDGES, WIDE), lambda i, o, h, s: (i, 0, 0)),
                whole((DEPTH, SHARE + EDGES, WIDE)),
                whole((RANK, INNER)),
                whole((1, INNER)),
                whole((STATE, INNER)),
                whole((1, INNER)),
                pl.BlockSpec((1, TURN, INNER), lambda i, o, h, s: (first + i, 0, 0)),
                pl.BlockSpec((1, TURN, INNER), lambda i, o, h, s: (o[first + i], 0, 0)),
                pl.BlockSpec(
                    (1, STATE, TILES, LANES),
                    lambda i, o, h, s: (h[first + i], s[1 if own else 0], 0, 0),
                ),
                ends(PER),
                ends(0),
                pl.BlockSpec(memory_space=pl.ANY),
            ],
            out_specs=[
                pl.BlockSpec((1, TURN, INNER), lambda i, o, h, s: (o[first + i], 0, 0)),
                whole((GROUPS, blocks, TILES, LANES)),
            ],
            scratch_shapes=[
                pltpu.VMEM((TURN * TILES, LANES), F32),
                pltpu.VMEM((TURN * TILES, LANES), F32),
                pltpu.VMEM((TURN * 2 * STATE, LANES), F32),
                pltpu.VMEM((STATE * TILES, LANES), F32),
                pltpu.VMEM((STATE * TILES, LANES), F32),
                pltpu.VMEM((PER, 8, WIDE), F32),
            ],
        ),
        out_shape=[
            jax.ShapeDtypeStruct((REQUESTS, TURN, INNER), BF16),
            jax.ShapeDtypeStruct((GROUPS, blocks, TILES, LANES), BF16),
        ],
        input_output_aliases={} if own else {14: 0},
        compiler_params=params(),
        cost_estimate=cost(15, 4 * 2**20),
        name="scan",
    )(order, holder, sides, normed, normed, dt_weight, dt_bias, a_log, skip, conv, gate, fetched, hidden,
      hidden, skip if own else base)


def widen(came, wide, g, row):
    for part in range(STATE // 8):
        for tile in range(TILES):
            rows, cols = block_of(part, tile)
            wide[row, rows, cols] = came[g, part * TILES + tile].astype(F32)


def place_kernel(slots, other_slots, came, ssm, conv, new_ssm, new_conv, inputs, sem):
    base = pltpu.make_async_copy(ssm, new_ssm, sem)
    base.start()
    for k in range(KEPT):
        rows_to_tiles(inputs, k * SLOTS * TILES, conv[k])

    def put(slot, g, first):
        for k in range(KEPT):
            row = pl.multiple_of((k * SLOTS + slot) * TILES, TILES)
            inputs[pl.ds(row, TILES), :] = came[g, first + k].astype(F32)

    def each(g, carry):
        @pl.when(slots[g] < SLOTS)
        def _():
            widen(came, new_ssm, g, slots[g])
            put(slots[g], g, STATE)

        @pl.when(other_slots[g] < SLOTS)
        def _():
            put(other_slots[g], g, STATE + KEPT)

        return carry

    base.wait()
    lax.fori_loop(0, GROUPS, each, 0)
    for k in range(KEPT):
        for tile in range(TILES):
            new_conv[k, :, tile * LANES : (tile + 1) * LANES] = inputs[
                pl.ds(k * SLOTS * TILES + tile, SLOTS, stride=TILES), :
            ]


def place(slots, other_slots, came, ssm, conv):
    rows = pl.BlockSpec((KEPT, SLOTS, INNER), lambda i, s, o: (0, 0, 0))
    return pl.pallas_call(
        place_kernel,
        grid_spec=pltpu.PrefetchScalarGridSpec(
            num_scalar_prefetch=2,
            grid=(1,),
            in_specs=[
                pl.BlockSpec((GROUPS, RETURNED, TILES, LANES), lambda i, s, o: (0, 0, 0, 0)),
                pl.BlockSpec(memory_space=pl.ANY),
                rows,
            ],
            out_specs=[pl.BlockSpec((SLOTS, STATE, INNER), lambda i, s, o: (0, 0, 0)), rows],
            scratch_shapes=[
                pltpu.VMEM((KEPT * SLOTS * TILES, LANES), F32),
                pltpu.SemaphoreType.DMA,
            ],
        ),
        out_shape=[
            jax.ShapeDtypeStruct((SLOTS, STATE, INNER), F32),
            jax.ShapeDtypeStruct((KEPT, SLOTS, INNER), F32),
        ],
        compiler_params=params(),
        cost_estimate=cost(6, 6 * 2**20),
        name="place",
    )(slots, other_slots, came, ssm, conv)


def store_kernel(slots, came, ssm_in, new_ssm, wide, sems):
    def copy(g):
        return pltpu.make_async_copy(wide.at[g], new_ssm.at[slots[g]], sems.at[g])

    def begin(g, carry):
        @pl.when(slots[g] < SLOTS)
        def _():
            widen(came, wide, g, g)
            copy(g).start()

        return carry

    def finish(g, carry):
        @pl.when(slots[g] < SLOTS)
        def _():
            copy(g).wait()

        return carry

    lax.fori_loop(0, GROUPS, begin, 0)
    lax.fori_loop(0, GROUPS, finish, 0)


def store(slots, came, ssm):
    anywhere = pl.BlockSpec(memory_space=pl.ANY)
    return pl.pallas_call(
        store_kernel,
        grid_spec=pltpu.PrefetchScalarGridSpec(
            num_scalar_prefetch=1,
            grid=(1,),
            in_specs=[
                pl.BlockSpec((GROUPS, STATE, TILES, LANES), lambda i, s: (0, 0, 0, 0)),
                anywhere,
            ],
            out_specs=anywhere,
            scratch_shapes=[
                pltpu.VMEM((GROUPS, STATE, INNER), F32),
                pltpu.SemaphoreType.DMA((GROUPS,)),
            ],
        ),
        out_shape=jax.ShapeDtypeStruct((SLOTS, STATE, INNER), F32),
        input_output_aliases={2: 0},
        compiler_params=params(),
        cost_estimate=cost(2, 2 * 2**20),
        name="store",
    )(slots, came, ssm)


def exchange(values, axis):
    return lax.all_to_all(values, axis, split_axis=0, concat_axis=0, tiled=True)


def body(
    hidden_x,
    gate_z,
    conv_weight,
    conv_bias,
    x_weight,
    dt_weight,
    dt_bias,
    a_log,
    skip_gain,
    ssm_cache,
    conv_cache,
    holder_of,
    slot_of,
):
    me = lax.axis_index("dp")
    core = lax.axis_index("core")
    holders = holder_of.reshape(GROUPS, REQUESTS)
    places = slot_of.reshape(GROUPS, REQUESTS)

    keys = holders * REQUESTS + jnp.arange(REQUESTS, dtype=jnp.int32)
    rank = jnp.sum((keys[:, None, :] < keys[:, :, None]).astype(jnp.int32), axis=2)
    served = (holders == me)[:, None, :] & (
        rank[:, None, :] % CHUNKS == jnp.arange(CHUNKS, dtype=jnp.int32)[None, :, None]
    )
    slots = jnp.sum(jnp.where(served, places[:, None, :], 0), axis=2)
    targets = jnp.where(jnp.any(served, axis=2), slots, SLOTS)
    own_slots = jnp.where(core == 0, targets[:, 0], targets[:, 1])
    other_slots = jnp.where(core == 0, targets[:, 1], targets[:, 0])

    at = jnp.arange(REQUESTS, dtype=jnp.int32)
    sides = jnp.stack([1 - core, core]).astype(jnp.int32)
    number = at % PER * CHUNKS + jnp.where(at < PER, 1 - core, core)
    chosen = rank[me][None, :] == number[:, None]
    order = jnp.sum(jnp.where(chosen, at[None, :], 0), axis=1)
    holder = jnp.sum(jnp.where(chosen, holders[me][None, :], 0), axis=1)

    conv_rows = jnp.swapaxes(conv_cache, 0, 1)
    bias = conv_bias.reshape(1, INNER)
    x_weight = jnp.pad(x_weight, ((0, 0), (0, WIDE - USED)))
    packed = pack(slots.reshape(-1), ssm_cache, conv_rows)
    packed, order, x_weight = lax.optimization_barrier((packed, order, x_weight))
    fetched = exchange(packed, "dp")
    conv, sent, kept = convolve(order, hidden_x, conv_weight, bias, x_weight)
    parts = (kept + lax.ppermute(sent, "core", SWAP).astype(F32)).astype(BF16)
    parts, fetched = lax.optimization_barrier((parts, fetched))
    parts = exchange(parts.reshape(DEPTH, SHARE, WIDE), "z")
    conv, edge_sent, edge = put_heads(
        order, holder, sides, hidden_x, fetched, conv_weight, bias, x_weight, conv
    )
    normed = exchange(normalize(parts, edge, lax.ppermute(edge_sent, "core", SWAP)), "z")
    gated, came = None, []
    for values in (normed, lax.ppermute(normed, "core", SWAP)):
        gated, final = scan(
            order,
            holder,
            sides,
            values,
            dt_weight,
            dt_bias.reshape(1, INNER),
            a_log,
            skip_gain.reshape(1, INNER),
            conv,
            gate_z,
            fetched,
            hidden_x,
            gated,
        )
        if came:
            came[0], final = lax.optimization_barrier((came[0], final))
        came.append(exchange(final, "dp"))
    new_ssm, new_conv = place(own_slots, other_slots, came[0], ssm_cache, conv_rows)
    new_ssm = store(other_slots, came[1], new_ssm)
    return (gated, new_ssm, jnp.swapaxes(new_conv, 0, 1))


def solution(mesh):
    fine = Mesh(mesh.devices.reshape(GROUPS, DEPTH, CORES), ("dp", "z", "core"))
    tensor = ("z", "core")
    placed = (
        P("dp", None, tensor),
        P("dp", None, tensor),
        P(None, tensor),
        P(tensor),
        P(tensor, None),
        P(None, tensor),
        P(tensor),
        P(None, tensor),
        P(tensor),
        P("dp", None, tensor),
        P("dp", None, tensor),
        P(),
        P(),
    )
    return jax.shard_map(
        body,
        mesh=fine,
        in_specs=placed,
        out_specs=(P("dp", None, tensor),) * 3,
        check_vma=False,
    )
```

```python
import functools

import jax
import jax.numpy as jnp
from jax import lax
from jax.experimental import pallas as pl
from jax.experimental.pallas import tpu as pltpu
from jax.sharding import Mesh, PartitionSpec as P

EPSILON = 1e-06
NORM_FLOOR = 0.25
LOG2_E = 1.4426950408889634

GROUPS = 16
REQUESTS = 8
CHUNKS = 2
PER = REQUESTS // CHUNKS
TURN = 128
INNER = 1024
RANK = 512
STATE = 16
USED = RANK + 2 * STATE
WIDE = 640
SLOTS = 32
KEPT = 3
DEPTH = 8
CORES = 2
SHARE = PER * TURN // DEPTH
HEAD = 16
EDGE = 4
EDGES = PER * EDGE
PAIR = 2

ORDER, HOLDER, OWN, OTHER, SIDES, ROUTING = 0, 8, 16, 32, 48, 64
FETCHED = CHUNKS * (STATE + KEPT)
RETURNED = STATE + CHUNKS * KEPT
LANES = 128
TILES = INNER // LANES
UNROLL = 16

F32 = jnp.float32
BF16 = jnp.bfloat16
SWAP = [(0, 1), (1, 0)]


def params():
    return pltpu.CompilerParams(vmem_limit_bytes=56 * 2**20)


def cost(us, bytes_accessed):
    return pl.CostEstimate(
        flops=int(us * 1.0e9), bytes_accessed=bytes_accessed, transcendentals=0
    )


def rows_to_tiles(tiles, first, rows):
    for tile in range(TILES):
        tiles[pl.ds(first + tile, rows.shape[0], stride=TILES), :] = rows[
            :, tile * LANES : (tile + 1) * LANES
        ]


def block_of(part, tile):
    return slice(part * 8, (part + 1) * 8), slice(tile * LANES, (tile + 1) * LANES)


def pack_kernel(
    holders, places, ssm, conv, routing, out, slots, ranks, states, inputs, packed, sems, out_sems
):
    me = lax.axis_index("dp")
    core = lax.axis_index("core")

    def copy(e):
        return pltpu.make_async_copy(ssm.at[slots[e]], states.at[e], sems.at[e])

    def begin(g, carry):
        held = [holders[g * REQUESTS + i] for i in range(REQUESTS)]
        rank = [jnp.int32(0)] * REQUESTS
        for i in range(REQUESTS):
            for j in range(i + 1, REQUESTS):
                below = (held[j] < held[i]).astype(jnp.int32)
                rank[i] = rank[i] + below
                rank[j] = rank[j] + (1 - below)
        found = [jnp.int32(-1)] * CHUNKS
        for i in range(REQUESTS):
            here = held[i] == me
            place = places[g * REQUESTS + i]
            for c in range(CHUNKS):
                found[c] = jnp.where(here & (rank[i] % CHUNKS == c), place, found[c])
            ranks[g * REQUESTS + i] = rank[i]
        for c in range(CHUNKS):
            slots[g * CHUNKS + c] = jnp.maximum(found[c], 0)
            copy(g * CHUNKS + c).start()
        first = jnp.where(found[0] < 0, SLOTS, found[0])
        second = jnp.where(found[1] < 0, SLOTS, found[1])
        routing[OWN + g] = jnp.where(core == 0, first, second)
        routing[OTHER + g] = jnp.where(core == 0, second, first)
        return carry

    lax.fori_loop(0, GROUPS, begin, 0)
    for i in range(REQUESTS):
        rank = ranks[me * REQUESTS + i]
        at = rank // CHUNKS + jnp.where(rank % CHUNKS == core, PER, 0)
        routing[ORDER + at] = jnp.int32(i)
        routing[HOLDER + at] = holders[me * REQUESTS + i]
    routing[SIDES] = 1 - core
    routing[SIDES + 1] = core
    for k in range(KEPT):
        rows_to_tiles(inputs, k * SLOTS * TILES, conv[k])

    def finish(g, carry):
        for c in range(CHUNKS):
            e = g * CHUNKS + c
            for k in range(KEPT):
                row = pl.multiple_of((k * SLOTS + slots[e]) * TILES, TILES)
                packed[g, CHUNKS * STATE + c * KEPT + k] = inputs[pl.ds(row, TILES), :].astype(BF16)
            copy(e).wait()
            for part in range(STATE // 8):
                for tile in range(TILES):
                    rows, cols = block_of(part, tile)
                    packed[g, c * STATE + part * TILES + tile] = states[e, rows, cols].astype(BF16)
        pltpu.make_async_copy(packed.at[g], out.at[g], out_sems.at[g]).start()
        return carry

    def end(g, carry):
        pltpu.make_async_copy(packed.at[g], out.at[g], out_sems.at[g]).wait()
        return carry

    lax.fori_loop(0, GROUPS, finish, 0)
    lax.fori_loop(0, GROUPS, end, 0)


def pack(holders, places, ssm, conv):
    anywhere = pl.BlockSpec(memory_space=pl.ANY)
    return pl.pallas_call(
        pack_kernel,
        grid_spec=pltpu.PrefetchScalarGridSpec(
            num_scalar_prefetch=2,
            grid=(1,),
            in_specs=[
                anywhere,
                pl.BlockSpec((KEPT, SLOTS, INNER), lambda i, h, p: (0, 0, 0)),
            ],
            out_specs=[pl.BlockSpec(memory_space=pltpu.SMEM), anywhere],
            scratch_shapes=[
                pltpu.SMEM((GROUPS * CHUNKS,), jnp.int32),
                pltpu.SMEM((GROUPS * REQUESTS,), jnp.int32),
                pltpu.VMEM((GROUPS * CHUNKS, STATE, INNER), F32),
                pltpu.VMEM((KEPT * SLOTS * TILES, LANES), F32),
                pltpu.VMEM((GROUPS, FETCHED, TILES, LANES), BF16),
                pltpu.SemaphoreType.DMA((GROUPS * CHUNKS,)),
                pltpu.SemaphoreType.DMA((GROUPS,)),
            ],
        ),
        out_shape=[
            jax.ShapeDtypeStruct((ROUTING,), jnp.int32),
            jax.ShapeDtypeStruct((GROUPS, FETCHED, TILES, LANES), BF16),
        ],
        compiler_params=params(),
        cost_estimate=cost(4, 4 * 2**20),
        name="pack",
    )(holders, places, ssm, conv)


def silu(v):
    half = 0.5 * v
    return half + half * jnp.tanh(half)


def project(values, x_weight):
    return lax.dot_general(
        values, x_weight[...], (((1,), (1,)), ((), ())), preferred_element_type=F32
    )


def conv_kernel(
    routing, hidden, hidden_too, weight, bias, x_weight, conv_out, sent, kept, rows
):
    step = pl.program_id(0)
    rows[:8, :] = jnp.zeros((8, INNER), F32)
    for which, source in enumerate((hidden, hidden_too)):
        for tile in range(TILES):
            cols = slice(tile * LANES, (tile + 1) * LANES)
            rows[8:, cols] = source[0, :, cols].astype(F32)
            total = jnp.zeros((TURN, LANES), F32) + bias[:, cols]
            for tap in range(KEPT + 1):
                first = 8 - KEPT + tap
                total = total + rows[first : first + TURN, cols] * weight[tap : tap + 1, cols]
            conv_out[which, :, cols] = silu(total).astype(BF16)
    part = project(conv_out[...].reshape(PAIR * TURN, INNER), x_weight).reshape(PAIR, TURN, USED)
    rest = jnp.zeros((PAIR, TURN, WIDE - USED), F32)

    @pl.when(step < PER // PAIR)
    def _():
        sent[:, :, :USED] = part.astype(BF16)
        sent[:, :, USED:] = rest.astype(BF16)

    @pl.when(step >= PER // PAIR)
    def _():
        kept[:, :, :USED] = part
        kept[:, :, USED:] = rest


def convolve(routing, hidden, weight, bias, x_weight):
    half = PER // PAIR
    return pl.pallas_call(
        conv_kernel,
        grid_spec=pltpu.PrefetchScalarGridSpec(
            num_scalar_prefetch=1,
            grid=(REQUESTS // PAIR,),
            in_specs=[
                pl.BlockSpec((1, TURN, INNER), lambda i, r: (r[ORDER + PAIR * i], 0, 0)),
                pl.BlockSpec((1, TURN, INNER), lambda i, r: (r[ORDER + PAIR * i + 1], 0, 0)),
                pl.BlockSpec((KEPT + 1, INNER), lambda i, r: (0, 0)),
                pl.BlockSpec((1, INNER), lambda i, r: (0, 0)),
                pl.BlockSpec((USED, INNER), lambda i, r: (0, 0)),
            ],
            out_specs=[
                pl.BlockSpec((PAIR, TURN, INNER), lambda i, r: (i, 0, 0)),
                pl.BlockSpec((PAIR, TURN, WIDE), lambda i, r: (jnp.minimum(i, half - 1), 0, 0)),
                pl.BlockSpec((PAIR, TURN, WIDE), lambda i, r: (jnp.maximum(i - half, 0), 0, 0)),
            ],
            scratch_shapes=[pltpu.VMEM((8 + TURN, INNER), F32)],
        ),
        out_shape=[
            jax.ShapeDtypeStruct((REQUESTS, TURN, INNER), BF16),
            jax.ShapeDtypeStruct((PER, TURN, WIDE), BF16),
            jax.ShapeDtypeStruct((PER, TURN, WIDE), F32),
        ],
        compiler_params=params(),
        cost_estimate=cost(8, 8 * 2**20),
        name="convolve",
    )(routing, hidden, hidden, weight, bias, x_weight)


def head_kernel(
    routing, hidden, fetched, weight, bias, x_weight, conv_in,
    conv_out, sent, kept, starts, rows, tiles, head, sems, start_sems,
):
    arriving = []
    for i in range(REQUESTS):
        first = CHUNKS * STATE + routing[SIDES + i // PER] * KEPT
        arriving.append(
            pltpu.make_async_copy(
                fetched.at[routing[HOLDER + i], pl.ds(first, KEPT)], starts.at[i], start_sems.at[i]
            )
        )
        arriving[i].start()
    leaving = []
    for i in range(REQUESTS):
        arriving[i].wait()
        for k in range(KEPT):
            tiles[k * TILES : (k + 1) * TILES, :] = starts[i, k].astype(F32)
        for tile in range(TILES):
            rows[8 - KEPT : 8, tile * LANES : (tile + 1) * LANES] = tiles[
                pl.ds(tile, KEPT, stride=TILES), :
            ]
        rows[8:, :] = hidden[routing[ORDER + i]].astype(F32)
        total = jnp.zeros((HEAD, INNER), F32) + bias[...]
        for tap in range(KEPT + 1):
            first = 8 - KEPT + tap
            total = total + rows[first : first + HEAD, :] * weight[tap : tap + 1, :]
        head[i] = silu(total).astype(BF16)
        leaving.append(pltpu.make_async_copy(head.at[i], conv_out.at[i, :HEAD], sems.at[i]))
        leaving[i].start()
    part = project(head[...].reshape(REQUESTS * HEAD, INNER), x_weight)
    part = part.reshape(REQUESTS, HEAD, USED)[:, :EDGE]
    rest = jnp.zeros((EDGES, WIDE - USED), F32)
    sent[:, :USED] = part[:PER].reshape(EDGES, USED).astype(BF16)
    sent[:, USED:] = rest.astype(BF16)
    kept[:, :USED] = part[PER:].reshape(EDGES, USED)
    kept[:, USED:] = rest
    for one in leaving:
        one.wait()


def put_heads(routing, hidden, fetched, weight, bias, x_weight, conv_out):
    anywhere = pl.BlockSpec(memory_space=pl.ANY)
    edges = pl.BlockSpec((EDGES, WIDE), lambda i, r: (0, 0))
    return pl.pallas_call(
        head_kernel,
        grid_spec=pltpu.PrefetchScalarGridSpec(
            num_scalar_prefetch=1,
            grid=(1,),
            in_specs=[
                pl.BlockSpec((REQUESTS, HEAD, INNER), lambda i, r: (0, 0, 0)),
                anywhere,
                pl.BlockSpec((KEPT + 1, INNER), lambda i, r: (0, 0)),
                pl.BlockSpec((1, INNER), lambda i, r: (0, 0)),
                pl.BlockSpec((USED, INNER), lambda i, r: (0, 0)),
                anywhere,
            ],
            out_specs=[anywhere, edges, edges],
            scratch_shapes=[
                pltpu.VMEM((REQUESTS, KEPT, TILES, LANES), BF16),
                pltpu.VMEM((8 + HEAD, INNER), F32),
                pltpu.VMEM((KEPT * TILES, LANES), F32),
                pltpu.VMEM((REQUESTS, HEAD, INNER), BF16),
                pltpu.SemaphoreType.DMA((REQUESTS,)),
                pltpu.SemaphoreType.DMA((REQUESTS,)),
            ],
        ),
        out_shape=[
            jax.ShapeDtypeStruct(conv_out.shape, conv_out.dtype),
            jax.ShapeDtypeStruct((EDGES, WIDE), BF16),
            jax.ShapeDtypeStruct((EDGES, WIDE), F32),
        ],
        input_output_aliases={6: 0},
        compiler_params=params(),
        cost_estimate=cost(4, 4 * 2**20),
        name="put_heads",
    )(routing, hidden, fetched, weight, bias, x_weight, conv_out)


def norm(total):
    rank = total[:, :RANK]
    inject = total[:, RANK : RANK + STATE]
    readout = total[:, RANK + STATE : USED]
    rank = rank * lax.rsqrt(jnp.mean(rank * rank, axis=1, keepdims=True) + EPSILON)
    inject = inject * lax.rsqrt(
        jnp.maximum(jnp.mean(inject * inject, axis=1, keepdims=True), NORM_FLOOR)
    )
    readout = readout * lax.rsqrt(
        jnp.maximum(jnp.mean(readout * readout, axis=1, keepdims=True), NORM_FLOOR)
    )
    rest = jnp.zeros((total.shape[0], WIDE - USED), F32)
    return jnp.concatenate([rank, inject, readout, rest], axis=1)


def norm_kernel(parts, edge, edge_came, out, came, sem):
    arriving = pltpu.make_async_copy(edge_came, came, sem)
    arriving.start()
    total = parts[0].astype(F32)
    for k in range(1, DEPTH):
        total = total + parts[k].astype(F32)
    joined = norm(total).astype(BF16)
    arriving.wait()
    edges = (edge[...] + came[...].astype(F32)).astype(BF16)
    for k in range(DEPTH):
        out[k, :SHARE] = joined
        out[k, SHARE:] = edges


def normalize(parts, edge, edge_came):
    return pl.pallas_call(
        norm_kernel,
        in_specs=[
            pl.BlockSpec(memory_space=pltpu.VMEM),
            pl.BlockSpec(memory_space=pltpu.VMEM),
            pl.BlockSpec(memory_space=pl.ANY),
        ],
        scratch_shapes=[pltpu.VMEM((EDGES, WIDE), BF16), pltpu.SemaphoreType.DMA],
        out_shape=jax.ShapeDtypeStruct((DEPTH, SHARE + EDGES, WIDE), BF16),
        compiler_params=params(),
        cost_estimate=cost(1.5, 2**20),
        name="normalize",
    )(parts, edge, edge_came)


def scan_kernel(
    own, routing, came, dt_weight, dt_bias, a_log, skip, conv, gate, start,
    last, other_last, base, gated, final, dts, us, spread, rates, states, shares, sem,
):
    step = pl.program_id(0)
    to = routing[HOLDER + (PER if own else 0) + step]

    @pl.when(step == 0)
    def _():
        arriving = pltpu.make_async_copy(came, shares, sem)
        arriving.start()
        rows_to_tiles(rates, 0, -LOG2_E * jnp.exp(a_log[...]))
        arriving.wait()
        total = shares[0, SHARE:].astype(F32)
        for k in range(1, DEPTH):
            total = total + shares[k, SHARE:].astype(F32)
        total = norm(total)
        edge = lax.broadcasted_iota(jnp.int32, (HEAD, WIDE), 0) < KEPT
        rest = jnp.zeros((HEAD - EDGE, WIDE), F32)
        for k in range(PER):
            at = k * (DEPTH // PER)
            first = jnp.concatenate([total[k * EDGE : (k + 1) * EDGE], rest], axis=0)
            shares[at, :HEAD] = jnp.where(edge, first, shares[at, :HEAD].astype(F32)).astype(BF16)

    span = DEPTH // PER
    normed = shares[pl.ds(step * span, span), :SHARE].reshape(TURN, WIDE)
    columns = normed[:, RANK:].astype(F32).T[: 2 * STATE]
    for t in range(TURN):
        spread[t * 2 * STATE : (t + 1) * 2 * STATE, :] = jnp.broadcast_to(
            columns[:, t : t + 1], (2 * STATE, LANES)
        )
    if own:
        for which, (rows, at) in enumerate(((last, to), (other_last, routing[HOLDER + step]))):
            rows_to_tiles(states, 0, rows[0].astype(F32)[HEAD - KEPT :, :])
            for k in range(KEPT):
                final[at, STATE + which * KEPT + k] = states[
                    k * TILES : (k + 1) * TILES, :
                ].astype(BF16)
    for part in range(STATE // 8):
        for tile in range(TILES):
            states[pl.ds(part * 8 * TILES + tile, 8, stride=TILES), :] = start[
                0, part * TILES + tile
            ].astype(F32)
    rank = normed[:, :RANK]
    pair = 2 * LANES
    for block in range(INNER // pair):
        cols = slice(block * pair, (block + 1) * pair)
        raw = jnp.dot(rank, dt_weight[:, cols], preferred_element_type=F32) + dt_bias[:, cols]
        dt = jnp.maximum(raw, 0.0) + jnp.log1p(jnp.exp(-jnp.abs(raw)))
        for k in range(2):
            tile = 2 * block + k
            dts[pl.ds(tile, TURN, stride=TILES), :] = dt[:, k * LANES : (k + 1) * LANES]
            us[pl.ds(tile, TURN, stride=TILES), :] = conv[
                0, :, tile * LANES : (tile + 1) * LANES
            ].astype(F32)
    decay = [rates[n * TILES : (n + 1) * TILES, :] for n in range(STATE)]

    def steps(i, carried):
        carried = list(carried)
        for k in range(UNROLL):
            t = i * UNROLL + k
            at = pl.multiple_of(t * TILES, TILES)
            row = pl.multiple_of(t * 2 * STATE, 2 * STATE)
            dt = dts[pl.ds(at, TILES), :]
            drive = dt * us[pl.ds(at, TILES), :]
            sums = [None] * 4
            for n in range(STATE):
                carried[n] = (
                    jnp.exp2(dt * decay[n]) * carried[n] + drive * spread[pl.ds(row + n, 1), :]
                )
                term = carried[n] * spread[pl.ds(row + STATE + n, 1), :]
                sums[n % 4] = term if sums[n % 4] is None else sums[n % 4] + term
            dts[pl.ds(at, TILES), :] = (sums[0] + sums[1]) + (sums[2] + sums[3])
        return tuple(carried)

    carried = tuple(states[n * TILES : (n + 1) * TILES, :] for n in range(STATE))
    carried = lax.fori_loop(0, TURN // UNROLL, steps, carried)
    for n in range(STATE):
        states[n * TILES : (n + 1) * TILES, :] = carried[n]
    for part in range(STATE // 8):
        for tile in range(TILES):
            final[to, part * TILES + tile] = states[
                pl.ds(part * 8 * TILES + tile, 8, stride=TILES), :
            ].astype(BF16)
    for tile in range(TILES):
        cols = slice(tile * LANES, (tile + 1) * LANES)
        z = gate[0, :, cols].astype(F32)
        y = dts[pl.ds(tile, TURN, stride=TILES), :] + skip[:, cols] * conv[0, :, cols].astype(F32)
        gated[0, :, cols] = (y * silu(z)).astype(BF16)


def scan(routing, came, dt_weight, dt_bias, a_log, skip, conv, gate, fetched, hidden, base):
    own = base is None
    first = PER if own else 0
    blocks = RETURNED if own else STATE
    whole = lambda shape: pl.BlockSpec(shape, lambda i, r: (0,) * len(shape))
    ends = lambda at: pl.BlockSpec(
        (1, HEAD, INNER), lambda i, r: (r[ORDER + at + i], TURN // HEAD - 1, 0)
    )
    return pl.pallas_call(
        functools.partial(scan_kernel, own),
        grid_spec=pltpu.PrefetchScalarGridSpec(
            num_scalar_prefetch=1,
            grid=(PER,),
            in_specs=[
                pl.BlockSpec(memory_space=pl.ANY),
                whole((RANK, INNER)),
                whole((1, INNER)),
                whole((STATE, INNER)),
                whole((1, INNER)),
                pl.BlockSpec((1, TURN, INNER), lambda i, r: (first + i, 0, 0)),
                pl.BlockSpec((1, TURN, INNER), lambda i, r: (r[ORDER + first + i], 0, 0)),
                pl.BlockSpec(
                    (1, STATE, TILES, LANES),
                    lambda i, r: (r[HOLDER + first + i], r[SIDES + own], 0, 0),
                ),
                ends(PER),
                ends(0),
                pl.BlockSpec(memory_space=pl.ANY),
            ],
            out_specs=[
                pl.BlockSpec((1, TURN, INNER), lambda i, r: (r[ORDER + first + i], 0, 0)),
                whole((GROUPS, blocks, TILES, LANES)),
            ],
            scratch_shapes=[
                pltpu.VMEM((TURN * TILES, LANES), F32),
                pltpu.VMEM((TURN * TILES, LANES), F32),
                pltpu.VMEM((TURN * 2 * STATE, LANES), F32),
                pltpu.VMEM((STATE * TILES, LANES), F32),
                pltpu.VMEM((STATE * TILES, LANES), F32),
                pltpu.VMEM((DEPTH, SHARE + EDGES, WIDE), BF16),
                pltpu.SemaphoreType.DMA,
            ],
        ),
        out_shape=[
            jax.ShapeDtypeStruct((REQUESTS, TURN, INNER), BF16),
            jax.ShapeDtypeStruct((GROUPS, blocks, TILES, LANES), BF16),
        ],
        input_output_aliases={} if own else {11: 0},
        compiler_params=params(),
        cost_estimate=cost(15, 4 * 2**20),
        name="scan",
    )(routing, came, dt_weight, dt_bias, a_log, skip, conv, gate, fetched, hidden,
      hidden, skip if own else base)


def widen(came, wide, g, row):
    for part in range(STATE // 8):
        for tile in range(TILES):
            rows, cols = block_of(part, tile)
            wide[row, rows, cols] = came[g, part * TILES + tile].astype(F32)


def place_kernel(routing, came, ssm, conv, new_ssm, new_conv, inputs, sem):
    base = pltpu.make_async_copy(ssm, new_ssm, sem)
    base.start()
    for k in range(KEPT):
        rows_to_tiles(inputs, k * SLOTS * TILES, conv[k])

    def put(slot, g, first):
        for k in range(KEPT):
            row = pl.multiple_of((k * SLOTS + slot) * TILES, TILES)
            inputs[pl.ds(row, TILES), :] = came[g, first + k].astype(F32)

    def each(g, carry):
        slot = routing[OWN + g]
        other_slot = routing[OTHER + g]

        @pl.when(slot < SLOTS)
        def _():
            widen(came, new_ssm, g, slot)
            put(slot, g, STATE)

        @pl.when(other_slot < SLOTS)
        def _():
            put(other_slot, g, STATE + KEPT)

        return carry

    base.wait()
    lax.fori_loop(0, GROUPS, each, 0)
    for k in range(KEPT):
        for tile in range(TILES):
            new_conv[k, :, tile * LANES : (tile + 1) * LANES] = inputs[
                pl.ds(k * SLOTS * TILES + tile, SLOTS, stride=TILES), :
            ]


def place(routing, came, ssm, conv):
    rows = pl.BlockSpec((KEPT, SLOTS, INNER), lambda i, r: (0, 0, 0))
    return pl.pallas_call(
        place_kernel,
        grid_spec=pltpu.PrefetchScalarGridSpec(
            num_scalar_prefetch=1,
            grid=(1,),
            in_specs=[
                pl.BlockSpec((GROUPS, RETURNED, TILES, LANES), lambda i, r: (0, 0, 0, 0)),
                pl.BlockSpec(memory_space=pl.ANY),
                rows,
            ],
            out_specs=[pl.BlockSpec((SLOTS, STATE, INNER), lambda i, r: (0, 0, 0)), rows],
            scratch_shapes=[
                pltpu.VMEM((KEPT * SLOTS * TILES, LANES), F32),
                pltpu.SemaphoreType.DMA,
            ],
        ),
        out_shape=[
            jax.ShapeDtypeStruct((SLOTS, STATE, INNER), F32),
            jax.ShapeDtypeStruct((KEPT, SLOTS, INNER), F32),
        ],
        compiler_params=params(),
        cost_estimate=cost(6, 6 * 2**20),
        name="place",
    )(routing, came, ssm, conv)


def store_kernel(routing, came, ssm_in, new_ssm, states, wide, sem, sems):
    def copy(g):
        return pltpu.make_async_copy(wide.at[g], new_ssm.at[routing[OTHER + g]], sems.at[g])

    def begin(g, carry):
        @pl.when(routing[OTHER + g] < SLOTS)
        def _():
            widen(states, wide, g, g)
            copy(g).start()

        return carry

    def finish(g, carry):
        @pl.when(routing[OTHER + g] < SLOTS)
        def _():
            copy(g).wait()

        return carry

    arriving = pltpu.make_async_copy(came, states, sem)
    arriving.start()
    arriving.wait()
    lax.fori_loop(0, GROUPS, begin, 0)
    lax.fori_loop(0, GROUPS, finish, 0)


def store(routing, came, ssm):
    anywhere = pl.BlockSpec(memory_space=pl.ANY)
    return pl.pallas_call(
        store_kernel,
        grid_spec=pltpu.PrefetchScalarGridSpec(
            num_scalar_prefetch=1,
            grid=(1,),
            in_specs=[anywhere, anywhere],
            out_specs=anywhere,
            scratch_shapes=[
                pltpu.VMEM((GROUPS, STATE, TILES, LANES), BF16),
                pltpu.VMEM((GROUPS, STATE, INNER), F32),
                pltpu.SemaphoreType.DMA,
                pltpu.SemaphoreType.DMA((GROUPS,)),
            ],
        ),
        out_shape=jax.ShapeDtypeStruct((SLOTS, STATE, INNER), F32),
        input_output_aliases={2: 0},
        compiler_params=params(),
        cost_estimate=cost(2, 2 * 2**20),
        name="store",
    )(routing, came, ssm)


def exchange(values, axis):
    return lax.all_to_all(values, axis, split_axis=0, concat_axis=0, tiled=True)


def body(
    hidden_x,
    gate_z,
    conv_weight,
    conv_bias,
    x_weight,
    dt_weight,
    dt_bias,
    a_log,
    skip_gain,
    ssm_cache,
    conv_cache,
    holder_of,
    slot_of,
):
    conv_rows = jnp.swapaxes(conv_cache, 0, 1)
    bias = conv_bias.reshape(1, INNER)
    x_weight = x_weight.T
    routing, packed = pack(holder_of, slot_of, ssm_cache, conv_rows)
    fetched = exchange(packed, "dp")
    conv, sent, kept = convolve(routing, hidden_x, conv_weight, bias, x_weight)
    parts = (kept + lax.ppermute(sent, "core", SWAP).astype(F32)).astype(BF16)
    parts, fetched = lax.optimization_barrier((parts, fetched))
    parts = exchange(parts.reshape(DEPTH, SHARE, WIDE), "z")
    conv, edge_sent, edge = put_heads(
        routing, hidden_x, fetched, conv_weight, bias, x_weight, conv
    )
    normed = exchange(normalize(parts, edge, lax.ppermute(edge_sent, "core", SWAP)), "z")
    gated, came = None, []
    for values in (normed, lax.ppermute(normed, "core", SWAP)):
        gated, final = scan(
            routing,
            values,
            dt_weight,
            dt_bias.reshape(1, INNER),
            a_log,
            skip_gain.reshape(1, INNER),
            conv,
            gate_z,
            fetched,
            hidden_x,
            gated,
        )
        if came:
            came[0], final = lax.optimization_barrier((came[0], final))
        came.append(exchange(final, "dp"))
    new_ssm, new_conv = place(routing, came[0], ssm_cache, conv_rows)
    new_ssm = store(routing, came[1], new_ssm)
    return (gated, new_ssm, jnp.swapaxes(new_conv, 0, 1))


def solution(mesh):
    fine = Mesh(mesh.devices.reshape(GROUPS, DEPTH, CORES), ("dp", "z", "core"))
    tensor = ("z", "core")
    placed = (
        P("dp", None, tensor),
        P("dp", None, tensor),
        P(None, tensor),
        P(tensor),
        P(tensor, None),
        P(None, tensor),
        P(tensor),
        P(None, tensor),
        P(tensor),
        P("dp", None, tensor),
        P("dp", None, tensor),
        P(),
        P(),
    )
    return jax.shard_map(
        body,
        mesh=fine,
        in_specs=placed,
        out_specs=(P("dp", None, tensor),) * 3,
        check_vma=False,
    )
```

```python
import functools

import jax
import jax.numpy as jnp
from jax import lax
from jax.experimental import pallas as pl
from jax.experimental.pallas import tpu as pltpu
from jax.sharding import Mesh, PartitionSpec as P

EPSILON = 1e-06
NORM_FLOOR = 0.25
LOG2_E = 1.4426950408889634

GROUPS = 16
REQUESTS = 8
CHUNKS = 2
PER = REQUESTS // CHUNKS
TURN = 128
INNER = 1024
RANK = 512
STATE = 16
USED = RANK + 2 * STATE
QUARTERS = RANK // 128
SLOTS = 32
KEPT = 3
DEPTH = 8
CORES = 2
SHARE = PER * TURN // DEPTH
HEAD = 16
EDGE = 4
EDGES = PER * EDGE
PAIR = 2
SPANS = TURN // SHARE

VECTORS = SHARE * QUARTERS
GROUP = 16
SUMMED = VECTORS + GROUP
EDGED = EDGES * QUARTERS
GATHERED = SUMMED + EDGED

ORDER, HOLDER, OWN, OTHER, SIDES, ROUTING = 0, 8, 16, 32, 48, 64
FETCHED = CHUNKS * (STATE + KEPT)
RETURNED = STATE + CHUNKS * KEPT
LANES = 128
TILES = INNER // LANES
UNROLL = 16

F32 = jnp.float32
BF16 = jnp.bfloat16
SWAP = [(0, 1), (1, 0)]


def params():
    return pltpu.CompilerParams(vmem_limit_bytes=56 * 2**20)


def cost(us, bytes_accessed):
    return pl.CostEstimate(
        flops=int(us * 1.0e9), bytes_accessed=bytes_accessed, transcendentals=0
    )


def rows_to_tiles(tiles, first, rows):
    for tile in range(TILES):
        tiles[pl.ds(first + tile, rows.shape[0], stride=TILES), :] = rows[
            :, tile * LANES : (tile + 1) * LANES
        ]


def block_of(part, tile):
    return slice(part * 8, (part + 1) * 8), slice(tile * LANES, (tile + 1) * LANES)


def pack_kernel(
    holders, places, ssm, conv, routing, out, slots, ranks, states, inputs, packed, sems, out_sems
):
    me = lax.axis_index("dp")
    core = lax.axis_index("core")

    def copy(e):
        return pltpu.make_async_copy(ssm.at[slots[e]], states.at[e], sems.at[e])

    def begin(g, carry):
        held = [holders[g * REQUESTS + i] for i in range(REQUESTS)]
        rank = [jnp.int32(0)] * REQUESTS
        for i in range(REQUESTS):
            for j in range(i + 1, REQUESTS):
                below = (held[j] < held[i]).astype(jnp.int32)
                rank[i] = rank[i] + below
                rank[j] = rank[j] + (1 - below)
        found = [jnp.int32(-1)] * CHUNKS
        for i in range(REQUESTS):
            here = held[i] == me
            place = places[g * REQUESTS + i]
            for c in range(CHUNKS):
                found[c] = jnp.where(here & (rank[i] % CHUNKS == c), place, found[c])
            ranks[g * REQUESTS + i] = rank[i]
        for c in range(CHUNKS):
            slots[g * CHUNKS + c] = jnp.maximum(found[c], 0)
            copy(g * CHUNKS + c).start()
        first = jnp.where(found[0] < 0, SLOTS, found[0])
        second = jnp.where(found[1] < 0, SLOTS, found[1])
        routing[OWN + g] = jnp.where(core == 0, first, second)
        routing[OTHER + g] = jnp.where(core == 0, second, first)
        return carry

    lax.fori_loop(0, GROUPS, begin, 0)
    for i in range(REQUESTS):
        rank = ranks[me * REQUESTS + i]
        at = rank // CHUNKS + jnp.where(rank % CHUNKS == core, PER, 0)
        routing[ORDER + at] = jnp.int32(i)
        routing[HOLDER + at] = holders[me * REQUESTS + i]
    routing[SIDES] = 1 - core
    routing[SIDES + 1] = core
    for k in range(KEPT):
        rows_to_tiles(inputs, k * SLOTS * TILES, conv[k])

    def finish(g, carry):
        for c in range(CHUNKS):
            e = g * CHUNKS + c
            for k in range(KEPT):
                row = pl.multiple_of((k * SLOTS + slots[e]) * TILES, TILES)
                packed[g, CHUNKS * STATE + c * KEPT + k] = inputs[pl.ds(row, TILES), :].astype(BF16)
            copy(e).wait()
            for part in range(STATE // 8):
                for tile in range(TILES):
                    rows, cols = block_of(part, tile)
                    packed[g, c * STATE + part * TILES + tile] = states[e, rows, cols].astype(BF16)
        pltpu.make_async_copy(packed.at[g], out.at[g], out_sems.at[g]).start()
        return carry

    def end(g, carry):
        pltpu.make_async_copy(packed.at[g], out.at[g], out_sems.at[g]).wait()
        return carry

    lax.fori_loop(0, GROUPS, finish, 0)
    lax.fori_loop(0, GROUPS, end, 0)


def pack(holders, places, ssm, conv):
    anywhere = pl.BlockSpec(memory_space=pl.ANY)
    return pl.pallas_call(
        pack_kernel,
        grid_spec=pltpu.PrefetchScalarGridSpec(
            num_scalar_prefetch=2,
            grid=(1,),
            in_specs=[
                anywhere,
                pl.BlockSpec((KEPT, SLOTS, INNER), lambda i, h, p: (0, 0, 0)),
            ],
            out_specs=[pl.BlockSpec(memory_space=pltpu.SMEM), anywhere],
            scratch_shapes=[
                pltpu.SMEM((GROUPS * CHUNKS,), jnp.int32),
                pltpu.SMEM((GROUPS * REQUESTS,), jnp.int32),
                pltpu.VMEM((GROUPS * CHUNKS, STATE, INNER), F32),
                pltpu.VMEM((KEPT * SLOTS * TILES, LANES), F32),
                pltpu.VMEM((GROUPS, FETCHED, TILES, LANES), BF16),
                pltpu.SemaphoreType.DMA((GROUPS * CHUNKS,)),
                pltpu.SemaphoreType.DMA((GROUPS,)),
            ],
        ),
        out_shape=[
            jax.ShapeDtypeStruct((ROUTING,), jnp.int32),
            jax.ShapeDtypeStruct((GROUPS, FETCHED, TILES, LANES), BF16),
        ],
        compiler_params=params(),
        cost_estimate=cost(4, 4 * 2**20),
        name="pack",
    )(holders, places, ssm, conv)


def silu(v):
    half = 0.5 * v
    return half + half * jnp.tanh(half)


def project(values, x_weight):
    return lax.dot_general(
        values, x_weight[...], (((1,), (1,)), ((), ())), preferred_element_type=F32
    )


def conv_kernel(
    routing, hidden, hidden_too, weight, bias, x_weight, conv_out, sent, kept, rows
):
    step = pl.program_id(0)
    rows[:8, :] = jnp.zeros((8, INNER), F32)
    for which, source in enumerate((hidden, hidden_too)):
        for tile in range(TILES):
            cols = slice(tile * LANES, (tile + 1) * LANES)
            rows[8:, cols] = source[0, :, cols].astype(F32)
            total = jnp.zeros((TURN, LANES), F32) + bias[:, cols]
            for tap in range(KEPT + 1):
                first = 8 - KEPT + tap
                total = total + rows[first : first + TURN, cols] * weight[tap : tap + 1, cols]
            conv_out[which, :, cols] = silu(total).astype(BF16)
    part = project(conv_out[...].reshape(PAIR * TURN, INNER), x_weight)

    def put(out):
        for span in range(PAIR * SPANS):
            rows_of = part[span * SHARE : (span + 1) * SHARE]
            at = (span // SPANS, span % SPANS)
            for q in range(QUARTERS):
                out[at[0], at[1], q * SHARE : (q + 1) * SHARE] = rows_of[
                    :, q * LANES : (q + 1) * LANES
                ].astype(out.dtype)
            vectors = [rows_of[a * GROUP : (a + 1) * GROUP, RANK:] for a in range(SHARE // GROUP)]
            out[at[0], at[1], VECTORS:] = jnp.concatenate(vectors, axis=1).astype(out.dtype)

    @pl.when(step < PER // PAIR)
    def _():
        put(sent)

    @pl.when(step >= PER // PAIR)
    def _():
        put(kept)


def convolve(routing, hidden, weight, bias, x_weight):
    half = PER // PAIR
    return pl.pallas_call(
        conv_kernel,
        grid_spec=pltpu.PrefetchScalarGridSpec(
            num_scalar_prefetch=1,
            grid=(REQUESTS // PAIR,),
            in_specs=[
                pl.BlockSpec((1, TURN, INNER), lambda i, r: (r[ORDER + PAIR * i], 0, 0)),
                pl.BlockSpec((1, TURN, INNER), lambda i, r: (r[ORDER + PAIR * i + 1], 0, 0)),
                pl.BlockSpec((KEPT + 1, INNER), lambda i, r: (0, 0)),
                pl.BlockSpec((1, INNER), lambda i, r: (0, 0)),
                pl.BlockSpec((USED, INNER), lambda i, r: (0, 0)),
            ],
            out_specs=[
                pl.BlockSpec((PAIR, TURN, INNER), lambda i, r: (i, 0, 0)),
                pl.BlockSpec(
                    (PAIR, SPANS, SUMMED, LANES), lambda i, r: (jnp.minimum(i, half - 1), 0, 0, 0)
                ),
                pl.BlockSpec(
                    (PAIR, SPANS, SUMMED, LANES), lambda i, r: (jnp.maximum(i - half, 0), 0, 0, 0)
                ),
            ],
            scratch_shapes=[pltpu.VMEM((8 + TURN, INNER), F32)],
        ),
        out_shape=[
            jax.ShapeDtypeStruct((REQUESTS, TURN, INNER), BF16),
            jax.ShapeDtypeStruct((PER, SPANS, SUMMED, LANES), BF16),
            jax.ShapeDtypeStruct((PER, SPANS, SUMMED, LANES), F32),
        ],
        compiler_params=params(),
        cost_estimate=cost(8, 8 * 2**20),
        name="convolve",
    )(routing, hidden, hidden, weight, bias, x_weight)


def head_kernel(
    routing, hidden, fetched, weight, bias, x_weight, conv_in,
    conv_out, sent, kept, starts, rows, tiles, head, edges, sems, start_sems,
):
    arriving = []
    for i in range(REQUESTS):
        first = CHUNKS * STATE + routing[SIDES + i // PER] * KEPT
        arriving.append(
            pltpu.make_async_copy(
                fetched.at[routing[HOLDER + i], pl.ds(first, KEPT)], starts.at[i], start_sems.at[i]
            )
        )
        arriving[i].start()
    leaving = []
    for i in range(REQUESTS):
        arriving[i].wait()
        for k in range(KEPT):
            tiles[k * TILES : (k + 1) * TILES, :] = starts[i, k].astype(F32)
        for tile in range(TILES):
            rows[8 - KEPT : 8, tile * LANES : (tile + 1) * LANES] = tiles[
                pl.ds(tile, KEPT, stride=TILES), :
            ]
        rows[8:, :] = hidden[routing[ORDER + i]].astype(F32)
        total = jnp.zeros((HEAD, INNER), F32) + bias[...]
        for tap in range(KEPT + 1):
            first = 8 - KEPT + tap
            total = total + rows[first : first + HEAD, :] * weight[tap : tap + 1, :]
        head[i] = silu(total).astype(BF16)
        leaving.append(pltpu.make_async_copy(head.at[i], conv_out.at[i, :HEAD], sems.at[i]))
        leaving[i].start()
    part = project(head[...].reshape(REQUESTS * HEAD, INNER), x_weight)
    for i in range(REQUESTS):
        half, k = i // PER, i % PER
        for q in range(QUARTERS):
            at = q * EDGES + k * EDGE
            edges[half, at : at + EDGE] = part[
                i * HEAD : i * HEAD + EDGE, q * LANES : (q + 1) * LANES
            ]
        last = k * EDGE + KEPT
        edges[half, last : last + 1] = jnp.concatenate(
            [part[i * HEAD + j : i * HEAD + j + 1, RANK:] for j in range(KEPT)]
            + [jnp.zeros((1, LANES - KEPT * 2 * STATE), F32)],
            axis=1,
        )
    sent[...] = edges[0].astype(BF16)
    kept[...] = edges[1]
    for one in leaving:
        one.wait()


def put_heads(routing, hidden, fetched, weight, bias, x_weight, conv_out):
    anywhere = pl.BlockSpec(memory_space=pl.ANY)
    edges = pl.BlockSpec((EDGED, LANES), lambda i, r: (0, 0))
    return pl.pallas_call(
        head_kernel,
        grid_spec=pltpu.PrefetchScalarGridSpec(
            num_scalar_prefetch=1,
            grid=(1,),
            in_specs=[
                pl.BlockSpec((REQUESTS, HEAD, INNER), lambda i, r: (0, 0, 0)),
                anywhere,
                pl.BlockSpec((KEPT + 1, INNER), lambda i, r: (0, 0)),
                pl.BlockSpec((1, INNER), lambda i, r: (0, 0)),
                pl.BlockSpec((USED, INNER), lambda i, r: (0, 0)),
                anywhere,
            ],
            out_specs=[anywhere, edges, edges],
            scratch_shapes=[
                pltpu.VMEM((REQUESTS, KEPT, TILES, LANES), BF16),
                pltpu.VMEM((8 + HEAD, INNER), F32),
                pltpu.VMEM((KEPT * TILES, LANES), F32),
                pltpu.VMEM((REQUESTS, HEAD, INNER), BF16),
                pltpu.VMEM((CHUNKS, EDGED, LANES), F32),
                pltpu.SemaphoreType.DMA((REQUESTS,)),
                pltpu.SemaphoreType.DMA((REQUESTS,)),
            ],
        ),
        out_shape=[
            jax.ShapeDtypeStruct(conv_out.shape, conv_out.dtype),
            jax.ShapeDtypeStruct((EDGED, LANES), BF16),
            jax.ShapeDtypeStruct((EDGED, LANES), F32),
        ],
        input_output_aliases={6: 0},
        compiler_params=params(),
        cost_estimate=cost(4, 4 * 2**20),
        name="put_heads",
    )(routing, hidden, fetched, weight, bias, x_weight, conv_out)


def norm_rank(quarters):
    square = sum(jnp.sum(q * q, axis=1, keepdims=True) for q in quarters)
    scale = lax.rsqrt(square * (1.0 / RANK) + EPSILON)
    return [q * scale for q in quarters]


def norm_vectors(values):
    parts = []
    for first in range(0, values.shape[1], STATE):
        one = values[:, first : first + STATE]
        mean = jnp.mean(one * one, axis=1, keepdims=True)
        parts.append(one * lax.rsqrt(jnp.maximum(mean, NORM_FLOOR)))
    return jnp.concatenate(parts, axis=1)


def norm_kernel(parts, edge, edge_came, out, came, sem):
    arriving = pltpu.make_async_copy(edge_came, came, sem)
    arriving.start()
    total = parts[0].astype(F32)
    for k in range(1, DEPTH):
        total = total + parts[k].astype(F32)
    ranks = norm_rank([total[q * SHARE : (q + 1) * SHARE] for q in range(QUARTERS)])
    ranks = [q.astype(BF16) for q in ranks]
    vectors = norm_vectors(total[VECTORS:]).astype(BF16)
    arriving.wait()
    edges = (edge[...] + came[...].astype(F32)).astype(BF16)
    for k in range(DEPTH):
        for q in range(QUARTERS):
            out[k, q * SHARE : (q + 1) * SHARE] = ranks[q]
        out[k, VECTORS:SUMMED] = vectors
        out[k, SUMMED:] = edges


def normalize(parts, edge, edge_came):
    return pl.pallas_call(
        norm_kernel,
        in_specs=[
            pl.BlockSpec(memory_space=pltpu.VMEM),
            pl.BlockSpec(memory_space=pltpu.VMEM),
            pl.BlockSpec(memory_space=pl.ANY),
        ],
        scratch_shapes=[pltpu.VMEM((EDGED, LANES), BF16), pltpu.SemaphoreType.DMA],
        out_shape=jax.ShapeDtypeStruct((DEPTH, GATHERED, LANES), BF16),
        compiler_params=params(),
        cost_estimate=cost(1.5, 2**20),
        name="normalize",
    )(parts, edge, edge_came)


def scan_kernel(
    own, routing, came, dt_weight, dt_bias, a_log, skip, conv, gate, start,
    last, other_last, base, gated, final, dts, us, spread, rates, states, shares, sem,
):
    step = pl.program_id(0)
    to = routing[HOLDER + (PER if own else 0) + step]

    @pl.when(step == 0)
    def _():
        arriving = pltpu.make_async_copy(came, shares, sem)
        arriving.start()
        rows_to_tiles(rates, 0, -LOG2_E * jnp.exp(a_log[...]))
        arriving.wait()
        total = shares[0, SUMMED:].astype(F32)
        for k in range(1, DEPTH):
            total = total + shares[k, SUMMED:].astype(F32)
        quarters = [total[q * EDGES : (q + 1) * EDGES] for q in range(QUARTERS)]
        row = lax.broadcasted_iota(jnp.int32, (GROUP, LANES), 0) < KEPT
        lane = lax.broadcasted_iota(jnp.int32, (GROUP, LANES), 1) < 2 * STATE

        def patch(at, first, values, where):
            old = shares[at, first : first + GROUP].astype(F32)
            shares[at, first : first + GROUP] = jnp.where(where, values, old).astype(BF16)

        below = jnp.zeros((GROUP - EDGE, LANES), F32)
        for q, values in enumerate(norm_rank(quarters)):
            for k in range(PER):
                values_of = jnp.concatenate([values[k * EDGE : (k + 1) * EDGE], below], axis=0)
                patch(k * SPANS, q * SHARE, values_of, row)
        beside = jnp.zeros((KEPT, LANES - 2 * STATE), F32)
        below = jnp.zeros((GROUP - KEPT, LANES), F32)
        for k in range(PER):
            last = k * EDGE + KEPT
            flat = norm_vectors(quarters[0][last : last + 1, : KEPT * 2 * STATE])
            lines = [flat[:, j * 2 * STATE : (j + 1) * 2 * STATE] for j in range(KEPT)]
            values_of = jnp.concatenate([jnp.concatenate(lines, axis=0), beside], axis=1)
            values_of = jnp.concatenate([values_of, below], axis=0)
            patch(k * SPANS, VECTORS, values_of, row & lane)

    ranks = []
    for span in range(SPANS):
        at = step * SPANS + span
        ranks.append(
            jnp.concatenate(
                [shares[at, q * SHARE : (q + 1) * SHARE] for q in range(QUARTERS)], axis=1
            )
        )
        columns = shares[at, VECTORS:SUMMED].astype(F32).T
        for k in range(SHARE):
            a, t = k // GROUP, span * SHARE + k
            spread[t * 2 * STATE : (t + 1) * 2 * STATE, :] = jnp.broadcast_to(
                columns[a * 2 * STATE : (a + 1) * 2 * STATE, k % GROUP : k % GROUP + 1],
                (2 * STATE, LANES),
            )
    rank = jnp.concatenate(ranks, axis=0)
    if own:
        for which, (rows, at) in enumerate(((last, to), (other_last, routing[HOLDER + step]))):
            rows_to_tiles(states, 0, rows[0].astype(F32)[HEAD - KEPT :, :])
            for k in range(KEPT):
                final[at, STATE + which * KEPT + k] = states[
                    k * TILES : (k + 1) * TILES, :
                ].astype(BF16)
    for part in range(STATE // 8):
        for tile in range(TILES):
            states[pl.ds(part * 8 * TILES + tile, 8, stride=TILES), :] = start[
                0, part * TILES + tile
            ].astype(F32)
    pair = 2 * LANES
    for block in range(INNER // pair):
        cols = slice(block * pair, (block + 1) * pair)
        raw = jnp.dot(rank, dt_weight[:, cols], preferred_element_type=F32) + dt_bias[:, cols]
        dt = jnp.maximum(raw, 0.0) + jnp.log1p(jnp.exp(-jnp.abs(raw)))
        for k in range(2):
            tile = 2 * block + k
            dts[pl.ds(tile, TURN, stride=TILES), :] = dt[:, k * LANES : (k + 1) * LANES]
            us[pl.ds(tile, TURN, stride=TILES), :] = conv[
                0, :, tile * LANES : (tile + 1) * LANES
            ].astype(F32)
    decay = [rates[n * TILES : (n + 1) * TILES, :] for n in range(STATE)]

    def steps(i, carried):
        carried = list(carried)
        for k in range(UNROLL):
            t = i * UNROLL + k
            at = pl.multiple_of(t * TILES, TILES)
            row = pl.multiple_of(t * 2 * STATE, 2 * STATE)
            dt = dts[pl.ds(at, TILES), :]
            drive = dt * us[pl.ds(at, TILES), :]
            sums = [None] * 4
            for n in range(STATE):
                carried[n] = (
                    jnp.exp2(dt * decay[n]) * carried[n] + drive * spread[pl.ds(row + n, 1), :]
                )
                term = carried[n] * spread[pl.ds(row + STATE + n, 1), :]
                sums[n % 4] = term if sums[n % 4] is None else sums[n % 4] + term
            dts[pl.ds(at, TILES), :] = (sums[0] + sums[1]) + (sums[2] + sums[3])
        return tuple(carried)

    carried = tuple(states[n * TILES : (n + 1) * TILES, :] for n in range(STATE))
    carried = lax.fori_loop(0, TURN // UNROLL, steps, carried)
    for n in range(STATE):
        states[n * TILES : (n + 1) * TILES, :] = carried[n]
    for part in range(STATE // 8):
        for tile in range(TILES):
            final[to, part * TILES + tile] = states[
                pl.ds(part * 8 * TILES + tile, 8, stride=TILES), :
            ].astype(BF16)
    for tile in range(TILES):
        cols = slice(tile * LANES, (tile + 1) * LANES)
        z = gate[0, :, cols].astype(F32)
        y = dts[pl.ds(tile, TURN, stride=TILES), :] + skip[:, cols] * conv[0, :, cols].astype(F32)
        gated[0, :, cols] = (y * silu(z)).astype(BF16)


def scan(routing, came, dt_weight, dt_bias, a_log, skip, conv, gate, fetched, hidden, base):
    own = base is None
    first = PER if own else 0
    blocks = RETURNED if own else STATE
    whole = lambda shape: pl.BlockSpec(shape, lambda i, r: (0,) * len(shape))
    ends = lambda at: pl.BlockSpec(
        (1, HEAD, INNER), lambda i, r: (r[ORDER + at + i], TURN // HEAD - 1, 0)
    )
    return pl.pallas_call(
        functools.partial(scan_kernel, own),
        grid_spec=pltpu.PrefetchScalarGridSpec(
            num_scalar_prefetch=1,
            grid=(PER,),
            in_specs=[
                pl.BlockSpec(memory_space=pl.ANY),
                whole((RANK, INNER)),
                whole((1, INNER)),
                whole((STATE, INNER)),
                whole((1, INNER)),
                pl.BlockSpec((1, TURN, INNER), lambda i, r: (first + i, 0, 0)),
                pl.BlockSpec((1, TURN, INNER), lambda i, r: (r[ORDER + first + i], 0, 0)),
                pl.BlockSpec(
                    (1, STATE, TILES, LANES),
                    lambda i, r: (r[HOLDER + first + i], r[SIDES + own], 0, 0),
                ),
                ends(PER),
                ends(0),
                pl.BlockSpec(memory_space=pl.ANY),
            ],
            out_specs=[
                pl.BlockSpec((1, TURN, INNER), lambda i, r: (r[ORDER + first + i], 0, 0)),
                whole((GROUPS, blocks, TILES, LANES)),
            ],
            scratch_shapes=[
                pltpu.VMEM((TURN * TILES, LANES), F32),
                pltpu.VMEM((TURN * TILES, LANES), F32),
                pltpu.VMEM((TURN * 2 * STATE, LANES), F32),
                pltpu.VMEM((STATE * TILES, LANES), F32),
                pltpu.VMEM((STATE * TILES, LANES), F32),
                pltpu.VMEM((DEPTH, GATHERED, LANES), BF16),
                pltpu.SemaphoreType.DMA,
            ],
        ),
        out_shape=[
            jax.ShapeDtypeStruct((REQUESTS, TURN, INNER), BF16),
            jax.ShapeDtypeStruct((GROUPS, blocks, TILES, LANES), BF16),
        ],
        input_output_aliases={} if own else {11: 0},
        compiler_params=params(),
        cost_estimate=cost(15, 4 * 2**20),
        name="scan",
    )(routing, came, dt_weight, dt_bias, a_log, skip, conv, gate, fetched, hidden,
      hidden, skip if own else base)


def widen(came, wide, g, row):
    for part in range(STATE // 8):
        for tile in range(TILES):
            rows, cols = block_of(part, tile)
            wide[row, rows, cols] = came[g, part * TILES + tile].astype(F32)


def place_kernel(routing, came, ssm, conv, new_ssm, new_conv, inputs, sem):
    base = pltpu.make_async_copy(ssm, new_ssm, sem)
    base.start()
    for k in range(KEPT):
        rows_to_tiles(inputs, k * SLOTS * TILES, conv[k])

    def put(slot, g, first):
        for k in range(KEPT):
            row = pl.multiple_of((k * SLOTS + slot) * TILES, TILES)
            inputs[pl.ds(row, TILES), :] = came[g, first + k].astype(F32)

    def each(g, carry):
        slot = routing[OWN + g]
        other_slot = routing[OTHER + g]

        @pl.when(slot < SLOTS)
        def _():
            widen(came, new_ssm, g, slot)
            put(slot, g, STATE)

        @pl.when(other_slot < SLOTS)
        def _():
            put(other_slot, g, STATE + KEPT)

        return carry

    base.wait()
    lax.fori_loop(0, GROUPS, each, 0)
    for k in range(KEPT):
        for tile in range(TILES):
            new_conv[k, :, tile * LANES : (tile + 1) * LANES] = inputs[
                pl.ds(k * SLOTS * TILES + tile, SLOTS, stride=TILES), :
            ]


def place(routing, came, ssm, conv):
    rows = pl.BlockSpec((KEPT, SLOTS, INNER), lambda i, r: (0, 0, 0))
    return pl.pallas_call(
        place_kernel,
        grid_spec=pltpu.PrefetchScalarGridSpec(
            num_scalar_prefetch=1,
            grid=(1,),
            in_specs=[
                pl.BlockSpec((GROUPS, RETURNED, TILES, LANES), lambda i, r: (0, 0, 0, 0)),
                pl.BlockSpec(memory_space=pl.ANY),
                rows,
            ],
            out_specs=[pl.BlockSpec((SLOTS, STATE, INNER), lambda i, r: (0, 0, 0)), rows],
            scratch_shapes=[
                pltpu.VMEM((KEPT * SLOTS * TILES, LANES), F32),
                pltpu.SemaphoreType.DMA,
            ],
        ),
        out_shape=[
            jax.ShapeDtypeStruct((SLOTS, STATE, INNER), F32),
            jax.ShapeDtypeStruct((KEPT, SLOTS, INNER), F32),
        ],
        compiler_params=params(),
        cost_estimate=cost(6, 6 * 2**20),
        name="place",
    )(routing, came, ssm, conv)


def store_kernel(routing, came, ssm_in, new_ssm, states, wide, sem, sems):
    def copy(g):
        return pltpu.make_async_copy(wide.at[g], new_ssm.at[routing[OTHER + g]], sems.at[g])

    def begin(g, carry):
        @pl.when(routing[OTHER + g] < SLOTS)
        def _():
            widen(states, wide, g, g)
            copy(g).start()

        return carry

    def finish(g, carry):
        @pl.when(routing[OTHER + g] < SLOTS)
        def _():
            copy(g).wait()

        return carry

    arriving = pltpu.make_async_copy(came, states, sem)
    arriving.start()
    arriving.wait()
    lax.fori_loop(0, GROUPS, begin, 0)
    lax.fori_loop(0, GROUPS, finish, 0)


def store(routing, came, ssm):
    anywhere = pl.BlockSpec(memory_space=pl.ANY)
    return pl.pallas_call(
        store_kernel,
        grid_spec=pltpu.PrefetchScalarGridSpec(
            num_scalar_prefetch=1,
            grid=(1,),
            in_specs=[anywhere, anywhere],
            out_specs=anywhere,
            scratch_shapes=[
                pltpu.VMEM((GROUPS, STATE, TILES, LANES), BF16),
                pltpu.VMEM((GROUPS, STATE, INNER), F32),
                pltpu.SemaphoreType.DMA,
                pltpu.SemaphoreType.DMA((GROUPS,)),
            ],
        ),
        out_shape=jax.ShapeDtypeStruct((SLOTS, STATE, INNER), F32),
        input_output_aliases={2: 0},
        compiler_params=params(),
        cost_estimate=cost(2, 2 * 2**20),
        name="store",
    )(routing, came, ssm)


def exchange(values, axis):
    return lax.all_to_all(values, axis, split_axis=0, concat_axis=0, tiled=True)


def body(
    hidden_x,
    gate_z,
    conv_weight,
    conv_bias,
    x_weight,
    dt_weight,
    dt_bias,
    a_log,
    skip_gain,
    ssm_cache,
    conv_cache,
    holder_of,
    slot_of,
):
    conv_rows = jnp.swapaxes(conv_cache, 0, 1)
    bias = conv_bias.reshape(1, INNER)
    x_weight = x_weight.T
    routing, packed = pack(holder_of, slot_of, ssm_cache, conv_rows)
    fetched = exchange(packed, "dp")
    conv, sent, kept = convolve(routing, hidden_x, conv_weight, bias, x_weight)
    parts = (kept + lax.ppermute(sent, "core", SWAP).astype(F32)).astype(BF16)
    parts, fetched = lax.optimization_barrier((parts, fetched))
    parts = exchange(parts.reshape(DEPTH, SUMMED, LANES), "z")
    conv, edge_sent, edge = put_heads(
        routing, hidden_x, fetched, conv_weight, bias, x_weight, conv
    )
    normed = exchange(normalize(parts, edge, lax.ppermute(edge_sent, "core", SWAP)), "z")
    gated, came = None, []
    for values in (normed, lax.ppermute(normed, "core", SWAP)):
        gated, final = scan(
            routing,
            values,
            dt_weight,
            dt_bias.reshape(1, INNER),
            a_log,
            skip_gain.reshape(1, INNER),
            conv,
            gate_z,
            fetched,
            hidden_x,
            gated,
        )
        if came:
            came[0], final = lax.optimization_barrier((came[0], final))
        came.append(exchange(final, "dp"))
    new_ssm, new_conv = place(routing, came[0], ssm_cache, conv_rows)
    new_ssm = store(routing, came[1], new_ssm)
    return (gated, new_ssm, jnp.swapaxes(new_conv, 0, 1))


def solution(mesh):
    fine = Mesh(mesh.devices.reshape(GROUPS, DEPTH, CORES), ("dp", "z", "core"))
    tensor = ("z", "core")
    placed = (
        P("dp", None, tensor),
        P("dp", None, tensor),
        P(None, tensor),
        P(tensor),
        P(tensor, None),
        P(None, tensor),
        P(tensor),
        P(None, tensor),
        P(tensor),
        P("dp", None, tensor),
        P("dp", None, tensor),
        P(),
        P(),
    )
    return jax.shard_map(
        body,
        mesh=fine,
        in_specs=placed,
        out_specs=(P("dp", None, tensor),) * 3,
        check_vma=False,
    )
```

```python
import functools

import jax
import jax.numpy as jnp
from jax import lax
from jax.experimental import pallas as pl
from jax.experimental.pallas import tpu as pltpu
from jax.sharding import Mesh, PartitionSpec as P

EPSILON = 1e-06
NORM_FLOOR = 0.25
LOG2_E = 1.4426950408889634

GROUPS = 16
REQUESTS = 8
CHUNKS = 2
PER = REQUESTS // CHUNKS
TURN = 128
INNER = 1024
RANK = 512
STATE = 16
USED = RANK + 2 * STATE
QUARTERS = RANK // 128
SLOTS = 32
KEPT = 3
DEPTH = 8
CORES = 2
SHARE = PER * TURN // DEPTH
HEAD = 16
EDGE = 4
EDGES = PER * EDGE
PAIR = 2
SPANS = TURN // SHARE

VECTORS = SHARE * QUARTERS
GROUP = 16
SUMMED = VECTORS + GROUP
EDGED = EDGES * QUARTERS
GATHERED = SUMMED + EDGED

ORDER, HOLDER, OWN, OTHER, SIDES, ROUTING = 0, 8, 16, 32, 48, 64
FETCHED = CHUNKS * (STATE + KEPT)
RETURNED = STATE + CHUNKS * KEPT
LANES = 128
TILES = INNER // LANES
UNROLL = 16

F32 = jnp.float32
BF16 = jnp.bfloat16
SWAP = [(0, 1), (1, 0)]


def params(mib=56):
    return pltpu.CompilerParams(vmem_limit_bytes=mib * 2**20)


def cost(us, bytes_accessed):
    return pl.CostEstimate(
        flops=int(us * 1.0e9), bytes_accessed=bytes_accessed, transcendentals=0
    )


def rows_to_tiles(tiles, first, rows):
    for tile in range(TILES):
        tiles[pl.ds(first + tile, rows.shape[0], stride=TILES), :] = rows[
            :, tile * LANES : (tile + 1) * LANES
        ]


def block_of(part, tile):
    return slice(part * 8, (part + 1) * 8), slice(tile * LANES, (tile + 1) * LANES)


def pack_kernel(
    holders, places, ssm, conv, routing, out, slots, ranks, states, lines, inputs, packed, sems,
    out_sems, lines_sem,
):
    me = lax.axis_index("dp")
    core = lax.axis_index("core")
    arriving = pltpu.make_async_copy(conv, lines, lines_sem)
    arriving.start()

    def copy(e):
        return pltpu.make_async_copy(ssm.at[slots[e]], states.at[e], sems.at[e])

    def begin(g, carry):
        held = [holders[g * REQUESTS + i] for i in range(REQUESTS)]
        rank = [jnp.int32(0)] * REQUESTS
        for i in range(REQUESTS):
            for j in range(i + 1, REQUESTS):
                below = (held[j] < held[i]).astype(jnp.int32)
                rank[i] = rank[i] + below
                rank[j] = rank[j] + (1 - below)
        found = [jnp.int32(-1)] * CHUNKS
        for i in range(REQUESTS):
            here = held[i] == me
            place = places[g * REQUESTS + i]
            for c in range(CHUNKS):
                found[c] = jnp.where(here & (rank[i] % CHUNKS == c), place, found[c])
            ranks[g * REQUESTS + i] = rank[i]
        for c in range(CHUNKS):
            slots[g * CHUNKS + c] = found[c]

            @pl.when(found[c] >= 0)
            def _():
                copy(g * CHUNKS + c).start()

        first = jnp.where(found[0] < 0, SLOTS, found[0])
        second = jnp.where(found[1] < 0, SLOTS, found[1])
        routing[OWN + g] = jnp.where(core == 0, first, second)
        routing[OTHER + g] = jnp.where(core == 0, second, first)
        return carry

    lax.fori_loop(0, GROUPS, begin, 0)
    for i in range(REQUESTS):
        rank = ranks[me * REQUESTS + i]
        at = rank // CHUNKS + jnp.where(rank % CHUNKS == core, PER, 0)
        routing[ORDER + at] = jnp.int32(i)
        routing[HOLDER + at] = holders[me * REQUESTS + i]
    routing[SIDES] = 1 - core
    routing[SIDES + 1] = core
    arriving.wait()
    for k in range(KEPT):
        rows_to_tiles(inputs, k * SLOTS * TILES, lines[k])

    def fill(g, c):
        e = g * CHUNKS + c

        @pl.when(slots[e] >= 0)
        def _():
            for k in range(KEPT):
                row = pl.multiple_of((k * SLOTS + slots[e]) * TILES, TILES)
                packed[g, CHUNKS * STATE + c * KEPT + k] = inputs[pl.ds(row, TILES), :].astype(BF16)
            copy(e).wait()
            for part in range(STATE // 8):
                for tile in range(TILES):
                    rows, cols = block_of(part, tile)
                    packed[g, c * STATE + part * TILES + tile] = states[e, rows, cols].astype(BF16)

    def finish(g, carry):
        for c in range(CHUNKS):
            fill(g, c)
        pltpu.make_async_copy(packed.at[g], out.at[g], out_sems.at[g]).start()
        return carry

    def end(g, carry):
        pltpu.make_async_copy(packed.at[g], out.at[g], out_sems.at[g]).wait()
        return carry

    lax.fori_loop(0, GROUPS, finish, 0)
    lax.fori_loop(0, GROUPS, end, 0)


def pack(holders, places, ssm, conv):
    anywhere = pl.BlockSpec(memory_space=pl.ANY)
    return pl.pallas_call(
        pack_kernel,
        grid_spec=pltpu.PrefetchScalarGridSpec(
            num_scalar_prefetch=2,
            grid=(1,),
            in_specs=[anywhere, anywhere],
            out_specs=[pl.BlockSpec(memory_space=pltpu.SMEM), anywhere],
            scratch_shapes=[
                pltpu.SMEM((GROUPS * CHUNKS,), jnp.int32),
                pltpu.SMEM((GROUPS * REQUESTS,), jnp.int32),
                pltpu.VMEM((GROUPS * CHUNKS, STATE, INNER), F32),
                pltpu.VMEM((KEPT, SLOTS, INNER), F32),
                pltpu.VMEM((KEPT * SLOTS * TILES, LANES), F32),
                pltpu.VMEM((GROUPS, FETCHED, TILES, LANES), BF16),
                pltpu.SemaphoreType.DMA((GROUPS * CHUNKS,)),
                pltpu.SemaphoreType.DMA((GROUPS,)),
                pltpu.SemaphoreType.DMA,
            ],
        ),
        out_shape=[
            jax.ShapeDtypeStruct((ROUTING,), jnp.int32),
            jax.ShapeDtypeStruct((GROUPS, FETCHED, TILES, LANES), BF16),
        ],
        compiler_params=params(),
        cost_estimate=cost(4, 4 * 2**20),
        name="pack",
    )(holders, places, ssm, conv)


def silu(v):
    half = 0.5 * v
    return half + half * jnp.tanh(half)


def project(values, x_weight):
    return lax.dot_general(
        values, x_weight[...], (((1,), (1,)), ((), ())), preferred_element_type=F32
    )


def conv_kernel(
    routing, hidden, hidden_too, weight, bias, x_weight, conv_out, sent, kept, rows
):
    step = pl.program_id(0)
    rows[:8, :] = jnp.zeros((8, INNER), F32)
    for which, source in enumerate((hidden, hidden_too)):
        for tile in range(TILES):
            cols = slice(tile * LANES, (tile + 1) * LANES)
            rows[8:, cols] = source[0, :, cols].astype(F32)
            total = jnp.zeros((TURN, LANES), F32) + bias[:, cols]
            for tap in range(KEPT + 1):
                first = 8 - KEPT + tap
                total = total + rows[first : first + TURN, cols] * weight[tap : tap + 1, cols]
            conv_out[which, :, cols] = silu(total).astype(BF16)
    part = project(conv_out[...].reshape(PAIR * TURN, INNER), x_weight)

    def put(out):
        for span in range(PAIR * SPANS):
            rows_of = part[span * SHARE : (span + 1) * SHARE]
            at = (span // SPANS, span % SPANS)
            for q in range(QUARTERS):
                out[at[0], at[1], q * SHARE : (q + 1) * SHARE] = rows_of[
                    :, q * LANES : (q + 1) * LANES
                ].astype(out.dtype)
            vectors = [rows_of[a * GROUP : (a + 1) * GROUP, RANK:] for a in range(SHARE // GROUP)]
            out[at[0], at[1], VECTORS:] = jnp.concatenate(vectors, axis=1).astype(out.dtype)

    @pl.when(step < PER // PAIR)
    def _():
        put(sent)

    @pl.when(step >= PER // PAIR)
    def _():
        put(kept)


def convolve(routing, hidden, weight, bias, x_weight):
    half = PER // PAIR
    return pl.pallas_call(
        conv_kernel,
        grid_spec=pltpu.PrefetchScalarGridSpec(
            num_scalar_prefetch=1,
            grid=(REQUESTS // PAIR,),
            in_specs=[
                pl.BlockSpec((1, TURN, INNER), lambda i, r: (r[ORDER + PAIR * i], 0, 0)),
                pl.BlockSpec((1, TURN, INNER), lambda i, r: (r[ORDER + PAIR * i + 1], 0, 0)),
                pl.BlockSpec((KEPT + 1, INNER), lambda i, r: (0, 0)),
                pl.BlockSpec((1, INNER), lambda i, r: (0, 0)),
                pl.BlockSpec((USED, INNER), lambda i, r: (0, 0)),
            ],
            out_specs=[
                pl.BlockSpec((PAIR, TURN, INNER), lambda i, r: (i, 0, 0)),
                pl.BlockSpec(
                    (PAIR, SPANS, SUMMED, LANES), lambda i, r: (jnp.minimum(i, half - 1), 0, 0, 0)
                ),
                pl.BlockSpec(
                    (PAIR, SPANS, SUMMED, LANES), lambda i, r: (jnp.maximum(i - half, 0), 0, 0, 0)
                ),
            ],
            scratch_shapes=[pltpu.VMEM((8 + TURN, INNER), F32)],
        ),
        out_shape=[
            jax.ShapeDtypeStruct((REQUESTS, TURN, INNER), BF16),
            jax.ShapeDtypeStruct((PER, SPANS, SUMMED, LANES), BF16),
            jax.ShapeDtypeStruct((PER, SPANS, SUMMED, LANES), F32),
        ],
        compiler_params=params(),
        cost_estimate=cost(8, 8 * 2**20),
        name="convolve",
    )(routing, hidden, hidden, weight, bias, x_weight)


def head_kernel(
    routing, hidden, fetched, weight, bias, x_weight, conv_in,
    conv_out, sent, kept, starts, rows, tiles, head, edges, sems, start_sems,
):
    arriving = []
    for i in range(REQUESTS):
        first = CHUNKS * STATE + routing[SIDES + i // PER] * KEPT
        arriving.append(
            pltpu.make_async_copy(
                fetched.at[routing[HOLDER + i], pl.ds(first, KEPT)], starts.at[i], start_sems.at[i]
            )
        )
        arriving[i].start()
    leaving = []
    for i in range(REQUESTS):
        arriving[i].wait()
        for k in range(KEPT):
            tiles[k * TILES : (k + 1) * TILES, :] = starts[i, k].astype(F32)
        for tile in range(TILES):
            rows[8 - KEPT : 8, tile * LANES : (tile + 1) * LANES] = tiles[
                pl.ds(tile, KEPT, stride=TILES), :
            ]
        rows[8:, :] = hidden[routing[ORDER + i]].astype(F32)
        total = jnp.zeros((HEAD, INNER), F32) + bias[...]
        for tap in range(KEPT + 1):
            first = 8 - KEPT + tap
            total = total + rows[first : first + HEAD, :] * weight[tap : tap + 1, :]
        head[i] = silu(total).astype(BF16)
        leaving.append(pltpu.make_async_copy(head.at[i], conv_out.at[i, :HEAD], sems.at[i]))
        leaving[i].start()
    part = project(head[...].reshape(REQUESTS * HEAD, INNER), x_weight)
    for i in range(REQUESTS):
        half, k = i // PER, i % PER
        for q in range(QUARTERS):
            at = q * EDGES + k * EDGE
            edges[half, at : at + EDGE] = part[
                i * HEAD : i * HEAD + EDGE, q * LANES : (q + 1) * LANES
            ]
        last = k * EDGE + KEPT
        edges[half, last : last + 1] = jnp.concatenate(
            [part[i * HEAD + j : i * HEAD + j + 1, RANK:] for j in range(KEPT)]
            + [jnp.zeros((1, LANES - KEPT * 2 * STATE), F32)],
            axis=1,
        )
    sent[...] = edges[0].astype(BF16)
    kept[...] = edges[1]
    for one in leaving:
        one.wait()


def put_heads(routing, hidden, fetched, weight, bias, x_weight, conv_out):
    anywhere = pl.BlockSpec(memory_space=pl.ANY)
    edges = pl.BlockSpec((EDGED, LANES), lambda i, r: (0, 0))
    return pl.pallas_call(
        head_kernel,
        grid_spec=pltpu.PrefetchScalarGridSpec(
            num_scalar_prefetch=1,
            grid=(1,),
            in_specs=[
                pl.BlockSpec((REQUESTS, HEAD, INNER), lambda i, r: (0, 0, 0)),
                anywhere,
                pl.BlockSpec((KEPT + 1, INNER), lambda i, r: (0, 0)),
                pl.BlockSpec((1, INNER), lambda i, r: (0, 0)),
                pl.BlockSpec((USED, INNER), lambda i, r: (0, 0)),
                anywhere,
            ],
            out_specs=[anywhere, edges, edges],
            scratch_shapes=[
                pltpu.VMEM((REQUESTS, KEPT, TILES, LANES), BF16),
                pltpu.VMEM((8 + HEAD, INNER), F32),
                pltpu.VMEM((KEPT * TILES, LANES), F32),
                pltpu.VMEM((REQUESTS, HEAD, INNER), BF16),
                pltpu.VMEM((CHUNKS, EDGED, LANES), F32),
                pltpu.SemaphoreType.DMA((REQUESTS,)),
                pltpu.SemaphoreType.DMA((REQUESTS,)),
            ],
        ),
        out_shape=[
            jax.ShapeDtypeStruct(conv_out.shape, conv_out.dtype),
            jax.ShapeDtypeStruct((EDGED, LANES), BF16),
            jax.ShapeDtypeStruct((EDGED, LANES), F32),
        ],
        input_output_aliases={6: 0},
        compiler_params=params(),
        cost_estimate=cost(4, 4 * 2**20),
        name="put_heads",
    )(routing, hidden, fetched, weight, bias, x_weight, conv_out)


def norm_rank(quarters):
    square = sum(jnp.sum(q * q, axis=1, keepdims=True) for q in quarters)
    scale = lax.rsqrt(square * (1.0 / RANK) + EPSILON)
    return [q * scale for q in quarters]


def norm_vectors(values):
    parts = []
    for first in range(0, values.shape[1], STATE):
        one = values[:, first : first + STATE]
        mean = jnp.mean(one * one, axis=1, keepdims=True)
        parts.append(one * lax.rsqrt(jnp.maximum(mean, NORM_FLOOR)))
    return jnp.concatenate(parts, axis=1)


def norm_kernel(parts, edge, edge_came, out, came, sem):
    arriving = pltpu.make_async_copy(edge_came, came, sem)
    arriving.start()
    total = parts[0].astype(F32)
    for k in range(1, DEPTH):
        total = total + parts[k].astype(F32)
    ranks = norm_rank([total[q * SHARE : (q + 1) * SHARE] for q in range(QUARTERS)])
    ranks = [q.astype(BF16) for q in ranks]
    vectors = norm_vectors(total[VECTORS:]).astype(BF16)
    arriving.wait()
    edges = (edge[...] + came[...].astype(F32)).astype(BF16)
    for k in range(DEPTH):
        for q in range(QUARTERS):
            out[k, q * SHARE : (q + 1) * SHARE] = ranks[q]
        out[k, VECTORS:SUMMED] = vectors
        out[k, SUMMED:] = edges


def normalize(parts, edge, edge_came):
    return pl.pallas_call(
        norm_kernel,
        in_specs=[
            pl.BlockSpec(memory_space=pltpu.VMEM),
            pl.BlockSpec(memory_space=pltpu.VMEM),
            pl.BlockSpec(memory_space=pl.ANY),
        ],
        scratch_shapes=[pltpu.VMEM((EDGED, LANES), BF16), pltpu.SemaphoreType.DMA],
        out_shape=jax.ShapeDtypeStruct((DEPTH, GATHERED, LANES), BF16),
        compiler_params=params(12),
        cost_estimate=cost(1.5, 2**20),
        name="normalize",
    )(parts, edge, edge_came)


def scan_kernel(
    own, routing, came, dt_weight, dt_bias, a_log, skip, conv, gate, start,
    last, other_last, base, gated, final, dts, us, spread, rates, states, shares, sem,
):
    step = pl.program_id(0)
    to = routing[HOLDER + (PER if own else 0) + step]

    @pl.when(step == 0)
    def _():
        arriving = pltpu.make_async_copy(came, shares, sem)
        arriving.start()
        rows_to_tiles(rates, 0, -LOG2_E * jnp.exp(a_log[...]))
        arriving.wait()
        total = shares[0, SUMMED:].astype(F32)
        for k in range(1, DEPTH):
            total = total + shares[k, SUMMED:].astype(F32)
        quarters = [total[q * EDGES : (q + 1) * EDGES] for q in range(QUARTERS)]
        row = lax.broadcasted_iota(jnp.int32, (GROUP, LANES), 0) < KEPT
        lane = lax.broadcasted_iota(jnp.int32, (GROUP, LANES), 1) < 2 * STATE

        def patch(at, first, values, where):
            old = shares[at, first : first + GROUP].astype(F32)
            shares[at, first : first + GROUP] = jnp.where(where, values, old).astype(BF16)

        below = jnp.zeros((GROUP - EDGE, LANES), F32)
        for q, values in enumerate(norm_rank(quarters)):
            for k in range(PER):
                values_of = jnp.concatenate([values[k * EDGE : (k + 1) * EDGE], below], axis=0)
                patch(k * SPANS, q * SHARE, values_of, row)
        beside = jnp.zeros((KEPT, LANES - 2 * STATE), F32)
        below = jnp.zeros((GROUP - KEPT, LANES), F32)
        for k in range(PER):
            last = k * EDGE + KEPT
            flat = norm_vectors(quarters[0][last : last + 1, : KEPT * 2 * STATE])
            lines = [flat[:, j * 2 * STATE : (j + 1) * 2 * STATE] for j in range(KEPT)]
            values_of = jnp.concatenate([jnp.concatenate(lines, axis=0), beside], axis=1)
            values_of = jnp.concatenate([values_of, below], axis=0)
            patch(k * SPANS, VECTORS, values_of, row & lane)

    ranks = []
    for span in range(SPANS):
        at = step * SPANS + span
        ranks.append(
            jnp.concatenate(
                [shares[at, q * SHARE : (q + 1) * SHARE] for q in range(QUARTERS)], axis=1
            )
        )
        columns = shares[at, VECTORS:SUMMED].astype(F32).T
        for k in range(SHARE):
            a, t = k // GROUP, span * SHARE + k
            spread[t * 2 * STATE : (t + 1) * 2 * STATE, :] = jnp.broadcast_to(
                columns[a * 2 * STATE : (a + 1) * 2 * STATE, k % GROUP : k % GROUP + 1],
                (2 * STATE, LANES),
            )
    rank = jnp.concatenate(ranks, axis=0)
    if own:
        for which, (rows, at) in enumerate(((last, to), (other_last, routing[HOLDER + step]))):
            rows_to_tiles(states, 0, rows[0].astype(F32)[HEAD - KEPT :, :])
            for k in range(KEPT):
                final[at, STATE + which * KEPT + k] = states[
                    k * TILES : (k + 1) * TILES, :
                ].astype(BF16)
    for part in range(STATE // 8):
        for tile in range(TILES):
            states[pl.ds(part * 8 * TILES + tile, 8, stride=TILES), :] = start[
                0, part * TILES + tile
            ].astype(F32)
    pair = 2 * LANES
    for block in range(INNER // pair):
        cols = slice(block * pair, (block + 1) * pair)
        raw = jnp.dot(rank, dt_weight[:, cols], preferred_element_type=F32) + dt_bias[:, cols]
        dt = jnp.maximum(raw, 0.0) + jnp.log1p(jnp.exp(-jnp.abs(raw)))
        for k in range(2):
            tile = 2 * block + k
            dts[pl.ds(tile, TURN, stride=TILES), :] = dt[:, k * LANES : (k + 1) * LANES]
            us[pl.ds(tile, TURN, stride=TILES), :] = conv[
                0, :, tile * LANES : (tile + 1) * LANES
            ].astype(F32)
    decay = [rates[n * TILES : (n + 1) * TILES, :] for n in range(STATE)]

    def steps(i, carried):
        carried = list(carried)
        for k in range(UNROLL):
            t = i * UNROLL + k
            at = pl.multiple_of(t * TILES, TILES)
            row = pl.multiple_of(t * 2 * STATE, 2 * STATE)
            dt = dts[pl.ds(at, TILES), :]
            drive = dt * us[pl.ds(at, TILES), :]
            sums = [None] * 4
            for n in range(STATE):
                carried[n] = (
                    jnp.exp2(dt * decay[n]) * carried[n] + drive * spread[pl.ds(row + n, 1), :]
                )
                term = carried[n] * spread[pl.ds(row + STATE + n, 1), :]
                sums[n % 4] = term if sums[n % 4] is None else sums[n % 4] + term
            dts[pl.ds(at, TILES), :] = (sums[0] + sums[1]) + (sums[2] + sums[3])
        return tuple(carried)

    carried = tuple(states[n * TILES : (n + 1) * TILES, :] for n in range(STATE))
    carried = lax.fori_loop(0, TURN // UNROLL, steps, carried)
    for n in range(STATE):
        states[n * TILES : (n + 1) * TILES, :] = carried[n]
    for part in range(STATE // 8):
        for tile in range(TILES):
            final[to, part * TILES + tile] = states[
                pl.ds(part * 8 * TILES + tile, 8, stride=TILES), :
            ].astype(BF16)
    for tile in range(TILES):
        cols = slice(tile * LANES, (tile + 1) * LANES)
        z = gate[0, :, cols].astype(F32)
        y = dts[pl.ds(tile, TURN, stride=TILES), :] + skip[:, cols] * conv[0, :, cols].astype(F32)
        gated[0, :, cols] = (y * silu(z)).astype(BF16)


def scan(routing, came, dt_weight, dt_bias, a_log, skip, conv, gate, fetched, hidden, base):
    own = base is None
    first = PER if own else 0
    blocks = RETURNED if own else STATE
    whole = lambda shape: pl.BlockSpec(shape, lambda i, r: (0,) * len(shape))
    ends = lambda at: pl.BlockSpec(
        (1, HEAD, INNER), lambda i, r: (r[ORDER + at + i], TURN // HEAD - 1, 0)
    )
    return pl.pallas_call(
        functools.partial(scan_kernel, own),
        grid_spec=pltpu.PrefetchScalarGridSpec(
            num_scalar_prefetch=1,
            grid=(PER,),
            in_specs=[
                pl.BlockSpec(memory_space=pl.ANY),
                whole((RANK, INNER)),
                whole((1, INNER)),
                whole((STATE, INNER)),
                whole((1, INNER)),
                pl.BlockSpec((1, TURN, INNER), lambda i, r: (first + i, 0, 0)),
                pl.BlockSpec((1, TURN, INNER), lambda i, r: (r[ORDER + first + i], 0, 0)),
                pl.BlockSpec(
                    (1, STATE, TILES, LANES),
                    lambda i, r: (r[HOLDER + first + i], r[SIDES + own], 0, 0),
                ),
                ends(PER),
                ends(0),
                pl.BlockSpec(memory_space=pl.ANY),
            ],
            out_specs=[
                pl.BlockSpec((1, TURN, INNER), lambda i, r: (r[ORDER + first + i], 0, 0)),
                whole((GROUPS, blocks, TILES, LANES)),
            ],
            scratch_shapes=[
                pltpu.VMEM((TURN * TILES, LANES), F32),
                pltpu.VMEM((TURN * TILES, LANES), F32),
                pltpu.VMEM((TURN * 2 * STATE, LANES), F32),
                pltpu.VMEM((STATE * TILES, LANES), F32),
                pltpu.VMEM((STATE * TILES, LANES), F32),
                pltpu.VMEM((DEPTH, GATHERED, LANES), BF16),
                pltpu.SemaphoreType.DMA,
            ],
        ),
        out_shape=[
            jax.ShapeDtypeStruct((REQUESTS, TURN, INNER), BF16),
            jax.ShapeDtypeStruct((GROUPS, blocks, TILES, LANES), BF16),
        ],
        input_output_aliases={} if own else {11: 0},
        compiler_params=params(20 if own else 56),
        cost_estimate=cost(15, 4 * 2**20),
        name="scan",
    )(routing, came, dt_weight, dt_bias, a_log, skip, conv, gate, fetched, hidden,
      hidden, skip if own else base)


def widen(came, wide, g, row):
    for part in range(STATE // 8):
        for tile in range(TILES):
            rows, cols = block_of(part, tile)
            wide[row, rows, cols] = came[g, part * TILES + tile].astype(F32)


def place_kernel(routing, came, ssm, conv, new_ssm, new_conv, inputs, sem):
    base = pltpu.make_async_copy(ssm, new_ssm, sem)
    base.start()
    for k in range(KEPT):
        rows_to_tiles(inputs, k * SLOTS * TILES, conv[k])

    def put(slot, g, first):
        for k in range(KEPT):
            row = pl.multiple_of((k * SLOTS + slot) * TILES, TILES)
            inputs[pl.ds(row, TILES), :] = came[g, first + k].astype(F32)

    def each(g, carry):
        slot = routing[OWN + g]
        other_slot = routing[OTHER + g]

        @pl.when(slot < SLOTS)
        def _():
            widen(came, new_ssm, g, slot)
            put(slot, g, STATE)

        @pl.when(other_slot < SLOTS)
        def _():
            put(other_slot, g, STATE + KEPT)

        return carry

    base.wait()
    lax.fori_loop(0, GROUPS, each, 0)
    for k in range(KEPT):
        for tile in range(TILES):
            new_conv[k, :, tile * LANES : (tile + 1) * LANES] = inputs[
                pl.ds(k * SLOTS * TILES + tile, SLOTS, stride=TILES), :
            ]


def place(routing, came, ssm, conv):
    rows = pl.BlockSpec((KEPT, SLOTS, INNER), lambda i, r: (0, 0, 0))
    return pl.pallas_call(
        place_kernel,
        grid_spec=pltpu.PrefetchScalarGridSpec(
            num_scalar_prefetch=1,
            grid=(1,),
            in_specs=[
                pl.BlockSpec((GROUPS, RETURNED, TILES, LANES), lambda i, r: (0, 0, 0, 0)),
                pl.BlockSpec(memory_space=pl.ANY),
                rows,
            ],
            out_specs=[pl.BlockSpec((SLOTS, STATE, INNER), lambda i, r: (0, 0, 0)), rows],
            scratch_shapes=[
                pltpu.VMEM((KEPT * SLOTS * TILES, LANES), F32),
                pltpu.SemaphoreType.DMA,
            ],
        ),
        out_shape=[
            jax.ShapeDtypeStruct((SLOTS, STATE, INNER), F32),
            jax.ShapeDtypeStruct((KEPT, SLOTS, INNER), F32),
        ],
        compiler_params=params(20),
        cost_estimate=cost(6, 6 * 2**20),
        name="place",
    )(routing, came, ssm, conv)


def store_kernel(routing, came, ssm_in, new_ssm, states, wide, sem, sems):
    def copy(g):
        return pltpu.make_async_copy(wide.at[g], new_ssm.at[routing[OTHER + g]], sems.at[g])

    def begin(g, carry):
        @pl.when(routing[OTHER + g] < SLOTS)
        def _():
            widen(states, wide, g, g)
            copy(g).start()

        return carry

    def finish(g, carry):
        @pl.when(routing[OTHER + g] < SLOTS)
        def _():
            copy(g).wait()

        return carry

    arriving = pltpu.make_async_copy(came, states, sem)
    arriving.start()
    arriving.wait()
    lax.fori_loop(0, GROUPS, begin, 0)
    lax.fori_loop(0, GROUPS, finish, 0)


def store(routing, came, ssm):
    anywhere = pl.BlockSpec(memory_space=pl.ANY)
    return pl.pallas_call(
        store_kernel,
        grid_spec=pltpu.PrefetchScalarGridSpec(
            num_scalar_prefetch=1,
            grid=(1,),
            in_specs=[anywhere, anywhere],
            out_specs=anywhere,
            scratch_shapes=[
                pltpu.VMEM((GROUPS, STATE, TILES, LANES), BF16),
                pltpu.VMEM((GROUPS, STATE, INNER), F32),
                pltpu.SemaphoreType.DMA,
                pltpu.SemaphoreType.DMA((GROUPS,)),
            ],
        ),
        out_shape=jax.ShapeDtypeStruct((SLOTS, STATE, INNER), F32),
        input_output_aliases={2: 0},
        compiler_params=params(8),
        cost_estimate=cost(2, 2 * 2**20),
        name="store",
    )(routing, came, ssm)


def exchange(values, axis):
    return lax.all_to_all(values, axis, split_axis=0, concat_axis=0, tiled=True)


def body(
    hidden_x,
    gate_z,
    conv_weight,
    conv_bias,
    x_weight,
    dt_weight,
    dt_bias,
    a_log,
    skip_gain,
    ssm_cache,
    conv_cache,
    holder_of,
    slot_of,
):
    conv_rows = jnp.swapaxes(conv_cache, 0, 1)
    bias = conv_bias.reshape(1, INNER)
    x_weight = x_weight.T
    routing, packed = pack(holder_of, slot_of, ssm_cache, conv_rows)
    fetched = exchange(packed, "dp")
    conv, sent, kept = convolve(routing, hidden_x, conv_weight, bias, x_weight)
    parts = (kept + lax.ppermute(sent, "core", SWAP).astype(F32)).astype(BF16)
    parts, fetched = lax.optimization_barrier((parts, fetched))
    parts = exchange(parts.reshape(DEPTH, SUMMED, LANES), "z")
    conv, edge_sent, edge = put_heads(
        routing, hidden_x, fetched, conv_weight, bias, x_weight, conv
    )
    normed = exchange(normalize(parts, edge, lax.ppermute(edge_sent, "core", SWAP)), "z")
    gated, came = None, []
    for values in (normed, lax.ppermute(normed, "core", SWAP)):
        gated, final = scan(
            routing,
            values,
            dt_weight,
            dt_bias.reshape(1, INNER),
            a_log,
            skip_gain.reshape(1, INNER),
            conv,
            gate_z,
            fetched,
            hidden_x,
            gated,
        )
        if came:
            came[0], final = lax.optimization_barrier((came[0], final))
        came.append(exchange(final, "dp"))
    new_ssm, new_conv = place(routing, came[0], ssm_cache, conv_rows)
    new_ssm = store(routing, came[1], new_ssm)
    return (gated, new_ssm, jnp.swapaxes(new_conv, 0, 1))


def solution(mesh):
    fine = Mesh(mesh.devices.reshape(GROUPS, DEPTH, CORES), ("dp", "z", "core"))
    tensor = ("z", "core")
    placed = (
        P("dp", None, tensor),
        P("dp", None, tensor),
        P(None, tensor),
        P(tensor),
        P(tensor, None),
        P(None, tensor),
        P(tensor),
        P(None, tensor),
        P(tensor),
        P("dp", None, tensor),
        P("dp", None, tensor),
        P(),
        P(),
    )
    return jax.shard_map(
        body,
        mesh=fine,
        in_specs=placed,
        out_specs=(P("dp", None, tensor),) * 3,
        check_vma=False,
    )
```

```python
import functools

import jax
import jax.numpy as jnp
from jax import lax
from jax.experimental import pallas as pl
from jax.experimental.pallas import tpu as pltpu
from jax.sharding import Mesh, PartitionSpec as P

EPSILON = 1e-06
NORM_FLOOR = 0.25
LOG2_E = 1.4426950408889634

GROUPS = 16
REQUESTS = 8
CHUNKS = 2
PER = REQUESTS // CHUNKS
TURN = 128
INNER = 1024
RANK = 512
STATE = 16
USED = RANK + 2 * STATE
QUARTERS = RANK // 128
SLOTS = 32
KEPT = 3
DEPTH = 8
CORES = 2
SHARE = PER * TURN // DEPTH
HEAD = 16
EDGE = 4
EDGES = PER * EDGE
PAIR = 2
SPANS = TURN // SHARE

VECTORS = SHARE * QUARTERS
GROUP = 16
SUMMED = VECTORS + GROUP
EDGED = EDGES * QUARTERS
GATHERED = SUMMED + EDGED

ORDER, HOLDER, OWN, OTHER, SIDES, ROUTING = 0, 8, 16, 32, 48, 64
FETCHED = CHUNKS * (STATE + KEPT)
RETURNED = STATE + CHUNKS * KEPT
LANES = 128
TILES = INNER // LANES
UNROLL = 32

F32 = jnp.float32
BF16 = jnp.bfloat16
SWAP = [(0, 1), (1, 0)]


def params(mib=56):
    return pltpu.CompilerParams(vmem_limit_bytes=mib * 2**20)


def cost(us, bytes_accessed):
    return pl.CostEstimate(
        flops=int(us * 1.0e9), bytes_accessed=bytes_accessed, transcendentals=0
    )


def rows_to_tiles(tiles, first, rows):
    for tile in range(TILES):
        tiles[pl.ds(first + tile, rows.shape[0], stride=TILES), :] = rows[
            :, tile * LANES : (tile + 1) * LANES
        ]


def block_of(part, tile):
    return slice(part * 8, (part + 1) * 8), slice(tile * LANES, (tile + 1) * LANES)


def pack_kernel(
    holders, places, ssm, conv, routing, out, slots, ranks, states, lines, inputs, packed, sems,
    out_sems, lines_sem,
):
    me = lax.axis_index("dp")
    core = lax.axis_index("core")
    arriving = pltpu.make_async_copy(conv, lines, lines_sem)
    arriving.start()

    def copy(e):
        return pltpu.make_async_copy(ssm.at[slots[e]], states.at[e], sems.at[e])

    def begin(g, carry):
        held = [holders[g * REQUESTS + i] for i in range(REQUESTS)]
        rank = [jnp.int32(0)] * REQUESTS
        for i in range(REQUESTS):
            for j in range(i + 1, REQUESTS):
                below = (held[j] < held[i]).astype(jnp.int32)
                rank[i] = rank[i] + below
                rank[j] = rank[j] + (1 - below)
        found = [jnp.int32(-1)] * CHUNKS
        for i in range(REQUESTS):
            here = held[i] == me
            place = places[g * REQUESTS + i]
            for c in range(CHUNKS):
                found[c] = jnp.where(here & (rank[i] % CHUNKS == c), place, found[c])
            ranks[g * REQUESTS + i] = rank[i]
        for c in range(CHUNKS):
            slots[g * CHUNKS + c] = found[c]

            @pl.when(found[c] >= 0)
            def _():
                copy(g * CHUNKS + c).start()

        first = jnp.where(found[0] < 0, SLOTS, found[0])
        second = jnp.where(found[1] < 0, SLOTS, found[1])
        routing[OWN + g] = jnp.where(core == 0, first, second)
        routing[OTHER + g] = jnp.where(core == 0, second, first)
        return carry

    lax.fori_loop(0, GROUPS, begin, 0)
    for i in range(REQUESTS):
        rank = ranks[me * REQUESTS + i]
        at = rank // CHUNKS + jnp.where(rank % CHUNKS == core, PER, 0)
        routing[ORDER + at] = jnp.int32(i)
        routing[HOLDER + at] = holders[me * REQUESTS + i]
    routing[SIDES] = 1 - core
    routing[SIDES + 1] = core
    arriving.wait()
    for k in range(KEPT):
        rows_to_tiles(inputs, k * SLOTS * TILES, lines[k])

    def fill(g, c):
        e = g * CHUNKS + c

        @pl.when(slots[e] >= 0)
        def _():
            for k in range(KEPT):
                row = pl.multiple_of((k * SLOTS + slots[e]) * TILES, TILES)
                packed[g, CHUNKS * STATE + c * KEPT + k] = inputs[pl.ds(row, TILES), :].astype(BF16)
            copy(e).wait()
            for part in range(STATE // 8):
                for tile in range(TILES):
                    rows, cols = block_of(part, tile)
                    packed[g, c * STATE + part * TILES + tile] = states[e, rows, cols].astype(BF16)

    def finish(g, carry):
        for c in range(CHUNKS):
            fill(g, c)
        pltpu.make_async_copy(packed.at[g], out.at[g], out_sems.at[g]).start()
        return carry

    def end(g, carry):
        pltpu.make_async_copy(packed.at[g], out.at[g], out_sems.at[g]).wait()
        return carry

    lax.fori_loop(0, GROUPS, finish, 0)
    lax.fori_loop(0, GROUPS, end, 0)


def pack(holders, places, ssm, conv):
    anywhere = pl.BlockSpec(memory_space=pl.ANY)
    return pl.pallas_call(
        pack_kernel,
        grid_spec=pltpu.PrefetchScalarGridSpec(
            num_scalar_prefetch=2,
            grid=(1,),
            in_specs=[anywhere, anywhere],
            out_specs=[pl.BlockSpec(memory_space=pltpu.SMEM), anywhere],
            scratch_shapes=[
                pltpu.SMEM((GROUPS * CHUNKS,), jnp.int32),
                pltpu.SMEM((GROUPS * REQUESTS,), jnp.int32),
                pltpu.VMEM((GROUPS * CHUNKS, STATE, INNER), F32),
                pltpu.VMEM((KEPT, SLOTS, INNER), F32),
                pltpu.VMEM((KEPT * SLOTS * TILES, LANES), F32),
                pltpu.VMEM((GROUPS, FETCHED, TILES, LANES), BF16),
                pltpu.SemaphoreType.DMA((GROUPS * CHUNKS,)),
                pltpu.SemaphoreType.DMA((GROUPS,)),
                pltpu.SemaphoreType.DMA,
            ],
        ),
        out_shape=[
            jax.ShapeDtypeStruct((ROUTING,), jnp.int32),
            jax.ShapeDtypeStruct((GROUPS, FETCHED, TILES, LANES), BF16),
        ],
        compiler_params=params(),
        cost_estimate=cost(4, 4 * 2**20),
        name="pack",
    )(holders, places, ssm, conv)


def silu(v):
    half = 0.5 * v
    return half + half * jnp.tanh(half)


def project(values, x_weight):
    return lax.dot_general(
        values, x_weight[...], (((1,), (1,)), ((), ())), preferred_element_type=F32
    )


def conv_kernel(
    routing, hidden, hidden_too, weight, bias, x_weight, conv_out, sent, kept, rows
):
    step = pl.program_id(0)
    rows[:8, :] = jnp.zeros((8, INNER), F32)
    for which, source in enumerate((hidden, hidden_too)):
        for tile in range(TILES):
            cols = slice(tile * LANES, (tile + 1) * LANES)
            rows[8:, cols] = source[0, :, cols].astype(F32)
            total = jnp.zeros((TURN, LANES), F32) + bias[:, cols]
            for tap in range(KEPT + 1):
                first = 8 - KEPT + tap
                total = total + rows[first : first + TURN, cols] * weight[tap : tap + 1, cols]
            conv_out[which, :, cols] = silu(total).astype(BF16)
    part = project(conv_out[...].reshape(PAIR * TURN, INNER), x_weight)

    def put(out):
        for span in range(PAIR * SPANS):
            rows_of = part[span * SHARE : (span + 1) * SHARE]
            at = (span // SPANS, span % SPANS)
            for q in range(QUARTERS):
                out[at[0], at[1], q * SHARE : (q + 1) * SHARE] = rows_of[
                    :, q * LANES : (q + 1) * LANES
                ].astype(out.dtype)
            vectors = [rows_of[a * GROUP : (a + 1) * GROUP, RANK:] for a in range(SHARE // GROUP)]
            out[at[0], at[1], VECTORS:] = jnp.concatenate(vectors, axis=1).astype(out.dtype)

    @pl.when(step < PER // PAIR)
    def _():
        put(sent)

    @pl.when(step >= PER // PAIR)
    def _():
        put(kept)


def convolve(routing, hidden, weight, bias, x_weight):
    half = PER // PAIR
    return pl.pallas_call(
        conv_kernel,
        grid_spec=pltpu.PrefetchScalarGridSpec(
            num_scalar_prefetch=1,
            grid=(REQUESTS // PAIR,),
            in_specs=[
                pl.BlockSpec((1, TURN, INNER), lambda i, r: (r[ORDER + PAIR * i], 0, 0)),
                pl.BlockSpec((1, TURN, INNER), lambda i, r: (r[ORDER + PAIR * i + 1], 0, 0)),
                pl.BlockSpec((KEPT + 1, INNER), lambda i, r: (0, 0)),
                pl.BlockSpec((1, INNER), lambda i, r: (0, 0)),
                pl.BlockSpec((USED, INNER), lambda i, r: (0, 0)),
            ],
            out_specs=[
                pl.BlockSpec((PAIR, TURN, INNER), lambda i, r: (i, 0, 0)),
                pl.BlockSpec(
                    (PAIR, SPANS, SUMMED, LANES), lambda i, r: (jnp.minimum(i, half - 1), 0, 0, 0)
                ),
                pl.BlockSpec(
                    (PAIR, SPANS, SUMMED, LANES), lambda i, r: (jnp.maximum(i - half, 0), 0, 0, 0)
                ),
            ],
            scratch_shapes=[pltpu.VMEM((8 + TURN, INNER), F32)],
        ),
        out_shape=[
            jax.ShapeDtypeStruct((REQUESTS, TURN, INNER), BF16),
            jax.ShapeDtypeStruct((PER, SPANS, SUMMED, LANES), BF16),
            jax.ShapeDtypeStruct((PER, SPANS, SUMMED, LANES), F32),
        ],
        compiler_params=params(24),
        cost_estimate=cost(8, 8 * 2**20),
        name="convolve",
    )(routing, hidden, hidden, weight, bias, x_weight)


def head_kernel(
    routing, hidden, fetched, weight, bias, x_weight, conv_in,
    conv_out, sent, kept, starts, rows, tiles, head, edges, sems, start_sems,
):
    arriving = []
    for i in range(REQUESTS):
        first = CHUNKS * STATE + routing[SIDES + i // PER] * KEPT
        arriving.append(
            pltpu.make_async_copy(
                fetched.at[routing[HOLDER + i], pl.ds(first, KEPT)], starts.at[i], start_sems.at[i]
            )
        )
        arriving[i].start()
    leaving = []
    for i in range(REQUESTS):
        arriving[i].wait()
        for k in range(KEPT):
            tiles[k * TILES : (k + 1) * TILES, :] = starts[i, k].astype(F32)
        for tile in range(TILES):
            rows[8 - KEPT : 8, tile * LANES : (tile + 1) * LANES] = tiles[
                pl.ds(tile, KEPT, stride=TILES), :
            ]
        rows[8:, :] = hidden[routing[ORDER + i]].astype(F32)
        total = jnp.zeros((HEAD, INNER), F32) + bias[...]
        for tap in range(KEPT + 1):
            first = 8 - KEPT + tap
            total = total + rows[first : first + HEAD, :] * weight[tap : tap + 1, :]
        head[i] = silu(total).astype(BF16)
        leaving.append(pltpu.make_async_copy(head.at[i], conv_out.at[i, :HEAD], sems.at[i]))
        leaving[i].start()
    part = project(head[...].reshape(REQUESTS * HEAD, INNER), x_weight)
    for i in range(REQUESTS):
        half, k = i // PER, i % PER
        for q in range(QUARTERS):
            at = q * EDGES + k * EDGE
            edges[half, at : at + EDGE] = part[
                i * HEAD : i * HEAD + EDGE, q * LANES : (q + 1) * LANES
            ]
        last = k * EDGE + KEPT
        edges[half, last : last + 1] = jnp.concatenate(
            [part[i * HEAD + j : i * HEAD + j + 1, RANK:] for j in range(KEPT)]
            + [jnp.zeros((1, LANES - KEPT * 2 * STATE), F32)],
            axis=1,
        )
    sent[...] = edges[0].astype(BF16)
    kept[...] = edges[1]
    for one in leaving:
        one.wait()


def put_heads(routing, hidden, fetched, weight, bias, x_weight, conv_out):
    anywhere = pl.BlockSpec(memory_space=pl.ANY)
    edges = pl.BlockSpec((EDGED, LANES), lambda i, r: (0, 0))
    return pl.pallas_call(
        head_kernel,
        grid_spec=pltpu.PrefetchScalarGridSpec(
            num_scalar_prefetch=1,
            grid=(1,),
            in_specs=[
                pl.BlockSpec((REQUESTS, HEAD, INNER), lambda i, r: (0, 0, 0)),
                anywhere,
                pl.BlockSpec((KEPT + 1, INNER), lambda i, r: (0, 0)),
                pl.BlockSpec((1, INNER), lambda i, r: (0, 0)),
                pl.BlockSpec((USED, INNER), lambda i, r: (0, 0)),
                anywhere,
            ],
            out_specs=[anywhere, edges, edges],
            scratch_shapes=[
                pltpu.VMEM((REQUESTS, KEPT, TILES, LANES), BF16),
                pltpu.VMEM((8 + HEAD, INNER), F32),
                pltpu.VMEM((KEPT * TILES, LANES), F32),
                pltpu.VMEM((REQUESTS, HEAD, INNER), BF16),
                pltpu.VMEM((CHUNKS, EDGED, LANES), F32),
                pltpu.SemaphoreType.DMA((REQUESTS,)),
                pltpu.SemaphoreType.DMA((REQUESTS,)),
            ],
        ),
        out_shape=[
            jax.ShapeDtypeStruct(conv_out.shape, conv_out.dtype),
            jax.ShapeDtypeStruct((EDGED, LANES), BF16),
            jax.ShapeDtypeStruct((EDGED, LANES), F32),
        ],
        input_output_aliases={6: 0},
        compiler_params=params(16),
        cost_estimate=cost(4, 4 * 2**20),
        name="put_heads",
    )(routing, hidden, fetched, weight, bias, x_weight, conv_out)


def norm_rank(quarters):
    square = sum(jnp.sum(q * q, axis=1, keepdims=True) for q in quarters)
    scale = lax.rsqrt(square * (1.0 / RANK) + EPSILON)
    return [q * scale for q in quarters]


def norm_vectors(values):
    parts = []
    for first in range(0, values.shape[1], STATE):
        one = values[:, first : first + STATE]
        mean = jnp.mean(one * one, axis=1, keepdims=True)
        parts.append(one * lax.rsqrt(jnp.maximum(mean, NORM_FLOOR)))
    return jnp.concatenate(parts, axis=1)


def norm_kernel(parts, edge, edge_came, out, came, sem):
    arriving = pltpu.make_async_copy(edge_came, came, sem)
    arriving.start()
    total = parts[0].astype(F32)
    for k in range(1, DEPTH):
        total = total + parts[k].astype(F32)
    ranks = norm_rank([total[q * SHARE : (q + 1) * SHARE] for q in range(QUARTERS)])
    ranks = [q.astype(BF16) for q in ranks]
    vectors = norm_vectors(total[VECTORS:]).astype(BF16)
    arriving.wait()
    edges = (edge[...] + came[...].astype(F32)).astype(BF16)
    for k in range(DEPTH):
        for q in range(QUARTERS):
            out[k, q * SHARE : (q + 1) * SHARE] = ranks[q]
        out[k, VECTORS:SUMMED] = vectors
        out[k, SUMMED:] = edges


def normalize(parts, edge, edge_came):
    return pl.pallas_call(
        norm_kernel,
        in_specs=[
            pl.BlockSpec(memory_space=pltpu.VMEM),
            pl.BlockSpec(memory_space=pltpu.VMEM),
            pl.BlockSpec(memory_space=pl.ANY),
        ],
        scratch_shapes=[pltpu.VMEM((EDGED, LANES), BF16), pltpu.SemaphoreType.DMA],
        out_shape=jax.ShapeDtypeStruct((DEPTH, GATHERED, LANES), BF16),
        compiler_params=params(12),
        cost_estimate=cost(1.5, 2**20),
        name="normalize",
    )(parts, edge, edge_came)


def scan_kernel(
    own, routing, came, dt_weight, dt_bias, a_log, skip, conv, gate, start,
    last, other_last, base, gated, final, dts, us, spread, rates, states, shares, sem,
):
    step = pl.program_id(0)
    to = routing[HOLDER + (PER if own else 0) + step]

    @pl.when(step == 0)
    def _():
        arriving = pltpu.make_async_copy(came, shares, sem)
        arriving.start()
        rows_to_tiles(rates, 0, -LOG2_E * jnp.exp(a_log[...]))
        arriving.wait()
        total = shares[0, SUMMED:].astype(F32)
        for k in range(1, DEPTH):
            total = total + shares[k, SUMMED:].astype(F32)
        quarters = [total[q * EDGES : (q + 1) * EDGES] for q in range(QUARTERS)]
        row = lax.broadcasted_iota(jnp.int32, (GROUP, LANES), 0) < KEPT
        lane = lax.broadcasted_iota(jnp.int32, (GROUP, LANES), 1) < 2 * STATE

        def patch(at, first, values, where):
            old = shares[at, first : first + GROUP].astype(F32)
            shares[at, first : first + GROUP] = jnp.where(where, values, old).astype(BF16)

        below = jnp.zeros((GROUP - EDGE, LANES), F32)
        for q, values in enumerate(norm_rank(quarters)):
            for k in range(PER):
                values_of = jnp.concatenate([values[k * EDGE : (k + 1) * EDGE], below], axis=0)
                patch(k * SPANS, q * SHARE, values_of, row)
        beside = jnp.zeros((KEPT, LANES - 2 * STATE), F32)
        below = jnp.zeros((GROUP - KEPT, LANES), F32)
        for k in range(PER):
            last = k * EDGE + KEPT
            flat = norm_vectors(quarters[0][last : last + 1, : KEPT * 2 * STATE])
            lines = [flat[:, j * 2 * STATE : (j + 1) * 2 * STATE] for j in range(KEPT)]
            values_of = jnp.concatenate([jnp.concatenate(lines, axis=0), beside], axis=1)
            values_of = jnp.concatenate([values_of, below], axis=0)
            patch(k * SPANS, VECTORS, values_of, row & lane)

    ranks = []
    for span in range(SPANS):
        at = step * SPANS + span
        ranks.append(
            jnp.concatenate(
                [shares[at, q * SHARE : (q + 1) * SHARE] for q in range(QUARTERS)], axis=1
            )
        )
        columns = shares[at, VECTORS:SUMMED].astype(F32).T
        for k in range(SHARE):
            a, t = k // GROUP, span * SHARE + k
            spread[t * 2 * STATE : (t + 1) * 2 * STATE, :] = jnp.broadcast_to(
                columns[a * 2 * STATE : (a + 1) * 2 * STATE, k % GROUP : k % GROUP + 1],
                (2 * STATE, LANES),
            )
    rank = jnp.concatenate(ranks, axis=0)
    if own:
        for which, (rows, at) in enumerate(((last, to), (other_last, routing[HOLDER + step]))):
            rows_to_tiles(states, 0, rows[0].astype(F32)[HEAD - KEPT :, :])
            for k in range(KEPT):
                final[at, STATE + which * KEPT + k] = states[
                    k * TILES : (k + 1) * TILES, :
                ].astype(BF16)
    for part in range(STATE // 8):
        for tile in range(TILES):
            states[pl.ds(part * 8 * TILES + tile, 8, stride=TILES), :] = start[
                0, part * TILES + tile
            ].astype(F32)
    pair = 2 * LANES
    for block in range(INNER // pair):
        cols = slice(block * pair, (block + 1) * pair)
        raw = jnp.dot(rank, dt_weight[:, cols], preferred_element_type=F32) + dt_bias[:, cols]
        dt = jnp.maximum(raw, 0.0) + jnp.log1p(jnp.exp(-jnp.abs(raw)))
        for k in range(2):
            tile = 2 * block + k
            dts[pl.ds(tile, TURN, stride=TILES), :] = dt[:, k * LANES : (k + 1) * LANES]
            us[pl.ds(tile, TURN, stride=TILES), :] = conv[
                0, :, tile * LANES : (tile + 1) * LANES
            ].astype(F32)
    decay = [rates[n * TILES : (n + 1) * TILES, :] for n in range(STATE)]

    def steps(i, carried):
        carried = list(carried)
        for k in range(UNROLL):
            t = i * UNROLL + k
            at = pl.multiple_of(t * TILES, TILES)
            row = pl.multiple_of(t * 2 * STATE, 2 * STATE)
            dt = dts[pl.ds(at, TILES), :]
            drive = dt * us[pl.ds(at, TILES), :]
            sums = [None] * 4
            for n in range(STATE):
                carried[n] = (
                    jnp.exp2(dt * decay[n]) * carried[n] + drive * spread[pl.ds(row + n, 1), :]
                )
                term = carried[n] * spread[pl.ds(row + STATE + n, 1), :]
                sums[n % 4] = term if sums[n % 4] is None else sums[n % 4] + term
            dts[pl.ds(at, TILES), :] = (sums[0] + sums[1]) + (sums[2] + sums[3])
        return tuple(carried)

    carried = tuple(states[n * TILES : (n + 1) * TILES, :] for n in range(STATE))
    carried = lax.fori_loop(0, TURN // UNROLL, steps, carried)
    for n in range(STATE):
        states[n * TILES : (n + 1) * TILES, :] = carried[n]
    for part in range(STATE // 8):
        for tile in range(TILES):
            final[to, part * TILES + tile] = states[
                pl.ds(part * 8 * TILES + tile, 8, stride=TILES), :
            ].astype(BF16)
    for tile in range(TILES):
        cols = slice(tile * LANES, (tile + 1) * LANES)
        z = gate[0, :, cols].astype(F32)
        y = dts[pl.ds(tile, TURN, stride=TILES), :] + skip[:, cols] * conv[0, :, cols].astype(F32)
        gated[0, :, cols] = (y * silu(z)).astype(BF16)


def scan(routing, came, dt_weight, dt_bias, a_log, skip, conv, gate, fetched, hidden, base):
    own = base is None
    first = PER if own else 0
    blocks = RETURNED if own else STATE
    whole = lambda shape: pl.BlockSpec(shape, lambda i, r: (0,) * len(shape))
    ends = lambda at: pl.BlockSpec(
        (1, HEAD, INNER), lambda i, r: (r[ORDER + at + i], TURN // HEAD - 1, 0)
    )
    return pl.pallas_call(
        functools.partial(scan_kernel, own),
        grid_spec=pltpu.PrefetchScalarGridSpec(
            num_scalar_prefetch=1,
            grid=(PER,),
            in_specs=[
                pl.BlockSpec(memory_space=pl.ANY),
                whole((RANK, INNER)),
                whole((1, INNER)),
                whole((STATE, INNER)),
                whole((1, INNER)),
                pl.BlockSpec((1, TURN, INNER), lambda i, r: (first + i, 0, 0)),
                pl.BlockSpec((1, TURN, INNER), lambda i, r: (r[ORDER + first + i], 0, 0)),
                pl.BlockSpec(
                    (1, STATE, TILES, LANES),
                    lambda i, r: (r[HOLDER + first + i], r[SIDES + own], 0, 0),
                ),
                ends(PER),
                ends(0),
                pl.BlockSpec(memory_space=pl.ANY),
            ],
            out_specs=[
                pl.BlockSpec((1, TURN, INNER), lambda i, r: (r[ORDER + first + i], 0, 0)),
                whole((GROUPS, blocks, TILES, LANES)),
            ],
            scratch_shapes=[
                pltpu.VMEM((TURN * TILES, LANES), F32),
                pltpu.VMEM((TURN * TILES, LANES), F32),
                pltpu.VMEM((TURN * 2 * STATE, LANES), F32),
                pltpu.VMEM((STATE * TILES, LANES), F32),
                pltpu.VMEM((STATE * TILES, LANES), F32),
                pltpu.VMEM((DEPTH, GATHERED, LANES), BF16),
                pltpu.SemaphoreType.DMA,
            ],
        ),
        out_shape=[
            jax.ShapeDtypeStruct((REQUESTS, TURN, INNER), BF16),
            jax.ShapeDtypeStruct((GROUPS, blocks, TILES, LANES), BF16),
        ],
        input_output_aliases={} if own else {11: 0},
        compiler_params=params(20 if own else 56),
        cost_estimate=cost(15, 4 * 2**20),
        name="scan",
    )(routing, came, dt_weight, dt_bias, a_log, skip, conv, gate, fetched, hidden,
      hidden, skip if own else base)


def widen(came, wide, g, row):
    for part in range(STATE // 8):
        for tile in range(TILES):
            rows, cols = block_of(part, tile)
            wide[row, rows, cols] = came[g, part * TILES + tile].astype(F32)


def place_kernel(routing, came, ssm, conv, new_ssm, new_conv, inputs, sem):
    base = pltpu.make_async_copy(ssm, new_ssm, sem)
    base.start()
    for k in range(KEPT):
        rows_to_tiles(inputs, k * SLOTS * TILES, conv[k])

    def put(slot, g, first):
        for k in range(KEPT):
            row = pl.multiple_of((k * SLOTS + slot) * TILES, TILES)
            inputs[pl.ds(row, TILES), :] = came[g, first + k].astype(F32)

    def each(g, carry):
        slot = routing[OWN + g]
        other_slot = routing[OTHER + g]

        @pl.when(slot < SLOTS)
        def _():
            widen(came, new_ssm, g, slot)
            put(slot, g, STATE)

        @pl.when(other_slot < SLOTS)
        def _():
            put(other_slot, g, STATE + KEPT)

        return carry

    base.wait()
    lax.fori_loop(0, GROUPS, each, 0)
    for k in range(KEPT):
        for tile in range(TILES):
            new_conv[k, :, tile * LANES : (tile + 1) * LANES] = inputs[
                pl.ds(k * SLOTS * TILES + tile, SLOTS, stride=TILES), :
            ]


def place(routing, came, ssm, conv):
    rows = pl.BlockSpec((KEPT, SLOTS, INNER), lambda i, r: (0, 0, 0))
    return pl.pallas_call(
        place_kernel,
        grid_spec=pltpu.PrefetchScalarGridSpec(
            num_scalar_prefetch=1,
            grid=(1,),
            in_specs=[
                pl.BlockSpec((GROUPS, RETURNED, TILES, LANES), lambda i, r: (0, 0, 0, 0)),
                pl.BlockSpec(memory_space=pl.ANY),
                rows,
            ],
            out_specs=[pl.BlockSpec((SLOTS, STATE, INNER), lambda i, r: (0, 0, 0)), rows],
            scratch_shapes=[
                pltpu.VMEM((KEPT * SLOTS * TILES, LANES), F32),
                pltpu.SemaphoreType.DMA,
            ],
        ),
        out_shape=[
            jax.ShapeDtypeStruct((SLOTS, STATE, INNER), F32),
            jax.ShapeDtypeStruct((KEPT, SLOTS, INNER), F32),
        ],
        compiler_params=params(20),
        cost_estimate=cost(6, 6 * 2**20),
        name="place",
    )(routing, came, ssm, conv)


def store_kernel(routing, came, ssm_in, new_ssm, states, wide, sem, sems):
    def copy(g):
        return pltpu.make_async_copy(wide.at[g], new_ssm.at[routing[OTHER + g]], sems.at[g])

    def begin(g, carry):
        @pl.when(routing[OTHER + g] < SLOTS)
        def _():
            widen(states, wide, g, g)
            copy(g).start()

        return carry

    def finish(g, carry):
        @pl.when(routing[OTHER + g] < SLOTS)
        def _():
            copy(g).wait()

        return carry

    arriving = pltpu.make_async_copy(came, states, sem)
    arriving.start()
    arriving.wait()
    lax.fori_loop(0, GROUPS, begin, 0)
    lax.fori_loop(0, GROUPS, finish, 0)


def store(routing, came, ssm):
    anywhere = pl.BlockSpec(memory_space=pl.ANY)
    return pl.pallas_call(
        store_kernel,
        grid_spec=pltpu.PrefetchScalarGridSpec(
            num_scalar_prefetch=1,
            grid=(1,),
            in_specs=[anywhere, anywhere],
            out_specs=anywhere,
            scratch_shapes=[
                pltpu.VMEM((GROUPS, STATE, TILES, LANES), BF16),
                pltpu.VMEM((GROUPS, STATE, INNER), F32),
                pltpu.SemaphoreType.DMA,
                pltpu.SemaphoreType.DMA((GROUPS,)),
            ],
        ),
        out_shape=jax.ShapeDtypeStruct((SLOTS, STATE, INNER), F32),
        input_output_aliases={2: 0},
        compiler_params=params(8),
        cost_estimate=cost(2, 2 * 2**20),
        name="store",
    )(routing, came, ssm)


def exchange(values, axis):
    return lax.all_to_all(values, axis, split_axis=0, concat_axis=0, tiled=True)


def body(
    hidden_x,
    gate_z,
    conv_weight,
    conv_bias,
    x_weight,
    dt_weight,
    dt_bias,
    a_log,
    skip_gain,
    ssm_cache,
    conv_cache,
    holder_of,
    slot_of,
):
    conv_rows = jnp.swapaxes(conv_cache, 0, 1)
    bias = conv_bias.reshape(1, INNER)
    x_weight = x_weight.T
    routing, packed = pack(holder_of, slot_of, ssm_cache, conv_rows)
    fetched = exchange(packed, "dp")
    conv, sent, kept = convolve(routing, hidden_x, conv_weight, bias, x_weight)
    parts = (kept + lax.ppermute(sent, "core", SWAP).astype(F32)).astype(BF16)
    parts, fetched = lax.optimization_barrier((parts, fetched))
    parts = exchange(parts.reshape(DEPTH, SUMMED, LANES), "z")
    conv, edge_sent, edge = put_heads(
        routing, hidden_x, fetched, conv_weight, bias, x_weight, conv
    )
    normed = exchange(normalize(parts, edge, lax.ppermute(edge_sent, "core", SWAP)), "z")
    gated, came = None, []
    for values in (normed, lax.ppermute(normed, "core", SWAP)):
        gated, final = scan(
            routing,
            values,
            dt_weight,
            dt_bias.reshape(1, INNER),
            a_log,
            skip_gain.reshape(1, INNER),
            conv,
            gate_z,
            fetched,
            hidden_x,
            gated,
        )
        if came:
            came[0], final = lax.optimization_barrier((came[0], final))
        came.append(exchange(final, "dp"))
    new_ssm, new_conv = place(routing, came[0], ssm_cache, conv_rows)
    new_ssm = store(routing, came[1], new_ssm)
    return (gated, new_ssm, jnp.swapaxes(new_conv, 0, 1))


def solution(mesh):
    fine = Mesh(mesh.devices.reshape(GROUPS, DEPTH, CORES), ("dp", "z", "core"))
    tensor = ("z", "core")
    placed = (
        P("dp", None, tensor),
        P("dp", None, tensor),
        P(None, tensor),
        P(tensor),
        P(tensor, None),
        P(None, tensor),
        P(tensor),
        P(None, tensor),
        P(tensor),
        P("dp", None, tensor),
        P("dp", None, tensor),
        P(),
        P(),
    )
    return jax.shard_map(
        body,
        mesh=fine,
        in_specs=placed,
        out_specs=(P("dp", None, tensor),) * 3,
        check_vma=False,
    )
```
